128 devices in a mesh: section: 2 (over x_hi), rep: 8 (over z, x_lo), shard: 8 (over y, core).
Axes of the slice: x: 4 (x_hi: 2, x_lo: 2; x = x_hi * 2 + x_lo), y: 4, z: 4, core: 2. Of those that a mesh axis runs over, the one named last changes fastest.
Arguments:
- tokens_in: bfloat16 [2, 8, 512, 1536], P(None, 'rep', 'shard'), may hold values from -6 to 6
- cotangent: bfloat16 [2, 8, 512, 1536], P(None, 'rep', 'shard'), may hold values from -6 to 6
- routes: int32 [2, 2, 8, 512, 4], P('section', None, 'rep', 'shard'), may hold values from 0 to 7, all different within a row; in each aligned block of 64 rows (0 to 63, 64 to 127, ..., all dimensions but the last counted through in order) at most 40 rows name the same one
- gain_attn: bfloat16 [2, 1536], P('section', 'shard'), may hold values from 0.5 to 1.5
- w_query: bfloat16 [2, 1536, 1536], P('section', 'shard'), may hold values from -0.21875 to 0.21875
- w_keyval: bfloat16 [2, 1536, 512], P('section', 'shard'), may hold values from -0.15625 to 0.15625
- w_out: bfloat16 [2, 1536, 1536], P('section', 'shard'), may hold values from -1.25 to 1.25
- gain_moe: bfloat16 [2, 1536], P('section', 'shard'), may hold values from 0.5 to 1.5
- w_router: bfloat16 [2, 1536, 8], P('section', 'shard'), may hold values from -0.078125 to 0.078125
- w_in: bfloat16 [2, 8, 1536, 1536], P('section', 'shard'), may hold values from -0.15625 to 0.15625
- w_down: bfloat16 [2, 8, 768, 1536], P('section', 'shard'), may hold values from -0.4375 to 0.4375
Outputs:
- acts: bfloat16 [2, 2, 8, 512, 1536], P('section', None, 'rep', 'shard')
- input_grads: float32 [2, 2, 8, 512, 1536], P('section', None, 'rep', 'shard')
- grad_gain_attn: float32 [2, 1536], P('section', 'shard')
- grad_query: float32 [2, 1536, 1536], P('section', 'shard', 'rep')
- grad_keyval: float32 [2, 1536, 512], P('section', 'shard', 'rep')
- grad_out: float32 [2, 1536, 1536], P('section', 'shard', 'rep')
- grad_gain_moe: float32 [2, 1536], P('section', 'shard')
- grad_router: float32 [2, 1536, 8], P('section', 'shard')
- grad_in: float32 [2, 8, 1536, 1536], P('section', 'shard', 'rep')
- grad_down: float32 [2, 8, 768, 1536], P('section', 'shard', 'rep')
The draws below stay inside these ranges and needn't reach their ends.
Inputs may be any that keep to these rules, and one draw needn't show every extreme that they name: `routes`: each token names 4 different experts; within the 64 positions of one device's part of a sequence no expert is named by more than 40 tokens, a bound that some expert reaches in some such block.
All inputs are finite; a program needn't handle non-finite values.
Results may differ from the reference program's by a relative error of at most 0.033.
Values may be sent and summed in bfloat16 or wider, within the bound.
No kernel may reach another device: no remote copies, remote signals or barrier semaphores. Data moves between devices by JAX's collectives and lax.ppermute only.
A program may use at most 256 MiB of HBM per device.

```python
import math
import jax
import jax.numpy as jnp
import numpy as np
from jax import lax

D = 1536
QUERY_HEADS = 12
KEY_VALUE_HEADS = 2
HEAD_SIZE = 128
FFE = 768
TOP = 4
EXPERTS = 8
MICRO = 2
TOK_MB = 64
LEN = 512
SEQS = 8
QD = 1536
KEY_WIDTH = 256
CAP = 40
N_SECTION = 2


def level_of(own_key, dims, split, least, high):
    loudness, own = 1.0, jax.random.fold_in(own_key, 6)
    for position, shards_of in split:
        heights = jnp.exp(jax.random.uniform(jax.random.fold_in(own, position), (shards_of,), jnp.float32, least / len(split), high / len(split)))
        loudness = loudness * jnp.repeat(heights, dims[position] // shards_of).reshape([-1 if axis == position else 1 for axis in range(len(dims))])
    return loudness


def deal_out(own_key, own, number, rows, count, top, most, skew):
    order = jax.random.permutation(own_key, count)
    crowded, common = portions_of(count, rows * top, most, skew, True), portions_of(count, rows * top, most, skew, False)
    places = jnp.arange(count)

    def named(lengths, rotation):
        used = int((lengths > 0).sum())
        fixed = max(1, used // 4)
        passed = fixed + (places - fixed + rotation * (used - fixed)) % max(1, count - fixed)
        return jnp.zeros((count,), jnp.int32).at[order[jnp.where(places < fixed, places, passed)]].set(jnp.asarray(lengths, jnp.int32))

    lengths = jnp.where(number % 4 == 0, named(crowded, number // 4), named(common, number - number // 4 - 1))
    mixed = jax.random.permutation(jax.random.fold_in(own, 3), count)
    donor, receiver = mixed[0:count // 2 * 2:2], mixed[1:count // 2 * 2:2]
    slack = jnp.minimum(lengths[donor] - 1, most - lengths[receiver]) // 2
    slack = jnp.where((donor == order[0]) | (receiver == order[0]) | (lengths[receiver] == 0), 0, jnp.maximum(slack, 0))
    passed = jax.random.randint(jax.random.fold_in(own, 4), (count // 2,), 0, 1 << 20) % (slack + 1)
    lengths = lengths.at[donor].add(-passed).at[receiver].add(passed)
    items = jnp.searchsorted(jnp.cumsum(lengths), jnp.arange(rows * top), side="right").astype(jnp.int32)
    grid = items.reshape(top, rows).T
    grid = grid[jax.random.permutation(jax.random.fold_in(own, 1), rows)]
    rotation = jax.random.randint(jax.random.fold_in(own, 2), (rows, 1), 0, top)
    return jnp.take_along_axis(grid, (jnp.arange(top)[None, :] + rotation) % top, axis=1)


def portions_of(amount, total, most, slope, full):
    weights = [(1 << 20) // math.isqrt(rank ** slope) + 1 for rank in range(1, amount + 1)]
    largest = most if full else min(most, max(-(-total // amount), total * weights[0] // sum(weights)))
    least = 1 if total - largest >= amount - 1 else 0
    given, spare = [largest] + [least] * (amount - 1), total - largest - least * (amount - 1)
    while spare > 0:
        movable = [i for i in range(1, amount) if given[i] < largest] or [i for i in range(1, amount) if given[i] < most]
        pool, remaining = sum([weights[i] for i in movable]), spare
        for i in movable:
            more = min(most - given[i], max(1, remaining * weights[i] // pool), spare)
            given[i] = given[i] + more
            spare = spare - more
    return np.array(given)


def gaussian(own_key, dims, spread, most, shards=(), kind=jnp.bfloat16):
    result = jax.random.normal(own_key, dims, jnp.float32) * spread
    if len(shards) > 0:
        result = level_of(own_key, dims, shards, -0.22, 0.18) * result
    return jnp.clip(result, min=-most, max=most).astype(kind)


def setup_inputs(seed: int = 0) -> dict:
    key_of = jax.random.split(jax.random.key(seed), 12)
    tokens_in = gaussian(key_of[0], (MICRO, SEQS, LEN, D), 1.0, 6.0, ((1, 8), (2, 8)))
    cotangent = gaussian(key_of[1], (MICRO, SEQS, LEN, D), 1.0, 6.0, ((1, 8), (2, 8)))
    routes_keys = jax.random.split(jax.random.fold_in(key_of[2], 1), N_SECTION * MICRO * SEQS * LEN // TOK_MB)
    routes_turns = jax.random.permutation(jax.random.fold_in(key_of[2], 3), N_SECTION * MICRO * SEQS * LEN // TOK_MB)
    routes = jax.vmap(lambda own, number: deal_out(jax.random.fold_in(key_of[2], 2), own, number, TOK_MB, EXPERTS, TOP, CAP, 2))(routes_keys, routes_turns).reshape((N_SECTION, MICRO, SEQS, LEN, TOP))
    gain_attn = jnp.clip(1.0 + 0.1 * jax.random.normal(key_of[3], (N_SECTION, D), jnp.float32), 0.5, 1.5).astype(jnp.bfloat16)
    w_query = gaussian(key_of[4], (N_SECTION, D, QD), (D // 2) ** -0.5, 0.21875, ((0, 2), (1, 8)))
    w_keyval = gaussian(key_of[5], (N_SECTION, D, 2 * KEY_WIDTH), D ** -0.5, 0.15625, ((0, 2), (1, 8)))
    w_out = gaussian(key_of[6], (N_SECTION, QD, D), (QD // 64) ** -0.5, 1.25, ((0, 2), (1, 8)))
    gain_moe = jnp.clip(1.0 + 0.1 * jax.random.normal(key_of[7], (N_SECTION, D), jnp.float32), 0.5, 1.5).astype(jnp.bfloat16)
    w_router = gaussian(key_of[8], (N_SECTION, D, EXPERTS), (4 * D) ** -0.5, 0.078125, ((0, 2), (1, 8)))
    w_in = gaussian(key_of[9], (N_SECTION, EXPERTS, D, 2 * FFE), D ** -0.5, 0.15625, ((0, 2), (1, 8)))
    w_down = gaussian(key_of[10], (N_SECTION, EXPERTS, FFE, D), (FFE // 4) ** -0.5, 0.4375, ((0, 2), (1, 8)))
    return dict(tokens_in=tokens_in, cotangent=cotangent, routes=routes, gain_attn=gain_attn, w_query=w_query, w_keyval=w_keyval, w_out=w_out, gain_moe=gain_moe, w_router=w_router, w_in=w_in, w_down=w_down)


EPS = 1e-06
ROPE_BASE = 1000000.0
PRECISE = lax.Precision.HIGHEST

@jax.custom_vjp
def lower_precision(v):
    return lax.optimization_barrier(v.astype(jnp.bfloat16)).astype(jnp.float32)

@jax.custom_vjp
def low_back(v):
    return v

def low_keep(v):
    return (lower_precision(v), None)

def low_pass(kept, grad):
    return (grad,)

def back_keep(v):
    return (v, None)

def back_low(kept, grad):
    return (lower_precision(grad),)
lower_precision.defvjp(low_keep, low_pass)
low_back.defvjp(back_keep, back_low)

def matmul(left, right):
    return jnp.dot(left, right, precision=PRECISE, preferred_element_type=jnp.float32)

def norm_rows(vector, gain):
    return vector * lax.rsqrt(lax.optimization_barrier(jnp.mean(vector * vector, axis=-1, keepdims=True)) + EPS) * gain

def rope_tables(token_length):
    half_dim = HEAD_SIZE // 2
    frequency = ROPE_BASE ** (-jnp.arange(half_dim, dtype=jnp.float32) * 2.0 / HEAD_SIZE)
    angles = jnp.arange(token_length, dtype=jnp.float32)[:, None] * frequency[None, :]
    return (jnp.cos(angles), jnp.sin(angles))

def rotate_halves(vector, cosine_table, sine_table):
    half_dim = vector.shape[-1] // 2
    first_half = vector[..., :half_dim]
    second_half = vector[..., half_dim:]
    cos_b = cosine_table[:, None, :]
    sin_b = sine_table[:, None, :]
    return jnp.concatenate([first_half * cos_b - second_half * sin_b, second_half * cos_b + first_half * sin_b], axis=-1)

def run_layer(params, stream, route):
    gain_a, w_q, w_kv, w_o, gain_m, w_r, w_inner, w_outer = params
    token_length = stream.shape[0]
    groups_per_head = QUERY_HEADS // KEY_VALUE_HEADS
    cosine_table, sine_table = rope_tables(token_length)
    h_attn = lower_precision(norm_rows(stream, gain_a))
    q_pre = low_back(matmul(h_attn, w_q))
    key_value_projected = low_back(matmul(h_attn, w_kv))
    query_rows = lower_precision(rotate_halves(q_pre.reshape(token_length, QUERY_HEADS, HEAD_SIZE), cosine_table, sine_table))
    key_matrix = lower_precision(rotate_halves(key_value_projected[:, :KEY_WIDTH].reshape(token_length, KEY_VALUE_HEADS, HEAD_SIZE), cosine_table, sine_table))
    value_matrix = lower_precision(key_value_projected[:, KEY_WIDTH:]).reshape(token_length, KEY_VALUE_HEADS, HEAD_SIZE)
    grouped_rows = query_rows.reshape(token_length, KEY_VALUE_HEADS, groups_per_head, HEAD_SIZE)
    raw_scores = low_back(jnp.einsum('nkgd,lkd->kgnl', grouped_rows, key_matrix, precision=PRECISE))
    scores = raw_scores * HEAD_SIZE ** (-0.5)
    allowed = jnp.arange(token_length)[None, :] <= jnp.arange(token_length)[:, None]
    scores = jnp.where(allowed, scores, -1e+30)
    row_max = lax.optimization_barrier(jnp.max(scores, axis=-1, keepdims=True))
    exponent = jnp.exp(scores - row_max)
    probs = exponent / lax.optimization_barrier(jnp.sum(exponent, axis=-1, keepdims=True))
    mixed_out = jnp.einsum('kgnl,lkd->nkgd', lower_precision(probs), value_matrix, precision=PRECISE)
    attended = lower_precision(low_back(mixed_out.reshape(token_length, QD)))
    mid_stream = stream + low_back(matmul(attended, w_o))
    h_moe = lower_precision(norm_rows(mid_stream, gain_m))
    logits = low_back(matmul(h_moe, w_r))
    chosen = (route[:, :, None] == jnp.arange(EXPERTS)[None, None, :]).astype(jnp.float32)
    picked = lax.optimization_barrier(jnp.sum(chosen * logits[:, None, :], axis=-1))
    gate_vals = jax.nn.softmax(picked, axis=-1)
    gate_share = lax.optimization_barrier(jnp.sum(chosen * gate_vals[:, :, None], axis=1))
    copies = low_back(jnp.broadcast_to(h_moe[None], (EXPERTS,) + h_moe.shape))
    gate_up = low_back(jnp.einsum('end,edf->enf', copies, w_inner, precision=PRECISE))
    activated = jax.nn.silu(gate_up[..., :FFE]) * gate_up[..., FFE:]
    produced = lower_precision(low_back(jnp.einsum('enf,efd->end', lower_precision(activated), w_outer, precision=PRECISE)))
    return mid_stream + jnp.einsum('ne,end->nd', gate_share, produced, precision=PRECISE)

def reference(tokens_in, cotangent, routes, gain_attn, w_query, w_keyval, w_out, gain_moe, w_router, w_in, w_down):
    weights = tuple((item.astype(jnp.float32) for item in (gain_attn, w_query, w_keyval, w_out, gain_moe, w_router, w_in, w_down)))
    count = MICRO * SEQS
    inputs = tokens_in.astype(jnp.float32).reshape(count, LEN, D)
    grads_given = cotangent.astype(jnp.float32).reshape(count, LEN, D)
    route_rows = jnp.moveaxis(routes.reshape(N_SECTION, count, LEN, TOP), 0, 1)
    bump = jnp.zeros((count, LEN, D), jnp.float32)

    def forward(inputs, bump, weights):
        first_params = tuple((item[0] for item in weights))
        second_params = tuple((item[1] for item in weights))

        def one_sequence(carry, item):
            sequence, extra, route_pair = item
            middle = lower_precision(run_layer(first_params, sequence, route_pair[0])) + extra
            final = run_layer(second_params, middle, route_pair[1])
            return (carry, (middle, final))
        start = jnp.zeros((), jnp.float32)
        unused, (middles, finals) = lax.scan(jax.checkpoint(one_sequence), start, (inputs, bump, route_rows))
        return (middles, finals)
    (middles, finals), pull_back = jax.vjp(forward, inputs, bump, weights)
    grad_inputs, grad_bump, grad_weights = pull_back((jnp.zeros_like(middles), grads_given))
    acts = jnp.stack([middles, finals]).reshape(N_SECTION, MICRO, SEQS, LEN, D).astype(jnp.bfloat16)
    input_grads = jnp.stack([grad_inputs, grad_bump]).reshape(N_SECTION, MICRO, SEQS, LEN, D)
    return (acts, input_grads, grad_weights[0], grad_weights[1], grad_weights[2], grad_weights[3], grad_weights[4], grad_weights[5], grad_weights[6], grad_weights[7])
```

```python
import jax
import jax.numpy as jnp
from jax import lax
from jax.experimental import pallas as pl
from jax.experimental.pallas import tpu as pltpu
from jax.sharding import PartitionSpec as P

D = 1536
T = 64
HEADS = 12
KV_HEADS = 2
GROUP = HEADS // KV_HEADS
HS = 128
KW = KV_HEADS * HS
FF = 768
SEQ = 512
N_EXPERTS = 8
LANES = 128
EPS = 1e-06
ROPE_BASE = 1000000.0
SCALE = HS**-0.5
BF = jnp.bfloat16
F32 = jnp.float32

NN = (((1,), (0,)), ((), ()))
NT = (((1,), (1,)), ((), ()))
TN = (((0,), (0,)), ((), ()))


def mm(a, b, dims=NN):
    return lax.dot_general(a, b, dims, preferred_element_type=F32)


def sds(shape, dtype):
    return jax.ShapeDtypeStruct(shape, dtype)


def whole(shape):
    return pl.BlockSpec(shape, lambda *_: (0,) * len(shape))


def call(kernel, name, grid, in_specs, out_specs, out_shape, scratch, flops, nbytes, *args):
    return pl.pallas_call(
        kernel,
        name=name,
        grid=grid,
        in_specs=in_specs,
        out_specs=out_specs,
        out_shape=out_shape,
        scratch_shapes=scratch,
        compiler_params=pltpu.CompilerParams(
            dimension_semantics=("arbitrary",) * len(grid), vmem_limit_bytes=40 * 2**20
        ),
        cost_estimate=pl.CostEstimate(flops=flops, bytes_accessed=nbytes, transcendentals=0),
    )(*args)


def swap(x):
    return lax.ppermute(x, "shard", [(i, i ^ 1) for i in range(8)])


def along_y(x, k):
    return lax.ppermute(x, "shard", [(i, (i + 2 * k) % 8) for i in range(8)])


def gather_blocks(x):
    same = [x, along_y(x, 1), along_y(x, 2), along_y(x, 3)]
    return same + [swap(b) for b in same]


def scatter_sum_blocks(same, other):
    rows = same.shape[0] // 4
    got = swap(other)
    sums = []
    for k in range(4):
        part = slice(k * rows, (k + 1) * rows)
        sums.append((same[part].astype(F32) + got[part].astype(F32)).astype(BF))
    return [sums[0]] + [along_y(sums[k], -k) for k in (1, 2, 3)]


def rope(x, cos, sin):
    return x * cos + pltpu.roll(x, HS // 2, 1) * sin


def rope_back(x, cos, sin):
    return x * cos - pltpu.roll(x, HS // 2, 1) * sin


def qkv_kernel(x_ref, gain_ref, w_ref, cos_ref, sin_ref, q_ref, kv_ref, h_ref):
    j = pl.program_id(0)

    @pl.when(j == 0)
    def _():
        x = x_ref[...].astype(F32)
        r = lax.rsqrt(jnp.mean(x * x, axis=-1, keepdims=True) + EPS)
        h_ref[...] = (x * r * gain_ref[0:1, :]).astype(BF)

    y = mm(h_ref[...], w_ref[...])
    cos, sin = cos_ref[...], sin_ref[...]

    @pl.when(j < 3)
    def _():
        for i in range(4):
            at = slice(i * HS, (i + 1) * HS)
            q_ref[:, at] = rope(y[:, at], cos, sin).astype(BF)

    @pl.when(j == 3)
    def _():
        for i in range(2):
            at = slice(i * HS, (i + 1) * HS)
            kv_ref[:, at] = rope(y[:, at], cos, sin).astype(BF)
        kv_ref[:, KW:] = y[:, KW:].astype(BF)


def qkv(x, gains, w_packed, cos, sin):
    return call(
        qkv_kernel, "qkv", (4,),
        [whole((T, D)), whole((8, D)), pl.BlockSpec((D, 512), lambda j: (0, j)), whole((T, HS)), whole((T, HS))],
        [pl.BlockSpec((T, 512), lambda j: (0, jnp.minimum(j, 2))), whole((T, 512)), whole((T, D))],
        [sds((T, D), BF), sds((T, 512), BF), sds((T, D), BF)],
        [], 2 * T * D * 2048, 7 * 10**6,
        x, gains, w_packed, cos, sin,
    )


def stack_rows(blocks, dst, width):
    for i, b in enumerate(blocks):
        dst[i * T : (i + 1) * T, :] = b[:, :width]


def heads_of(ref, k):
    return jnp.concatenate([ref[:, h * HS : (h + 1) * HS] for h in range(k * GROUP, (k + 1) * GROUP)], axis=0)


def probs_of(q6, keys, allowed):
    s = mm(q6, keys, NT) * SCALE
    s = jnp.where(allowed[None] > 0, s.reshape(GROUP, T, SEQ), -1e30)
    e = jnp.exp(s - jnp.max(s, axis=-1, keepdims=True))
    p = e * (1.0 / jnp.sum(e, axis=-1, keepdims=True))
    return p.reshape(GROUP * T, SEQ)


def attend_kernel(*refs):
    q_ref, kv_refs, rest = refs[0], refs[1:9], refs[9:]
    allowed_ref, x_ref, w_ref, gain_ref, wr_ref, chosen_ref, att_ref, mid_ref, hm_ref, kv_s, mid_s = rest
    j = pl.program_id(0)

    @pl.when(j == 0)
    def _():
        stack_rows(kv_refs, kv_s, 512)
        allowed = allowed_ref[...]
        for k in range(KV_HEADS):
            p = probs_of(heads_of(q_ref, k), kv_s[:, k * HS : (k + 1) * HS], allowed).astype(BF)
            o = mm(p, kv_s[:, KW + k * HS : KW + (k + 1) * HS])
            for g in range(GROUP):
                h = k * GROUP + g
                att_ref[:, h * HS : (h + 1) * HS] = o[g * T : (g + 1) * T].astype(BF)

    mid_s[j] = mm(att_ref[...], w_ref[...])

    @pl.when(j == 3)
    def _():
        mids = [x_ref[:, i * 384 : (i + 1) * 384].astype(F32) + mid_s[i] for i in range(4)]
        square = sum(jnp.sum(v * v, axis=-1, keepdims=True) for v in mids)
        r = lax.rsqrt(square * (1.0 / D) + EPS)
        logits = jnp.zeros((T, LANES), F32)
        for i in range(4):
            at = slice(i * 384, (i + 1) * 384)
            mid_ref[:, at] = mids[i]
            h = (mids[i] * r * gain_ref[1:2, at]).astype(BF)
            hm_ref[:, at] = h
            logits = logits + mm(h, wr_ref[at, :])
        chosen = chosen_ref[...] > 0
        top = jnp.max(jnp.where(chosen, logits, -jnp.inf), axis=-1, keepdims=True)
        e = jnp.where(chosen, jnp.exp(jnp.minimum(logits - top, 0.0)), 0.0)
        gate = e / jnp.sum(e, axis=-1, keepdims=True)
        high = gate.astype(BF).astype(F32)
        hm_ref[:, D:] = (high + pltpu.roll(gate - high, N_EXPERTS, 1)).astype(BF)


def attend(q, kvs, allowed, x, w_out, gains, w_r, chosen):
    return call(
        attend_kernel, "attend", (4,),
        [whole((T, D))] + [whole((T, 512))] * 8
        + [whole((T, SEQ)), whole((T, D)), pl.BlockSpec((D, 384), lambda j: (0, j)), whole((8, D)), whole((D, LANES)), whole((T, LANES))],
        [whole((T, D)), whole((T, D)), whole((T, D + LANES))],
        [sds((T, D), BF), sds((T, D), F32), sds((T, D + LANES), BF)],
        [pltpu.VMEM((SEQ, 512), BF), pltpu.VMEM((4, T, 384), F32)],
        2 * T * D * D + 4 * T * D * SEQ, 8 * 10**6,
        q, *kvs, allowed, x, w_out, gains, w_r, chosen,
    )


def expert_kernel(save, *refs):
    hm_refs, (mine_ref, wg_ref, wu_ref, wd_ref), rest = refs[:8], refs[8:12], refs[12:]
    if save:
        same_ref, other_ref, h_ref, g_ref, gate_ref, up_ref, act_ref, prod_ref, acc = rest
    else:
        same_ref, other_ref, h_ref, g_ref, acc = rest
    j = pl.program_id(0)

    @pl.when(j == 0)
    def _():
        stack_rows(hm_refs, h_ref, D)
        mine = mine_ref[0:1, :]
        for i, b in enumerate(hm_refs):
            g = jnp.sum(b[:, D:].astype(F32) * mine, axis=-1, keepdims=True)
            g_ref[i * T : (i + 1) * T, :] = jnp.broadcast_to(g, (T, LANES))

    h = h_ref[...]
    gate = mm(h, wg_ref[...])
    up = mm(h, wu_ref[...])
    act = (gate / (1.0 + jnp.exp(-gate)) * up).astype(BF)
    if save:
        gate_ref[...] = gate
        up_ref[...] = up
        act_ref[...] = act
    add = mm(act, wd_ref[...])

    @pl.when(j == 0)
    def _():
        acc[...] = add

    @pl.when(j > 0)
    def _():
        acc[...] += add

    @pl.when(j == 2)
    def _():
        prod = acc[...].astype(BF)
        if save:
            prod_ref[...] = prod
        part = (prod.astype(F32) * g_ref[:, 0:1]).astype(BF)
        same_ref[...] = part[:256]
        other_ref[...] = part[256:]


def expert(hms, mine, w_in, w_down, save):
    f_block = pl.BlockSpec((SEQ, 256), lambda j: (0, j))
    out_specs = [whole((256, D)), whole((256, D))]
    out_shape = [sds((256, D), BF), sds((256, D), BF)]
    extra_specs = [whole((SEQ, D)), whole((SEQ, LANES))]
    extra_shape = [sds((SEQ, D), BF), sds((SEQ, LANES), F32)]
    scratch = [pltpu.VMEM((SEQ, D), F32)]
    if save:
        out_specs += extra_specs + [f_block, f_block, f_block, whole((SEQ, D))]
        out_shape += extra_shape + [sds((SEQ, FF), F32), sds((SEQ, FF), F32), sds((SEQ, FF), BF), sds((SEQ, D), BF)]
    else:
        scratch = [pltpu.VMEM((SEQ, D), BF), pltpu.VMEM((SEQ, LANES), F32)] + scratch
    return call(
        lambda *refs: expert_kernel(save, *refs), "expert", (3,),
        [whole((T, D + LANES))] * 8
        + [whole((8, LANES)), pl.BlockSpec((D, 256), lambda j: (0, j)), pl.BlockSpec((D, 256), lambda j: (0, j + 3)),
           pl.BlockSpec((256, D), lambda j: (j, 0))],
        out_specs, out_shape, scratch, 6 * SEQ * D * FF, 12 * 10**6,
        *hms, mine, w_in, w_in, w_down,
    )


def expert_back_kernel(save, *refs):
    gs, (g_ref, gate_ref, up_ref, prod_ref, put_ref, wd_ref, wg_ref, wu_ref), rest = refs[:8], refs[8:16], refs[16:]
    if save:
        same_ref, other_ref, dprod, dg_ref, du_ref, acc = rest
    else:
        same_ref, other_ref, dprod, acc = rest
    j = pl.program_id(0)

    @pl.when(j == 0)
    def _():
        put = put_ref[...]
        for i, b in enumerate(gs):
            at = slice(i * T, (i + 1) * T)
            g = b[...].astype(F32)
            dprod[at, :] = (g * g_ref[at, 0:1]).astype(BF)
            d = jnp.sum(g * prod_ref[at, :].astype(F32), axis=-1, keepdims=True)
            high = d.astype(BF).astype(F32)
            lanes = (high * put[0:1, :] + (d - high) * put[1:2, :]).astype(BF)
            dst = same_ref if i < 4 else other_ref
            dst[(i % 4) * T : (i % 4 + 1) * T, D:] = lanes

    d_act = mm(dprod[...], wd_ref[...], NT)
    gate, up = gate_ref[...], up_ref[...]
    s = 1.0 / (1.0 + jnp.exp(-gate))
    dg = (d_act * up * (s * (1.0 + gate * (1.0 - s)))).astype(BF)
    du = (d_act * (gate * s)).astype(BF)
    if save:
        dg_ref[...] = dg
        du_ref[...] = du
    add = mm(dg, wg_ref[...], NT) + mm(du, wu_ref[...], NT)

    @pl.when(j == 0)
    def _():
        acc[...] = add

    @pl.when(j > 0)
    def _():
        acc[...] += add

    @pl.when(j == 2)
    def _():
        same_ref[:, :D] = acc[:256].astype(BF)
        other_ref[:, :D] = acc[256:].astype(BF)


def expert_back(gs, kept, put, w_in, w_down, save):
    g_share, gate, up, produced = kept
    f_block = pl.BlockSpec((SEQ, 256), lambda j: (0, j))
    out_specs = [whole((256, D + LANES)), whole((256, D + LANES))]
    out_shape = [sds((256, D + LANES), BF), sds((256, D + LANES), BF)]
    scratch = [pltpu.VMEM((SEQ, D), F32)]
    if save:
        out_specs += [whole((SEQ, D)), f_block, f_block]
        out_shape += [sds((SEQ, D), BF), sds((SEQ, FF), BF), sds((SEQ, FF), BF)]
    else:
        scratch = [pltpu.VMEM((SEQ, D), BF)] + scratch
    return call(
        lambda *refs: expert_back_kernel(save, *refs), "expert_back", (3,),
        [whole((T, D))] * 8
        + [whole((SEQ, LANES)), f_block, f_block, whole((SEQ, D)), whole((8, LANES)),
           pl.BlockSpec((256, D), lambda j: (j, 0)), pl.BlockSpec((D, 256), lambda j: (0, j)), pl.BlockSpec((D, 256), lambda j: (0, j + 3))],
        out_specs, out_shape, scratch, 6 * SEQ * D * FF, 14 * 10**6,
        *gs, g_share, gate, up, produced, put, w_down, w_in, w_in,
    )


def norm_back(x, gain, grad):
    r = lax.rsqrt(jnp.mean(x * x, axis=-1, keepdims=True) + EPS)
    n = x * r
    scaled = grad * gain
    back = r * (scaled - n * jnp.mean(scaled * n, axis=-1, keepdims=True))
    return jnp.sum(grad * n, axis=0, keepdims=True), back


def attend_back_kernel(*refs):
    rets, (g_ref, mid_ref, hm_ref, gain_ref, wr_ref, w_ref, q_ref), kv_refs, rest = refs[:4], refs[4:11], refs[11:19], refs[19:]
    allowed_ref, cos_ref, sin_ref, dmid_ref, datt_ref, dq_ref, same_ref, other_ref, dl_ref, gain_out, da, kv_s, kv_acc = rest
    j = pl.program_id(0)

    @pl.when(j == 0)
    def _():
        total = sum(r[...].astype(F32) for r in rets)
        lanes = total[:, D:]
        d_gate = lanes + pltpu.roll(lanes, LANES - N_EXPERTS, 1)
        share = hm_ref[:, D:].astype(F32)
        gate = share + pltpu.roll(share, LANES - N_EXPERTS, 1)
        gate = jnp.where(lax.broadcasted_iota(jnp.int32, (T, LANES), 1) < N_EXPERTS, gate, 0.0)
        inner = jnp.sum(gate * d_gate, axis=-1, keepdims=True)
        d_logits = (gate * (d_gate - inner)).astype(BF)
        dl_ref[...] = d_logits
        d_hm = total[:, :D] + mm(d_logits, wr_ref[...], NT)
        grad_gain, back = norm_back(mid_ref[...], gain_ref[1:2, :], d_hm)
        gain_out[...] = jnp.broadcast_to(grad_gain, (8, D))
        d_mid = g_ref[...].astype(F32) + back
        dmid_ref[...] = d_mid
        datt_ref[...] = d_mid.astype(BF)
        stack_rows(kv_refs, kv_s, 512)

    piece = mm(datt_ref[...], w_ref[...], NT).astype(BF)
    for i in range(3):
        da[j * 3 + i] = piece[:, i * HS : (i + 1) * HS]

    @pl.when(j == 3)
    def _():
        allowed = allowed_ref[...]
        cos, sin = cos_ref[...], sin_ref[...]
        for k in range(KV_HEADS):
            keys = kv_s[:, k * HS : (k + 1) * HS]
            values = kv_s[:, KW + k * HS : KW + (k + 1) * HS]
            q6 = heads_of(q_ref, k)
            d6 = da[k * GROUP : (k + 1) * GROUP].reshape(GROUP * T, HS)
            p = probs_of(q6, keys, allowed)
            dp = mm(d6, values, NT)
            ds = (p * (dp - jnp.sum(p * dp, axis=-1, keepdims=True)) * SCALE).astype(BF)
            dq = mm(ds, keys)
            for g in range(GROUP):
                h = k * GROUP + g
                dq_ref[:, h * HS : (h + 1) * HS] = rope_back(dq[g * T : (g + 1) * T], cos, sin).astype(BF)
            kv_acc[:, k * HS : (k + 1) * HS] = mm(ds, q6, TN)
            kv_acc[:, KW + k * HS : KW + (k + 1) * HS] = mm(p.astype(BF), d6, TN)
        same_ref[...] = kv_acc[:256].astype(BF)
        other_ref[...] = kv_acc[256:].astype(BF)


def attend_back(rets, g, mid, hm, gains, w_r, w_out, q, kvs, allowed, cos, sin):
    return call(
        attend_back_kernel, "attend_back", (4,),
        [whole((T, D + LANES))] * 4
        + [whole((T, D)), whole((T, D)), whole((T, D + LANES)), whole((8, D)), whole((D, LANES)), pl.BlockSpec((384, D), lambda j: (j, 0)), whole((T, D))]
        + [whole((T, 512))] * 8 + [whole((T, SEQ)), whole((T, HS)), whole((T, HS))],
        [whole((T, D)), whole((T, D)), whole((T, D)), whole((256, 512)), whole((256, 512)), whole((T, LANES)), whole((8, D))],
        [sds((T, D), F32), sds((T, D), BF), sds((T, D), BF), sds((256, 512), BF), sds((256, 512), BF), sds((T, LANES), BF), sds((8, D), F32)],
        [pltpu.VMEM((HEADS, T, HS), BF), pltpu.VMEM((SEQ, 512), BF), pltpu.VMEM((SEQ, 512), F32)],
        2 * T * D * D + 10 * T * D * SEQ, 8 * 10**6,
        *rets, g, mid, hm, gains, w_r, w_out, q, *kvs, allowed, cos, sin,
    )


MSG = 2048 + LANES


def qkv_back_kernel(*refs):
    rets, (dq_ref, dl_ref, gm_ref, x_ref, gain_ref, w_ref, cos_ref, sin_ref, dmid_ref), rest = refs[:4], refs[4:13], refs[13:]
    gin_ref, glow_ref, msg_ref, dh = rest
    j = pl.program_id(0)

    @pl.when(j == 0)
    def _():
        d_kv = sum(r[...].astype(F32) for r in rets)
        cos, sin = cos_ref[...], sin_ref[...]
        msg_ref[:T, :D] = dq_ref[...]
        for i in range(KV_HEADS):
            msg_ref[:T, D + i * HS : D + (i + 1) * HS] = rope_back(d_kv[:, i * HS : (i + 1) * HS], cos, sin).astype(BF)
        msg_ref[:T, D + KW : 2048] = d_kv[:, KW:].astype(BF)
        msg_ref[:T, 2048:] = dl_ref[...]

    dh[j] = mm(msg_ref[:T, :2048], w_ref[...], NT)

    @pl.when(j == 3)
    def _():
        d_h = jnp.concatenate([dh[i] for i in range(4)], axis=1)
        grad_gain, back = norm_back(x_ref[...].astype(F32), gain_ref[0:1, :], d_h)
        g_in = dmid_ref[...] + back
        gin_ref[...] = g_in
        glow_ref[...] = g_in.astype(BF)
        row = lax.broadcasted_iota(jnp.int32, (16, D), 0)
        gm = jnp.broadcast_to(gm_ref[0:1, :], (16, D))
        both = jnp.where(row == 0, jnp.broadcast_to(grad_gain, (16, D)), jnp.where(row == 1, gm, 0.0))
        msg_ref[T:, :D] = both.astype(BF)
        msg_ref[T:, D:] = jnp.zeros((16, MSG - D), BF)


def qkv_back(rets, dq, dl, gm, x, gains, w_packed, cos, sin, d_mid):
    return call(
        qkv_back_kernel, "qkv_back", (4,),
        [whole((T, 512))] * 4
        + [whole((T, D)), whole((T, LANES)), whole((8, D)), whole((T, D)), whole((8, D)), pl.BlockSpec((384, 2048), lambda j: (j, 0)),
           whole((T, HS)), whole((T, HS)), whole((T, D))],
        [whole((T, D)), whole((T, D)), whole((T + 16, MSG))],
        [sds((T, D), F32), sds((T, D), BF), sds((T + 16, MSG), BF)],
        [pltpu.VMEM((4, T, 384), F32)],
        2 * T * D * 2048, 9 * 10**6,
        *rets, dq, dl, gm, x, gains, w_packed, cos, sin, d_mid,
    )


SLICE = D // 8


def attn_grad_kernel(*refs):
    order_ref, left_ref = refs[0], refs[1]
    msgs, datts = refs[2:18], refs[18:34]
    gq_ref, go_ref, gr_ref, gain_ref = refs[34:38]
    lh, rq, ro = refs[38:41]
    gains = jnp.zeros((16, D), F32)
    for m in range(2):
        for i in range(8):
            at = slice((m * 8 + i) * T, (m * 8 + i + 1) * T)
            lh[at, :] = left_ref[order_ref[i], m * T : (m + 1) * T, :]
            rq[at, :] = msgs[m * 8 + i][:T, :]
            ro[at, :] = datts[m * 8 + i][...]
            gains = gains + msgs[m * 8 + i][T:, :D].astype(F32)
    gain_ref[...] = gains
    for c in range(4):
        at = slice(c * 512, (c + 1) * 512)
        gq_ref[:, at] = mm(lh[:, :256], rq[:, at], TN)[:SLICE].astype(BF)
    for c in range(3):
        at = slice(c * 512, (c + 1) * 512)
        go_ref[:, at] = mm(lh[:, 256:512], ro[:, at], TN)[:SLICE].astype(BF)
    gr_ref[...] = mm(lh[:, 512:], rq[:, 2048:], TN)[:SLICE]


def attn_grad(order, left, msgs, datts):
    vm = pl.BlockSpec(memory_space=pltpu.VMEM)
    return pl.pallas_call(
        attn_grad_kernel,
        name="attn_grad",
        in_specs=[pl.BlockSpec(memory_space=pltpu.SMEM)] + [vm] * 33,
        out_specs=[vm] * 4,
        out_shape=[sds((SLICE, 2048), BF), sds((SLICE, D), BF), sds((SLICE, LANES), F32), sds((16, D), F32)],
        scratch_shapes=[pltpu.VMEM((1024, 768), BF), pltpu.VMEM((1024, MSG), BF), pltpu.VMEM((1024, D), BF)],
        compiler_params=pltpu.CompilerParams(vmem_limit_bytes=40 * 2**20),
        cost_estimate=pl.CostEstimate(flops=2 * 1024 * 256 * 3584, bytes_accessed=10 * 10**6, transcendentals=0),
    )(order, left, *msgs, *datts)


def body(tokens_in, cotangent, routes, gain_attn, w_query, w_keyval, w_out, gain_moe, w_router, w_in, w_down):
    is_first = lax.axis_index("section") == 0
    shard = lax.axis_index("shard")
    chip, core = shard // 2, shard % 2

    extra = jnp.concatenate([w_router[0], gain_attn[0][:, None], gain_moe[0][:, None]], axis=1)
    extra = jnp.pad(extra, ((0, 0), (0, LANES - extra.shape[1])))
    packed = jnp.concatenate([w_query[0], w_keyval[0], extra], axis=1)
    w_packed = lax.all_gather(packed, "shard", axis=0, tiled=True)
    w_o = lax.all_gather(w_out[0], "shard", axis=0, tiled=True)
    w_r = w_packed[:, 2048:]
    pick = (jnp.arange(LANES)[None, :] == (jnp.arange(8)[:, None] + N_EXPERTS)) & (jnp.arange(8)[:, None] < 2)
    gains = mm(pick.astype(BF), w_r, NT)
    inner, outer = w_in[0, 0], w_down[0, 0]

    half = HS // 2
    frequency = ROPE_BASE ** (-jnp.arange(half, dtype=F32) * 2.0 / HS)
    place = shard * T + jnp.arange(T, dtype=jnp.int32)
    angles = place.astype(F32)[:, None] * frequency[None, :]
    cos = jnp.concatenate([jnp.cos(angles)] * 2, axis=1)
    sin = jnp.concatenate([-jnp.sin(angles), jnp.sin(angles)], axis=1)
    order = jnp.stack([((chip - k) % 4) * 2 + c for c in (core, 1 - core) for k in range(4)]).astype(jnp.int32)
    key_place = (order[:, None] * T + jnp.arange(T, dtype=jnp.int32)[None, :]).reshape(1, SEQ)
    allowed = (key_place <= place[:, None]).astype(F32)
    lane = jnp.arange(LANES, dtype=jnp.int32)
    mine = ((lane == shard) | (lane == shard + N_EXPERTS)).astype(F32)
    mine = jnp.broadcast_to(mine[None, :], (8, LANES))
    put = jnp.stack([lane == shard, lane == shard + N_EXPERTS]).astype(F32)
    put = jnp.pad(put, ((0, 6), (0, 0)))

    def layer(x, route, save):
        chosen = jnp.any(route[:, :, None] == lane[None, None, :], axis=1).astype(F32)
        q, kv, h_attn = qkv(x, gains, w_packed, cos, sin)
        kvs = gather_blocks(kv)
        att, mid, hm = attend(q, kvs, allowed, x, w_o, gains, w_r, chosen)
        hms = gather_blocks(hm)
        out = expert(hms, mine, inner, outer, save)
        rets = scatter_sum_blocks(out[0], out[1])
        y = (mid + sum(r.astype(F32) for r in rets)).astype(BF)
        return y, (x, q, h_attn, kvs, att, mid, hm) + tuple(out[2:])

    def layer_back(g, kept, save):
        x, q, h_attn, kvs, att, mid, hm, h_all, g_share, gate, up, act, produced = kept
        gs = gather_blocks(g)
        out = expert_back(gs, (g_share, gate, up, produced), put, inner, outer, save)
        rets = scatter_sum_blocks(out[0], out[1])
        d_mid, d_att, dq, kv_same, kv_other, dl, gm = attend_back(
            rets, g, mid, hm, gains, w_r, w_o, q, kvs, allowed, cos, sin
        )
        kv_rets = scatter_sum_blocks(kv_same, kv_other)
        g_in, g_low, msg = qkv_back(kv_rets, dq, dl, gm, x, gains, w_packed, cos, sin, d_mid)
        return g_in, g_low, msg, d_att, out[2:]

    micros = range(2)
    first = [layer(tokens_in[m, 0], routes[0, m, 0], False)[0] for m in micros]
    arrived = [lax.ppermute(first[m], "section", [(0, 1)]) for m in micros]
    inputs = [jnp.where(is_first, tokens_in[m, 0], arrived[m]) for m in micros]
    second = [layer(inputs[m], routes[0, m, 0], True) for m in micros]
    acts = [second[m][0] for m in micros]
    kept = [second[m][1] for m in micros]

    back = [layer_back(cotangent[m, 0], kept[m], False)[1] for m in micros]
    arrived = [lax.ppermute(back[m], "section", [(1, 0)]) for m in micros]
    given = [jnp.where(is_first, arrived[m], cotangent[m, 0]) for m in micros]
    final = [layer_back(given[m], kept[m], True) for m in micros]

    h_all = [kept[m][7] for m in micros]
    act = [kept[m][11] for m in micros]
    d_prod = [final[m][4][0] for m in micros]
    d_gate = [final[m][4][1] for m in micros]
    d_up = [final[m][4][2] for m in micros]

    def both(left, right):
        return sum(mm(left[m], right[m], TN) for m in micros).astype(BF)

    send_in = jnp.concatenate([both(h_all, d_gate), both(h_all, d_up)], axis=1)
    send_down = both(act, d_prod)
    send = jnp.concatenate([send_in.reshape(8, SLICE, D), send_down.reshape(8, SLICE // 2, D)], axis=1)
    got = lax.all_to_all(send, "rep", split_axis=0, concat_axis=0, tiled=True)
    expert_sums = jnp.sum(got.astype(F32), axis=0)

    def columns(rows):
        cut = rows[:, :D].reshape(T, 8, SLICE).transpose(1, 0, 2)
        return jnp.pad(cut, ((0, 0), (0, 0), (0, 256 - SLICE)))

    left = jnp.concatenate(
        [jnp.concatenate([columns(kept[m][2]), columns(kept[m][4]), columns(kept[m][6])], axis=2) for m in micros], axis=1
    )
    left = lax.all_to_all(left, "shard", split_axis=0, concat_axis=0, tiled=True)
    msgs = [b for m in micros for b in gather_blocks(final[m][2])]
    datts = [b for m in micros for b in gather_blocks(final[m][3])]
    gq, go, gr, gg = attn_grad(order, left, msgs, datts)
    gg = lax.dynamic_slice(gg[:2], (0, shard * SLICE), (2, SLICE))
    small = jnp.concatenate([gr[:, :N_EXPERTS], gg.T], axis=1).astype(BF)
    small = jnp.pad(small, ((0, 0), (0, 64 - small.shape[1])))

    def pieces(rows):
        return rows.reshape(SLICE, 8, -1).transpose(1, 0, 2)

    send = jnp.concatenate(
        [pieces(gq[:, :D]), pieces(gq[:, D:]), jnp.broadcast_to(small[None], (8, SLICE, 64)), pieces(go)], axis=2
    )
    got = lax.all_to_all(send, "rep", split_axis=0, concat_axis=0, tiled=True)
    sums = jnp.sum(got.astype(F32), axis=0)
    g_q, g_kv, g_small, g_o = sums[:, :SLICE], sums[:, SLICE : SLICE + 64], sums[:, SLICE + 64 : SLICE + 128], sums[:, SLICE + 128 :]

    return (
        jnp.stack(acts)[None, :, None],
        jnp.stack([final[m][0] for m in micros])[None, :, None],
        g_small[None, :, N_EXPERTS],
        g_q[None],
        g_kv[None],
        g_o[None],
        g_small[None, :, N_EXPERTS + 1],
        g_small[None, :, :N_EXPERTS],
        expert_sums[None, None, :SLICE],
        expert_sums[None, None, SLICE:],
    )


def solution(mesh):
    in_specs = (
        P(None, "rep", "shard", None),
        P(None, "rep", "shard", None),
        P("section", None, "rep", "shard", None),
        P("section", "shard"),
        P("section", "shard", None),
        P("section", "shard", None),
        P("section", "shard", None),
        P("section", "shard"),
        P("section", "shard", None),
        P("section", "shard", None, None),
        P("section", "shard", None, None),
    )
    out_specs = (
        P("section", None, "rep", "shard", None),
        P("section", None, "rep", "shard", None),
        P("section", "shard"),
        P("section", "shard", "rep"),
        P("section", "shard", "rep"),
        P("section", "shard", "rep"),
        P("section", "shard"),
        P("section", "shard", None),
        P("section", "shard", "rep", None),
        P("section", "shard", "rep", None),
    )
    return jax.shard_map(body, mesh=mesh, in_specs=in_specs, out_specs=out_specs, check_vma=False)
```

```python
import jax
import jax.numpy as jnp
from jax import lax
from jax.experimental import pallas as pl
from jax.experimental.pallas import tpu as pltpu
from jax.sharding import PartitionSpec as P

D = 1536
T = 64
R = 2 * T
C = 4 * T
HEADS = 12
KV_HEADS = 2
GROUP = HEADS // KV_HEADS
HS = 128
KW = KV_HEADS * HS
SLICE = D // 8
FF = 768
SEQ = 512
N_EXPERTS = 8
LANES = 128
EPS = 1e-06
ROPE_BASE = 1000000.0
SCALE = HS**-0.5
BF = jnp.bfloat16
VMEM = 24 * 2**20
F32 = jnp.float32

NN = (((1,), (0,)), ((), ()))
NT = (((1,), (1,)), ((), ()))
TN = (((0,), (0,)), ((), ()))


def mm(a, b, dims=NN):
    return lax.dot_general(a, b, dims, preferred_element_type=F32)


def sds(shape, dtype):
    return jax.ShapeDtypeStruct(shape, dtype)


def whole(shape):
    return pl.BlockSpec(shape, lambda *_: (0,) * len(shape))


def call(kernel, name, grid, in_specs, out_specs, out_shape, scratch, flops, nbytes, *args):
    return pl.pallas_call(
        kernel,
        name=name,
        grid=grid,
        in_specs=in_specs,
        out_specs=out_specs,
        out_shape=out_shape,
        scratch_shapes=scratch,
        compiler_params=pltpu.CompilerParams(
            dimension_semantics=("arbitrary",) * len(grid), vmem_limit_bytes=VMEM
        ),
        cost_estimate=pl.CostEstimate(flops=flops, bytes_accessed=nbytes, transcendentals=0),
    )(*args)


def swap(x):
    return lax.ppermute(x, "shard", [(i, i ^ 1) for i in range(8)])


def along_y(x, k):
    return lax.ppermute(x, "shard", [(i, (i + 2 * k) % 8) for i in range(8)])


def from_chips(x):
    return [x, along_y(x, 1), along_y(x, 2), along_y(x, 3)]


def to_chips(blocks):
    return [blocks[0]] + [along_y(blocks[k], -k) for k in (1, 2, 3)]


def gather_blocks(x):
    same = from_chips(x)
    return same + [swap(b) for b in same]


def z_near(x):
    return lax.ppermute(x, "rep", [(i, (i // 2 ^ 1) * 2 + i % 2) for i in range(8)])


def z_far(x):
    return lax.ppermute(x, "rep", [(i, (3 - i // 2) * 2 + i % 2) for i in range(8)])


def x_pair(x):
    return lax.ppermute(x, "rep", [(i, i ^ 1) for i in range(8)])


def plus(a, b):
    return (a.astype(F32) + b.astype(F32)).astype(BF)


def rope(x, cos, sin):
    return x * cos + pltpu.roll(x, HS // 2, 1) * sin


def rope_back(x, cos, sin):
    return x * cos - pltpu.roll(x, HS // 2, 1) * sin


def qkv_kernel(x0_ref, x1_ref, gain_ref, w_ref, cos_ref, sin_ref, q_ref, kv_ref, h_ref):
    j = pl.program_id(0)

    @pl.when(j == 0)
    def _():
        for m, x_ref in enumerate((x0_ref, x1_ref)):
            x = x_ref[...].astype(F32)
            r = lax.rsqrt(jnp.mean(x * x, axis=-1, keepdims=True) + EPS)
            h_ref[m * T : (m + 1) * T, :] = (x * r * gain_ref[0:1, :]).astype(BF)

    y = mm(h_ref[...], w_ref[...])
    cos, sin = cos_ref[...], sin_ref[...]

    @pl.when(j < 3)
    def _():
        for i in range(4):
            at = slice(i * HS, (i + 1) * HS)
            q_ref[:, at] = rope(y[:, at], cos, sin).astype(BF)

    @pl.when(j == 3)
    def _():
        for i in range(2):
            at = slice(i * HS, (i + 1) * HS)
            kv_ref[:, at] = rope(y[:, at], cos, sin).astype(BF)
        kv_ref[:, KW:] = y[:, KW:].astype(BF)


def qkv(x0, x1, gains, w, cos, sin):
    return call(
        qkv_kernel, "qkv", (4,),
        [whole((T, D)), whole((T, D)), whole((8, D)), pl.BlockSpec((D, 512), lambda j: (0, j)), whole((R, HS)), whole((R, HS))],
        [pl.BlockSpec((R, 512), lambda j: (0, jnp.minimum(j, 2))), whole((R, 512)), whole((R, D))],
        [sds((R, D), BF), sds((R, 512), BF), sds((R, D), BF)],
        [], 2 * R * D * 2048, 7 * 10**6,
        x0, x1, gains, w, cos, sin,
    )


def stack_keys(kv_refs, kv_s):
    for m in range(2):
        for i, b in enumerate(kv_refs):
            kv_s[m, i * T : (i + 1) * T, :] = b[m * T : (m + 1) * T, :]


def heads_of(ref, m, k):
    rows = slice(m * T, (m + 1) * T)
    return jnp.concatenate([ref[rows, h * HS : (h + 1) * HS] for h in range(k * GROUP, (k + 1) * GROUP)], axis=0)


def probs_of(q6, keys, allowed):
    s = mm(q6, keys, NT) * SCALE
    s = jnp.where(allowed[None] > 0, s.reshape(GROUP, T, SEQ), -1e30)
    e = jnp.exp(s - jnp.max(s, axis=-1, keepdims=True))
    p = e * (1.0 / jnp.sum(e, axis=-1, keepdims=True))
    return p.reshape(GROUP * T, SEQ)


def attend_kernel(save, *refs):
    q_ref, kv_refs, rest = refs[0], refs[1:9], refs[9:]
    allowed_ref, x0_ref, x1_ref, w_ref, gain_ref, wr_ref, chosen_ref = rest[:7]
    if save:
        h_ref, att_ref, mid_ref, hm0_ref, hm1_ref, left_ref, kv_s, mid_s = rest[7:]
    else:
        att_ref, mid_ref, hm0_ref, hm1_ref, kv_s, mid_s = rest[7:]
    j = pl.program_id(0)

    @pl.when(j == 0)
    def _():
        stack_keys(kv_refs, kv_s)
        allowed = allowed_ref[...]
        for m in range(2):
            for k in range(KV_HEADS):
                p = probs_of(heads_of(q_ref, m, k), kv_s[m, :, k * HS : (k + 1) * HS], allowed).astype(BF)
                o = mm(p, kv_s[m, :, KW + k * HS : KW + (k + 1) * HS])
                for g in range(GROUP):
                    h = k * GROUP + g
                    att_ref[m * T : (m + 1) * T, h * HS : (h + 1) * HS] = o[g * T : (g + 1) * T].astype(BF)

    mid_s[j] = mm(att_ref[...], w_ref[...])

    @pl.when(j == 2)
    def _():
        for m, (x_ref, hm_ref) in enumerate(((x0_ref, hm0_ref), (x1_ref, hm1_ref))):
            rows = slice(m * T, (m + 1) * T)
            mids = [x_ref[:, i * 512 : (i + 1) * 512].astype(F32) + mid_s[i, rows] for i in range(3)]
            square = sum(jnp.sum(v * v, axis=-1, keepdims=True) for v in mids)
            r = lax.rsqrt(square * (1.0 / D) + EPS)
            logits = jnp.zeros((T, LANES), F32)
            for i in range(3):
                at = slice(i * 512, (i + 1) * 512)
                mid_ref[rows, at] = mids[i]
                h = (mids[i] * r * gain_ref[1:2, at]).astype(BF)
                hm_ref[:, at] = h
                logits = logits + mm(h, wr_ref[at, :])
            chosen = chosen_ref[rows, :] > 0
            top = jnp.max(jnp.where(chosen, logits, -jnp.inf), axis=-1, keepdims=True)
            e = jnp.where(chosen, jnp.exp(jnp.minimum(logits - top, 0.0)), 0.0)
            gate = e / jnp.sum(e, axis=-1, keepdims=True)
            high = gate.astype(BF).astype(F32)
            hm_ref[:, D:] = (high + pltpu.roll(gate - high, N_EXPERTS, 1)).astype(BF)
            if save:
                for a in range(3):
                    for i in range(8):
                        cut = slice(i * SLICE, (i + 1) * SLICE)
                        rows_of = hm_ref[:, cut] if a == 2 else (h_ref, att_ref)[a][rows, cut]
                        left_ref[i, rows, a * 256 : a * 256 + SLICE] = rows_of
                        left_ref[i, rows, a * 256 + SLICE : (a + 1) * 256] = jnp.zeros((T, 256 - SLICE), BF)


def attend(q, kvs, allowed, x0, x1, w, gains, chosen, h_attn, save):
    more = [h_attn] if save else []
    return call(
        lambda *refs: attend_kernel(save, *refs), "attend", (3,),
        [whole((R, D))] + [whole((R, 512))] * 8
        + [whole((T, SEQ)), whole((T, D)), whole((T, D)), pl.BlockSpec((D, 512), lambda j: (0, 4 + j)), whole((8, D)),
           pl.BlockSpec((D, LANES), lambda j: (0, 28)), whole((R, LANES))]
        + [whole((R, D)) for _ in more],
        [whole((R, D)), whole((R, D)), whole((T, D + LANES)), whole((T, D + LANES))] + [whole((8, R, 768)) for _ in more],
        [sds((R, D), BF), sds((R, D), F32), sds((T, D + LANES), BF), sds((T, D + LANES), BF)] + [sds((8, R, 768), BF) for _ in more],
        [pltpu.VMEM((2, SEQ, 512), BF), pltpu.VMEM((3, R, 512), F32)],
        2 * R * D * D + 4 * R * D * SEQ, 8 * 10**6,
        q, *kvs, allowed, x0, x1, w, gains, w, chosen, *more,
    )


FW = D + FF
GW = 2 * D


def expert_kernel(save, *refs):
    hm_refs, (mine_ref, wg_ref, wu_ref, wd_ref), outs, rest = refs[:4], refs[4:8], refs[8:12], refs[12:]
    if save:
        f_refs, (g_ref, gate_ref, up_ref, prod_ref, acc, total) = rest[:2], rest[2:]
        h_ref = f_refs[0]
    else:
        h_ref, g_ref, acc, total = rest
    j = pl.program_id(0)

    @pl.when(j == 0)
    def _():
        for i, b in enumerate(hm_refs):
            at = slice(i * T, (i + 1) * T)
            h_ref[at, :D] = b[:, :D]
            lanes = b[:, D:].astype(F32)
            for e in range(2):
                g = jnp.sum(lanes * mine_ref[e : e + 1, :], axis=-1, keepdims=True)
                g_ref[e, at, :] = jnp.broadcast_to(g, (T, LANES))
        if save:
            f_refs[1][:, :D] = f_refs[0][:, :D]

    h = h_ref[:, :D]
    gate = mm(h, wg_ref[0])
    up = mm(h, wu_ref[0])
    act = (gate / (1.0 + jnp.exp(-gate)) * up).astype(BF)
    if save:
        gate_ref[0] = gate
        up_ref[0] = up
        for step in range(6):

            @pl.when(j == step)
            def _(step=step):
                at = D + (step % 3) * 256
                f_refs[step // 3][:, at : at + 256] = act

    add = mm(act, wd_ref[0])

    @pl.when(j % 3 == 0)
    def _():
        acc[...] = add

    @pl.when(j % 3 > 0)
    def _():
        acc[...] += add

    @pl.when(j == 2)
    def _():
        prod = acc[...].astype(BF)
        if save:
            prod_ref[0] = prod
        total[...] = prod.astype(F32) * g_ref[0, :, 0:1]

    @pl.when(j == 5)
    def _():
        prod = acc[...].astype(BF)
        if save:
            prod_ref[1] = prod
        part = (total[...] + prod.astype(F32) * g_ref[1, :, 0:1]).astype(BF)
        for i, o in enumerate(outs):
            o[...] = part[i * T : (i + 1) * T]


def expert(hms, mine, w_in, w_down, save):
    f_block = pl.BlockSpec((1, C, 256), lambda j: (j // 3, 0, j % 3))
    out_specs = [whole((T, D))] * 4
    out_shape = [sds((T, D), BF)] * 4
    scratch = [pltpu.VMEM((C, D), F32), pltpu.VMEM((C, D), F32)]
    if save:
        out_specs += [whole((C, FW)), whole((C, FW)), whole((2, C, LANES)), f_block, f_block, whole((2, C, D))]
        out_shape += [sds((C, FW), BF), sds((C, FW), BF), sds((2, C, LANES), F32), sds((2, C, FF), F32), sds((2, C, FF), F32), sds((2, C, D), BF)]
    else:
        scratch = [pltpu.VMEM((C, D), BF), pltpu.VMEM((2, C, LANES), F32)] + scratch
    return call(
        lambda *refs: expert_kernel(save, *refs), "expert", (6,),
        [whole((T, D + LANES))] * 4
        + [whole((8, LANES)), pl.BlockSpec((1, D, 256), lambda j: (j // 3, 0, j % 3)), pl.BlockSpec((1, D, 256), lambda j: (j // 3, 0, j % 3 + 3)),
           pl.BlockSpec((1, 256, D), lambda j: (j // 3, j % 3, 0))],
        out_specs, out_shape, scratch, 12 * C * D * FF, 18 * 10**6,
        *hms, mine, w_in, w_in, w_down,
    )


def expert_back_kernel(save, *refs):
    gs, (g_ref, gate_ref, up_ref, prod_ref, put_ref, wd_ref, wg_ref, wu_ref), outs, rest = refs[:4], refs[4:12], refs[12:16], refs[16:]
    if save:
        d_refs, (lanes_s, dprod, acc, total) = rest[:2], rest[2:]
    else:
        lanes_s, dprod, acc, total = rest
    j = pl.program_id(0)

    for e in range(2):

        @pl.when(j == 3 * e)
        def _(e=e):
            put = put_ref[...]
            for i, b in enumerate(gs):
                at = slice(i * T, (i + 1) * T)
                g = b[...].astype(F32)
                d_prod = (g * g_ref[e, at, 0:1]).astype(BF)
                dprod[at, :] = d_prod
                if save:
                    d_refs[e][at, D:] = d_prod
                d = jnp.sum(g * prod_ref[e, at, :].astype(F32), axis=-1, keepdims=True)
                high = d.astype(BF).astype(F32)
                lanes = high * put[2 * e : 2 * e + 1, :] + (d - high) * put[2 * e + 1 : 2 * e + 2, :]
                lanes_s[at, :] = lanes if e == 0 else lanes_s[at, :] + lanes

    d_act = mm(dprod[...], wd_ref[0], NT)
    gate, up = gate_ref[0], up_ref[0]
    s = 1.0 / (1.0 + jnp.exp(-gate))
    dg = (d_act * up * (s * (1.0 + gate * (1.0 - s)))).astype(BF)
    du = (d_act * (gate * s)).astype(BF)
    if save:
        for step in range(6):

            @pl.when(j == step)
            def _(step=step):
                at = (step % 3) * 256
                d_refs[step // 3][:, at : at + 256] = dg
                d_refs[step // 3][:, FF + at : FF + at + 256] = du

    add = mm(dg, wg_ref[0], NT) + mm(du, wu_ref[0], NT)

    @pl.when(j % 3 == 0)
    def _():
        acc[...] = add

    @pl.when(j % 3 > 0)
    def _():
        acc[...] += add

    @pl.when(j == 2)
    def _():
        total[...] = acc[...].astype(BF).astype(F32)

    @pl.when(j == 5)
    def _():
        part = (total[...] + acc[...].astype(BF).astype(F32)).astype(BF)
        for i, o in enumerate(outs):
            at = slice(i * T, (i + 1) * T)
            o[:, :D] = part[at]
            o[:, D:] = lanes_s[at, :].astype(BF)


def expert_back(gs, kept, put, w_in, w_down, save):
    g_share, gate, up, produced = kept
    f_block = pl.BlockSpec((1, C, 256), lambda j: (j // 3, 0, j % 3))
    out_specs = [whole((T, D + LANES))] * 4
    out_shape = [sds((T, D + LANES), BF)] * 4
    if save:
        out_specs += [whole((C, GW))] * 2
        out_shape += [sds((C, GW), BF)] * 2
    return call(
        lambda *refs: expert_back_kernel(save, *refs), "expert_back", (6,),
        [whole((T, D))] * 4
        + [whole((2, C, LANES)), f_block, f_block, whole((2, C, D)), whole((8, LANES)),
           pl.BlockSpec((1, 256, D), lambda j: (j // 3, j % 3, 0)), pl.BlockSpec((1, D, 256), lambda j: (j // 3, 0, j % 3)),
           pl.BlockSpec((1, D, 256), lambda j: (j // 3, 0, j % 3 + 3))],
        out_specs, out_shape,
        [pltpu.VMEM((C, LANES), F32), pltpu.VMEM((C, D), BF), pltpu.VMEM((C, D), F32), pltpu.VMEM((C, D), F32)],
        12 * C * D * FF, 20 * 10**6,
        *gs, g_share, gate, up, produced, put, w_down, w_in, w_in,
    )


def norm_back(x, gain, grad):
    r = lax.rsqrt(jnp.mean(x * x, axis=-1, keepdims=True) + EPS)
    n = x * r
    scaled = grad * gain
    back = r * (scaled - n * jnp.mean(scaled * n, axis=-1, keepdims=True))
    return jnp.sum(grad * n, axis=0, keepdims=True), back


def attend_back_kernel(*refs):
    rets, g_refs, mid_ref, hm_refs, rest = refs[:8], refs[8:10], refs[10], refs[11:13], refs[13:]
    gain_ref, wr_ref, w0_ref, w1_ref, w2_ref, q_ref = rest[:6]
    kv_refs, rest = rest[6:14], rest[14:]
    allowed_ref, cos_ref, sin_ref, dmid_ref, datt_ref, dq_ref, same_ref, other_ref, dl_ref, gain_out, da, kv_s, kv_acc = rest
    j = pl.program_id(0)

    @pl.when(j == 0)
    def _():
        grads = jnp.zeros((1, D), F32)
        for m in range(2):
            rows = slice(m * T, (m + 1) * T)
            total = sum(r[...].astype(F32) for r in rets[4 * m : 4 * m + 4])
            lanes = total[:, D:]
            d_gate = lanes + pltpu.roll(lanes, LANES - N_EXPERTS, 1)
            share = hm_refs[m][:, D:].astype(F32)
            gate = share + pltpu.roll(share, LANES - N_EXPERTS, 1)
            gate = jnp.where(lax.broadcasted_iota(jnp.int32, (T, LANES), 1) < N_EXPERTS, gate, 0.0)
            inner = jnp.sum(gate * d_gate, axis=-1, keepdims=True)
            d_logits = (gate * (d_gate - inner)).astype(BF)
            dl_ref[rows, :] = d_logits
            d_hm = total[:, :D] + mm(d_logits, wr_ref[...], NT)
            grad_gain, back = norm_back(mid_ref[rows, :], gain_ref[1:2, :], d_hm)
            grads = grads + grad_gain
            d_mid = g_refs[m][...].astype(F32) + back
            dmid_ref[rows, :] = d_mid
            datt_ref[rows, :] = d_mid.astype(BF)
        gain_out[...] = jnp.broadcast_to(grads, (8, D))
        stack_keys(kv_refs, kv_s)

    piece = mm(datt_ref[:, 0:512], w0_ref[...], NT) + mm(datt_ref[:, 512:1024], w1_ref[...], NT) + mm(datt_ref[:, 1024:], w2_ref[...], NT)
    piece = piece.astype(BF)
    for m in range(2):
        for i in range(3):
            da[m, j * 3 + i] = piece[m * T : (m + 1) * T, i * HS : (i + 1) * HS]

    @pl.when(j == 3)
    def _():
        allowed = allowed_ref[...]
        cos, sin = cos_ref[:T, :], sin_ref[:T, :]
        for m in range(2):
            rows = slice(m * T, (m + 1) * T)
            for k in range(KV_HEADS):
                keys = kv_s[m, :, k * HS : (k + 1) * HS]
                values = kv_s[m, :, KW + k * HS : KW + (k + 1) * HS]
                q6 = heads_of(q_ref, m, k)
                d6 = da[m, k * GROUP : (k + 1) * GROUP].reshape(GROUP * T, HS)
                p = probs_of(q6, keys, allowed)
                dp = mm(d6, values, NT)
                ds = (p * (dp - jnp.sum(p * dp, axis=-1, keepdims=True)) * SCALE).astype(BF)
                dq = mm(ds, keys)
                for g in range(GROUP):
                    h = k * GROUP + g
                    dq_ref[rows, h * HS : (h + 1) * HS] = rope_back(dq[g * T : (g + 1) * T], cos, sin).astype(BF)
                kv_acc[:, k * HS : (k + 1) * HS] = mm(ds, q6, TN)
                kv_acc[:, KW + k * HS : KW + (k + 1) * HS] = mm(p.astype(BF), d6, TN)
            for i in range(4):
                at = slice(i * R + m * T, i * R + (m + 1) * T)
                same_ref[at, :] = kv_acc[i * T : (i + 1) * T].astype(BF)
                other_ref[at, :] = kv_acc[C + i * T : C + (i + 1) * T].astype(BF)


def attend_back(rets, gs, mid, hms, gains, w, q, kvs, allowed, cos, sin):
    return call(
        attend_back_kernel, "attend_back", (4,),
        [whole((T, D + LANES))] * 8 + [whole((T, D))] * 2 + [whole((R, D))] + [whole((T, D + LANES))] * 2
        + [whole((8, D)), pl.BlockSpec((D, LANES), lambda j: (0, 28))]
        + [pl.BlockSpec((384, 512), lambda j, c=c: (j, 4 + c)) for c in range(3)]
        + [whole((R, D))] + [whole((R, 512))] * 8 + [whole((T, SEQ)), whole((R, HS)), whole((R, HS))],
        [whole((R, D)), whole((R, D)), whole((R, D)), whole((4 * R, 512)), whole((4 * R, 512)), whole((R, LANES)), whole((8, D))],
        [sds((R, D), F32), sds((R, D), BF), sds((R, D), BF), sds((4 * R, 512), BF), sds((4 * R, 512), BF), sds((R, LANES), BF), sds((8, D), F32)],
        [pltpu.VMEM((2, HEADS, T, HS), BF), pltpu.VMEM((2, SEQ, 512), BF), pltpu.VMEM((SEQ, 512), F32)],
        2 * R * D * D + 10 * R * D * SEQ, 8 * 10**6,
        *rets, *gs, mid, *hms, gains, w, w, w, w, q, *kvs, allowed, cos, sin,
    )


MSG = 512 + LANES


def qkv_back_kernel(*refs):
    rets, (dq_ref, dl_ref, gm_ref, x0_ref, x1_ref, gain_ref, w_ref, cos_ref, sin_ref, dmid_ref), rest = refs[:4], refs[4:14], refs[14:]
    gin_ref, low0_ref, low1_ref, msg_ref, dh = rest
    j = pl.program_id(0)

    @pl.when(j == 0)
    def _():
        d_kv = sum(r[...].astype(F32) for r in rets)
        cos, sin = cos_ref[...], sin_ref[...]
        for i in range(KV_HEADS):
            at = slice(i * HS, (i + 1) * HS)
            msg_ref[:R, at] = rope_back(d_kv[:, at], cos, sin).astype(BF)
        msg_ref[:R, KW:512] = d_kv[:, KW:].astype(BF)
        msg_ref[:R, 512:] = dl_ref[...]

    dh[j] = mm(dq_ref[...], w_ref[:, :D], NT) + mm(msg_ref[:R, :512], w_ref[:, D:], NT)

    @pl.when(j == 3)
    def _():
        d_h = jnp.concatenate([dh[i] for i in range(4)], axis=1)
        grads = jnp.zeros((1, D), F32)
        for m, (x_ref, low_ref) in enumerate(((x0_ref, low0_ref), (x1_ref, low1_ref))):
            rows = slice(m * T, (m + 1) * T)
            grad_gain, back = norm_back(x_ref[...].astype(F32), gain_ref[0:1, :], d_h[rows])
            grads = grads + grad_gain
            g_in = dmid_ref[rows, :] + back
            gin_ref[rows, :] = g_in
            low_ref[...] = g_in.astype(BF)
        for c in range(3):
            at = slice(c * 512, (c + 1) * 512)
            row = lax.broadcasted_iota(jnp.int32, (16, 512), 0)
            both = jnp.where(row == c, jnp.broadcast_to(grads[:, at], (16, 512)), 0.0)
            both = both + jnp.where(row == 3 + c, jnp.broadcast_to(gm_ref[0:1, at], (16, 512)), 0.0)
            msg_ref[R:, :512] = both.astype(BF) if c == 0 else msg_ref[R:, :512] + both.astype(BF)
        msg_ref[R:, 512:] = jnp.zeros((16, LANES), BF)


def qkv_back(rets, dq, dl, gm, x0, x1, gains, w, cos, sin, d_mid):
    return call(
        qkv_back_kernel, "qkv_back", (4,),
        [whole((R, 512))] * 4
        + [whole((R, D)), whole((R, LANES)), whole((8, D)), whole((T, D)), whole((T, D)), whole((8, D)), pl.BlockSpec((384, 2048), lambda j: (j, 0)),
           whole((R, HS)), whole((R, HS)), whole((R, D))],
        [whole((R, D)), whole((T, D)), whole((T, D)), whole((R + 16, MSG))],
        [sds((R, D), F32), sds((T, D), BF), sds((T, D), BF), sds((R + 16, MSG), BF)],
        [pltpu.VMEM((4, R, 384), F32)],
        2 * R * D * 2048, 9 * 10**6,
        *rets, dq, dl, gm, x0, x1, gains, w, cos, sin, d_mid,
    )


def attn_grad_kernel(*refs):
    order_ref, left_ref = refs[0], refs[1]
    msgs, dqs, datts = refs[2:10], refs[10:18], refs[18:26]
    gq_ref, gkv_ref, go_ref, gr_ref, gain_ref = refs[26:31]
    lh, rq, ro, rm = refs[31:35]
    gains = jnp.zeros((16, 512), F32)
    for i in range(8):
        at = slice(i * R, (i + 1) * R)
        lh[at, :] = left_ref[order_ref[i]]
        rq[at, :] = dqs[i][...]
        ro[at, :] = datts[i][...]
        rm[at, :] = msgs[i][:R, :]
        gains = gains + msgs[i][R:, :512].astype(F32)
    gain_ref[...] = gains
    for c in range(3):
        at = slice(c * 512, (c + 1) * 512)
        gq_ref[:, at] = mm(lh[:, :256], rq[:, at], TN)[:SLICE].astype(BF)
        go_ref[:, at] = mm(lh[:, 256:512], ro[:, at], TN)[:SLICE].astype(BF)
    gkv_ref[...] = mm(lh[:, :256], rm[:, :512], TN)[:SLICE].astype(BF)
    gr_ref[...] = mm(lh[:, 512:], rm[:, 512:], TN)[:SLICE]


def attn_grad(order, left, msgs, dqs, datts):
    return pl.pallas_call(
        attn_grad_kernel,
        name="attn_grad",
        grid=(1,),
        in_specs=[pl.BlockSpec(memory_space=pltpu.SMEM)] + [whole(a.shape) for a in (left, *msgs, *dqs, *datts)],
        out_specs=[whole((SLICE, D)), whole((SLICE, 512)), whole((SLICE, D)), whole((SLICE, LANES)), whole((16, 512))],
        out_shape=[sds((SLICE, D), BF), sds((SLICE, 512), BF), sds((SLICE, D), BF), sds((SLICE, LANES), F32), sds((16, 512), F32)],
        scratch_shapes=[pltpu.VMEM((8 * R, 768), BF), pltpu.VMEM((8 * R, D), BF), pltpu.VMEM((8 * R, D), BF), pltpu.VMEM((8 * R, MSG), BF)],
        compiler_params=pltpu.CompilerParams(vmem_limit_bytes=32 * 2**20),
        cost_estimate=pl.CostEstimate(flops=2 * 1024 * 256 * 3584, bytes_accessed=10 * 10**6, transcendentals=0),
    )(order, left, *msgs, *dqs, *datts)


def expert_grad_kernel(part, places, order_ref, *refs):
    lefts, rights, out_ref, turned, result = refs[:4], refs[4:8], refs[8], refs[9], refs[10]
    j = pl.program_id(0)
    rows = out_ref.shape[1]

    @pl.when(j == 0)
    def _():
        for i, left in enumerate(lefts):
            turned[:, i * C : (i + 1) * C] = left[:, part].T

    result[...] = sum(mm(turned[:, i * C : (i + 1) * C], rights[i][...]) for i in range(4))
    for i in range(8):
        out_ref[i] = result[pl.ds(pl.multiple_of(order_ref[i] * rows, rows), rows), :].astype(BF)


def expert_grad(order, lefts, rights, part, first, blocks):
    width = part.stop - part.start
    return pl.pallas_call(
        lambda *refs: expert_grad_kernel(part, None, *refs),
        name="expert_grad",
        grid_spec=pltpu.PrefetchScalarGridSpec(
            num_scalar_prefetch=1,
            grid=(blocks,),
            in_specs=[pl.BlockSpec((C, FW), lambda j, o: (0, 0))] * 4 + [pl.BlockSpec((C, 256), lambda j, o: (0, first + j))] * 4,
            out_specs=pl.BlockSpec((8, width // 8, 256), lambda j, o: (0, 0, j)),
            scratch_shapes=[pltpu.VMEM((width, 4 * C), BF), pltpu.VMEM((width, 256), F32)],
        ),
        out_shape=sds((8, width // 8, 256 * blocks), BF),
        compiler_params=pltpu.CompilerParams(dimension_semantics=("arbitrary",), vmem_limit_bytes=VMEM),
        cost_estimate=pl.CostEstimate(flops=2 * 4 * C * width * 256 * blocks, bytes_accessed=8 * 10**6, transcendentals=0),
    )(order, *lefts, *rights)


def body(tokens_in, cotangent, routes, gain_attn, w_query, w_keyval, w_out, gain_moe, w_router, w_in, w_down):
    is_first = lax.axis_index("section") == 0
    shard = lax.axis_index("shard")
    rep = lax.axis_index("rep")
    chip, core = shard // 2, shard % 2
    micros = range(2)

    extra = jnp.concatenate([w_router[0], gain_attn[0][:, None], gain_moe[0][:, None]], axis=1)
    extra = jnp.pad(extra, ((0, 0), (0, LANES - extra.shape[1])))
    packed = jnp.concatenate([w_query[0], w_keyval[0], w_out[0], extra], axis=1)
    w = lax.all_gather(packed, "shard", axis=0, tiled=True)
    pick = (jnp.arange(LANES)[None, :] == (jnp.arange(8)[:, None] + N_EXPERTS)) & (jnp.arange(8)[:, None] < 2)
    gains = mm(pick.astype(BF), w[:, 3584:], NT)
    inner = jnp.stack([w_in[0, 0], swap(w_in[0, 0])])
    outer = jnp.stack([w_down[0, 0], swap(w_down[0, 0])])

    w, gains, inner, outer = lax.optimization_barrier((w, gains, inner, outer))

    half = HS // 2
    frequency = ROPE_BASE ** (-jnp.arange(half, dtype=F32) * 2.0 / HS)
    place = shard * T + jnp.arange(T, dtype=jnp.int32)
    angles = place.astype(F32)[:, None] * frequency[None, :]
    angles = jnp.concatenate([angles, angles], axis=0)
    cos = jnp.concatenate([jnp.cos(angles)] * 2, axis=1)
    sin = jnp.concatenate([-jnp.sin(angles), jnp.sin(angles)], axis=1)
    order = jnp.stack([((chip - k) % 4) * 2 + c for c in (core, 1 - core) for k in range(4)]).astype(jnp.int32)
    key_place = (order[:, None] * T + jnp.arange(T, dtype=jnp.int32)[None, :]).reshape(1, SEQ)
    allowed = (key_place <= place[:, None]).astype(F32)
    lane = jnp.arange(LANES, dtype=jnp.int32)
    other = shard ^ 1
    mine = jnp.stack([(lane == e) | (lane == e + N_EXPERTS) for e in (shard, other)]).astype(F32)
    mine = jnp.pad(mine, ((0, 6), (0, 0)))
    put = jnp.stack([lane == shard, lane == shard + N_EXPERTS, lane == other, lane == other + N_EXPERTS]).astype(F32)
    put = jnp.pad(put, ((0, 4), (0, 0)))
    chosen = jnp.any(routes[0, :, 0].reshape(R, -1)[:, :, None] == lane[None, None, :], axis=1).astype(F32)

    def layer(x, save):
        q, kv, h_attn = qkv(x[0], x[1], gains, w, cos, sin)
        kvs = gather_blocks(kv)
        att, mid, hm0, hm1, *left = attend(q, kvs, allowed, x[0], x[1], w, gains, chosen, h_attn, save)
        hms = (hm0, hm1)
        y, more = [], []
        for m in micros:
            out = expert(from_chips(hms[m]), mine, inner, outer, save)
            rets = to_chips(out[:4])
            y.append((mid[m * T : (m + 1) * T] + sum(r.astype(F32) for r in rets)).astype(BF))
            more.append(out[4:])
        return y, (x, q, kvs, mid, hms), more, left

    def layer_back(g, kept, more, save, beside):
        x, q, kvs, mid, hms = kept
        rets, saved = [], []
        for m in micros:
            g_share, gate, up, produced = more[m][2:]
            out = expert_back(from_chips(g[m]), (g_share, gate, up, produced), put, inner, outer, save)
            rets += to_chips(out[:4])
            saved.append(out[4:])
        rets, sends = lax.optimization_barrier((rets, beside(saved)))
        d_mid, d_att, dq, kv_same, kv_other, dl, gm = attend_back(rets, g, mid, hms, gains, w, q, kvs, allowed, cos, sin)
        got = swap(kv_other)
        kv_rets = to_chips([plus(kv_same[k * R : (k + 1) * R], got[k * R : (k + 1) * R]) for k in range(4)])
        kv_rets, dq, d_att = lax.optimization_barrier((kv_rets, dq, d_att))
        g_in, low0, low1, msg = qkv_back(kv_rets, dq, dl, gm, x[0], x[1], gains, w, cos, sin, d_mid)
        return g_in, (low0, low1), msg, dq, d_att, sends

    tokens = [tokens_in[m, 0] for m in micros]
    given = [cotangent[m, 0] for m in micros]
    first, *_ = layer(tokens, False)
    arrived = [lax.ppermute(first[m], "section", [(0, 1)]) for m in micros]
    inputs = [jnp.where(is_first, tokens[m], arrived[m]) for m in micros]
    acts, kept, more, left = layer(inputs, True)
    left = lax.all_to_all(left[0], "shard", split_axis=0, concat_axis=0, tiled=True)
    f_own = [more[m][0] for m in micros]
    f_got = [swap(more[m][1]) for m in micros]

    z, x_lo = rep // 2, rep % 2
    rep_order = jnp.stack([zz * 2 + xx for zz in (z, 3 - z, z ^ 1, (3 - z) ^ 1) for xx in (x_lo, 1 - x_lo)]).astype(jnp.int32)

    def weights(saved):
        rights = [saved[m][0] for m in micros] + [swap(saved[m][1]) for m in micros]
        send_in = expert_grad(rep_order, lefts, rights, slice(0, D), 0, 6)
        send_down = expert_grad(rep_order, lefts, rights, slice(D, FW), 6, 6)
        return send_in.reshape(4, 2, SLICE, D), send_down.reshape(4, 2, SLICE // 2, D)

    def reduce_first(sends):
        send_in, send_down = sends
        near = send_in[..., :FF]
        far = send_in[..., FF:]
        near = plus(near[0:2], z_near(near[2:4]))
        got = z_far(jnp.concatenate([far[1:2], far[3:4]], axis=0))
        far = plus(jnp.concatenate([far[0:1], far[2:3]], axis=0), got)
        down = plus(send_down[:, 0], x_pair(send_down[:, 1]))
        return near, far, down

    def reduce_second(sends):
        near, far, down = sends
        near = near[0].astype(F32) + z_far(near[1]).astype(F32)
        far = far[0].astype(F32) + z_near(far[1]).astype(F32)
        down_near, down_far = down[..., :FF], down[..., FF:]
        down_near = plus(down_near[0:2], z_near(down_near[2:4]))
        got = z_far(jnp.concatenate([down_far[1:2], down_far[3:4]], axis=0))
        down_far = plus(jnp.concatenate([down_far[0:1], down_far[2:3]], axis=0), got)
        return near, far, down_near, down_far

    def reduce_third(sends):
        near, far, down_near, down_far = sends
        halves = [v[0] + x_pair(v[1].astype(BF)).astype(F32) for v in (near, far)]
        downs = [
            down_near[0].astype(F32) + z_far(down_near[1]).astype(F32),
            down_far[0].astype(F32) + z_near(down_far[1]).astype(F32),
        ]
        return jnp.concatenate(halves, axis=1), jnp.concatenate(downs, axis=1)

    _, back, *_, (left, f_got) = layer_back(given, kept, more, False, lambda saved: (left, f_got))
    lefts = f_own + f_got
    arrived = [lax.ppermute(back[m], "section", [(1, 0)]) for m in micros]
    given = [jnp.where(is_first, arrived[m], given[m]) for m in micros]
    g_in, _, msg, dq, d_att, sends = layer_back(given, kept, more, True, weights)

    msg, sends = lax.optimization_barrier((msg, reduce_first(sends)))
    msgs, dqs, datts = gather_blocks(msg), gather_blocks(dq), gather_blocks(d_att)
    msgs, sends = lax.optimization_barrier((msgs, reduce_second(sends)))
    grad_in, grad_down = reduce_third(sends)
    gq, gkv, go, gr, gg = attn_grad(order, left, msgs, dqs, datts)
    gg = lax.dynamic_slice(gg[:6].reshape(2, D), (0, shard * SLICE), (2, SLICE))
    small = jnp.concatenate([gr[:, :N_EXPERTS], gg.T], axis=1).astype(BF)
    small = jnp.pad(small, ((0, 0), (0, 64 - small.shape[1])))

    def pieces(rows):
        return rows.reshape(SLICE, 8, -1).transpose(1, 0, 2)

    send = jnp.concatenate([pieces(gq), pieces(gkv), jnp.broadcast_to(small[None], (8, SLICE, 64)), pieces(go)], axis=2)
    got = lax.all_to_all(send, "rep", split_axis=0, concat_axis=0, tiled=True)
    sums = jnp.sum(got.astype(F32), axis=0)
    g_q, g_kv, g_small, g_o = sums[:, :SLICE], sums[:, SLICE : SLICE + 64], sums[:, SLICE + 64 : SLICE + 128], sums[:, SLICE + 128 :]

    return (
        jnp.stack(acts)[None, :, None],
        g_in.reshape(1, 2, 1, T, D),
        g_small[None, :, N_EXPERTS],
        g_q[None],
        g_kv[None],
        g_o[None],
        g_small[None, :, N_EXPERTS + 1],
        g_small[None, :, :N_EXPERTS],
        grad_in[None, None],
        grad_down[None, None],
    )


def solution(mesh):
    in_specs = (
        P(None, "rep", "shard", None),
        P(None, "rep", "shard", None),
        P("section", None, "rep", "shard", None),
        P("section", "shard"),
        P("section", "shard", None),
        P("section", "shard", None),
        P("section", "shard", None),
        P("section", "shard"),
        P("section", "shard", None),
        P("section", "shard", None, None),
        P("section", "shard", None, None),
    )
    out_specs = (
        P("section", None, "rep", "shard", None),
        P("section", None, "rep", "shard", None),
        P("section", "shard"),
        P("section", "shard", "rep"),
        P("section", "shard", "rep"),
        P("section", "shard", "rep"),
        P("section", "shard"),
        P("section", "shard", None),
        P("section", "shard", "rep", None),
        P("section", "shard", "rep", None),
    )
    return jax.shard_map(body, mesh=mesh, in_specs=in_specs, out_specs=out_specs, check_vma=False)
```

```python
import jax
import jax.numpy as jnp
from jax import lax
from jax.experimental import pallas as pl
from jax.experimental.pallas import tpu as pltpu
from jax.sharding import PartitionSpec as P

D = 1536
T = 64
R = 2 * T
C = 4 * T
HEADS = 12
KV_HEADS = 2
GROUP = HEADS // KV_HEADS
HS = 128
KW = KV_HEADS * HS
SLICE = D // 8
FF = 768
SEQ = 512
N_EXPERTS = 8
LANES = 128
EPS = 1e-06
ROPE_BASE = 1000000.0
SCALE = HS**-0.5
BF = jnp.bfloat16
VMEM = 24 * 2**20
F32 = jnp.float32

NN = (((1,), (0,)), ((), ()))
NT = (((1,), (1,)), ((), ()))
TN = (((0,), (0,)), ((), ()))


def mm(a, b, dims=NN):
    return lax.dot_general(a, b, dims, preferred_element_type=F32)


def sds(shape, dtype):
    return jax.ShapeDtypeStruct(shape, dtype)


def whole(shape):
    return pl.BlockSpec(shape, lambda *_: (0,) * len(shape))


def in_hbm(args):
    return [pltpu.with_memory_space_constraint(a, pltpu.HBM) for a in args]


HERE = pl.BlockSpec(memory_space=pltpu.VMEM)
AWAY = pl.BlockSpec(memory_space=pltpu.HBM)
SCALARS = pl.BlockSpec(memory_space=pltpu.SMEM)


def work(us):
    return pl.CostEstimate(flops=1, bytes_accessed=int(us * 3.7 * 10**6), transcendentals=0)


def call(kernel, name, here, away, outs, outs_away, scratch, us, vmem, scalars=None):
    scalars = [] if scalars is None else [scalars]
    return pl.pallas_call(
        kernel,
        name=name,
        in_specs=[SCALARS] * len(scalars) + [HERE] * len(here) + [AWAY] * len(away),
        out_specs=[HERE] * len(outs) + [AWAY] * len(outs_away),
        out_shape=outs + [pltpu.HBM(o.shape, o.dtype) for o in outs_away],
        scratch_shapes=scratch,
        compiler_params=pltpu.CompilerParams(vmem_limit_bytes=vmem * 2**20),
        cost_estimate=work(us),
    )(*scalars, *here, *in_hbm(away))


def fetch(src, dst, sem):
    copy = pltpu.make_async_copy(src, dst, sem)
    copy.start()
    return copy


def swap(x):
    return lax.ppermute(x, "shard", [(i, i ^ 1) for i in range(8)])


def along_y(x, k):
    return lax.ppermute(x, "shard", [(i, (i + 2 * k) % 8) for i in range(8)])


def from_chips(x):
    return [x, along_y(x, 1), along_y(x, 2), along_y(x, 3)]


def to_chips(blocks):
    return [blocks[0]] + [along_y(blocks[k], -k) for k in (1, 2, 3)]


def gather_blocks(x):
    same = from_chips(x)
    return same + [swap(b) for b in same]


def plus(a, b):
    return (a.astype(F32) + b.astype(F32)).astype(BF)


def rope(x, cos, sin):
    return x * cos + pltpu.roll(x, HS // 2, 1) * sin


def rope_back(x, cos, sin):
    return x * cos - pltpu.roll(x, HS // 2, 1) * sin


def qkv_kernel(x0_ref, x1_ref, gain_ref, cos_ref, sin_ref, w_ref, q_ref, kv_ref, h_ref, w_s, sems):
    copies = [fetch(w_ref.at[:, j * 512 : (j + 1) * 512], w_s.at[j], sems.at[j]) for j in range(4)]
    for m, x_ref in enumerate((x0_ref, x1_ref)):
        x = x_ref[...].astype(F32)
        r = lax.rsqrt(jnp.mean(x * x, axis=-1, keepdims=True) + EPS)
        h_ref[m * T : (m + 1) * T, :] = (x * r * gain_ref[0:1, :]).astype(BF)
    cos, sin = cos_ref[...], sin_ref[...]
    for j in range(4):
        copies[j].wait()
        y = mm(h_ref[...], w_s[j])
        for i in range(4 if j < 3 else 2):
            at = slice(i * HS, (i + 1) * HS)
            turned = rope(y[:, at], cos, sin).astype(BF)
            if j < 3:
                q_ref[:, j * 512 + i * HS : j * 512 + (i + 1) * HS] = turned
            else:
                kv_ref[:, at] = turned
        if j == 3:
            kv_ref[:, KW:] = y[:, KW:].astype(BF)


def qkv(x0, x1, gains, w, cos, sin):
    return call(
        qkv_kernel, "qkv", [x0, x1, gains, cos, sin], [w],
        [sds((R, D), BF), sds((R, 512), BF), sds((R, D), BF)], [],
        [pltpu.VMEM((4, D, 512), BF), pltpu.SemaphoreType.DMA((4,))],
        3.5, 10,
    )


def fetch_keys(kv_refs, kv_s, sems):
    return [
        fetch(kv_refs[i].at[m * T : (m + 1) * T, :], kv_s.at[m, i * T : (i + 1) * T, :], sems.at[m, i]) for i in range(1, 8) for m in range(2)
    ]


def own_keys(own, kv_s):
    for m in range(2):
        kv_s[m, 0:T, :] = own[m * T : (m + 1) * T, :]


def heads_of(ref, m, k):
    rows = slice(m * T, (m + 1) * T)
    return jnp.concatenate([ref[rows, h * HS : (h + 1) * HS] for h in range(k * GROUP, (k + 1) * GROUP)], axis=0)


def probs_of(q6, keys, allowed):
    s = mm(q6, keys, NT) * SCALE
    s = jnp.where(allowed[None] > 0, s.reshape(GROUP, T, SEQ), -1e30)
    e = jnp.exp(s - jnp.max(s, axis=-1, keepdims=True))
    p = e * (1.0 / jnp.sum(e, axis=-1, keepdims=True))
    return p.reshape(GROUP * T, SEQ)


def fetch_w_out(spots_ref, pieces, w_s, sems):
    copies = []
    for p, piece in enumerate(pieces):
        for k in range(4):
            i = p * 4 + k
            at = pl.ds(pl.multiple_of(spots_ref[i], 16), SLICE // 4)
            copies.append(fetch(piece.at[k], w_s.at[at, :], sems.at[i]))
    return copies


def attend_kernel(save, *refs):
    spots_ref, q_ref, own_ref, allowed_ref, x0_ref, x1_ref, gain_ref, chosen_ref, rest = *refs[:8], refs[8:]
    if save:
        h_ref, rest = rest[0], rest[1:]
    w_refs, wp_ref, kv_refs, rest = rest[:8], rest[8], (None,) + rest[9:16], rest[16:]
    if save:
        att_ref, mid_ref, hm0_ref, hm1_ref, left_ref, kv_s, w_s, wr_s, sems, kv_sems = rest
    else:
        att_ref, mid_ref, hm0_ref, hm1_ref, kv_s, w_s, wr_s, sems, kv_sems = rest
    key_copies = fetch_keys(kv_refs, kv_s, kv_sems)
    router_copy = fetch(wp_ref.at[:, 2048:], wr_s, sems.at[32])
    copies = fetch_w_out(spots_ref, w_refs, w_s, sems)
    own_keys(own_ref, kv_s)
    allowed = allowed_ref[...]
    for copy in key_copies:
        copy.wait()
    for m in range(2):
        for k in range(KV_HEADS):
            p = probs_of(heads_of(q_ref, m, k), kv_s[m, :, k * HS : (k + 1) * HS], allowed).astype(BF)
            o = mm(p, kv_s[m, :, KW + k * HS : KW + (k + 1) * HS])
            for g in range(GROUP):
                h = k * GROUP + g
                att_ref[m * T : (m + 1) * T, h * HS : (h + 1) * HS] = o[g * T : (g + 1) * T].astype(BF)
    square = [0.0, 0.0]
    for copy in copies:
        copy.wait()
    for j in range(3):
        at = slice(j * 512, (j + 1) * 512)
        y = mm(att_ref[...], w_s[:, at])
        for m, x_ref in enumerate((x0_ref, x1_ref)):
            rows = slice(m * T, (m + 1) * T)
            mid = x_ref[:, at].astype(F32) + y[rows]
            mid_ref[rows, at] = mid
            square[m] = square[m] + jnp.sum(mid * mid, axis=-1, keepdims=True)
    router_copy.wait()
    for m, hm_ref in enumerate((hm0_ref, hm1_ref)):
        rows = slice(m * T, (m + 1) * T)
        r = lax.rsqrt(square[m] * (1.0 / D) + EPS)
        hm_ref[:, :D] = (mid_ref[rows, :] * r * gain_ref[1:2, :]).astype(BF)
        logits = mm(hm_ref[:, :D], wr_s[...])
        chosen = chosen_ref[rows, :] > 0
        top = jnp.max(jnp.where(chosen, logits, -jnp.inf), axis=-1, keepdims=True)
        e = jnp.where(chosen, jnp.exp(jnp.minimum(logits - top, 0.0)), 0.0)
        gate = e / jnp.sum(e, axis=-1, keepdims=True)
        high = gate.astype(BF).astype(F32)
        hm_ref[:, D:] = (high + pltpu.roll(gate - high, N_EXPERTS, 1)).astype(BF)
        if save:
            for a in range(3):
                for i in range(8):
                    cut = slice(i * SLICE, (i + 1) * SLICE)
                    rows_of = hm_ref[:, cut] if a == 2 else (h_ref, att_ref)[a][rows, cut]
                    left_ref[i, rows, a * 256 : a * 256 + SLICE] = rows_of
                    left_ref[i, rows, a * 256 + SLICE : (a + 1) * 256] = jnp.zeros((T, 256 - SLICE), BF)


def attend(spots, q, kvs, allowed, x0, x1, w_o, w, gains, chosen, h_attn, save):
    more = [h_attn] if save else []
    return call(
        lambda *refs: attend_kernel(save, *refs), "attend", [q, kvs[0], allowed, x0, x1, gains, chosen, *more], [*w_o, w, *kvs[1:]],
        [sds((R, D), BF), sds((R, D), F32), sds((T, D + LANES), BF), sds((T, D + LANES), BF)] + [sds((8, R, 768), BF) for _ in more], [],
        [pltpu.VMEM((2, SEQ, 512), BF), pltpu.VMEM((D, D), BF), pltpu.VMEM((D, LANES), BF), pltpu.SemaphoreType.DMA((33,)),
         pltpu.SemaphoreType.DMA((2, 8))],
        7, 14, spots,
    )


FW = D + FF
GW = 2 * D
SLOTS = 3
WEIGHT_SLOTS = [pltpu.VMEM((SLOTS, D, 512), BF), pltpu.VMEM((SLOTS, 256, D), BF), pltpu.SemaphoreType.DMA((SLOTS, 3))]


def fetch_step(step, w_in, w_down, w_s, d_s, sems):
    e, f, slot = step // 3, step % 3, step % SLOTS
    return [
        fetch(w_in[e].at[:, f * 256 : (f + 1) * 256], w_s.at[slot, :, 0:256], sems.at[slot, 0]),
        fetch(w_in[e].at[:, FF + f * 256 : FF + (f + 1) * 256], w_s.at[slot, :, 256:512], sems.at[slot, 1]),
        fetch(w_down[e].at[f * 256 : (f + 1) * 256, :], d_s.at[slot], sems.at[slot, 2]),
    ]


def expert_kernel(save, *refs):
    own_ref, mine_ref, w_in, w_down, hm_refs, outs, rest = refs[0], refs[1], refs[2:4], refs[4:6], refs[6:9], refs[9:13], refs[13:]
    if save:
        g_ref, f_out, (gate_out, up_out, prod_out), rest = rest[0], rest[1:3], rest[3:6], rest[6:]
        (f_s, act_s, gate_s, up_s, prod_s, out_sems), rest = rest[:6], rest[6:]
        h_ref = f_s
    else:
        h_ref, g_ref, rest = rest[0], rest[1], rest[2:]
    lanes_s, hm_sems, acc, total, w_s, d_s, sems = rest
    arrive = []
    for i, b in enumerate(hm_refs, 1):
        at = slice(i * T, (i + 1) * T)
        arrive.append(fetch(b.at[:, :D], h_ref.at[at, :D], hm_sems.at[i, 0]))
        arrive.append(fetch(b.at[:, D:], lanes_s.at[at, :], hm_sems.at[i, 1]))
    copies = [fetch_step(step, w_in, w_down, w_s, d_s, sems) for step in range(SLOTS)]
    h_ref[0:T, :D] = own_ref[:, :D]
    lanes_s[0:T, :] = own_ref[:, D:]
    for copy in arrive:
        copy.wait()
    lanes = lanes_s[...].astype(F32)
    for e in range(2):
        g = jnp.sum(lanes * mine_ref[e : e + 1, :], axis=-1, keepdims=True)
        g_ref[e] = jnp.broadcast_to(g, (C, LANES))
    sent = []
    for step in range(6):
        e, f, slot = step // 3, step % 3, step % SLOTS
        for copy in copies[step]:
            copy.wait()
        both = mm(h_ref[:, :D], w_s[slot])
        gate, up = both[:, :256], both[:, 256:]
        act = (gate / (1.0 + jnp.exp(-gate)) * up).astype(BF)
        add = mm(act, d_s[slot])
        if save:
            cols = slice(f * 256, (f + 1) * 256)
            gate_s[e, :, cols] = gate
            up_s[e, :, cols] = up
            if e == 0:
                f_s[:, D + f * 256 : D + (f + 1) * 256] = act
            else:
                act_s[:, cols] = act
        if step + SLOTS < 6:
            copies.append(fetch_step(step + SLOTS, w_in, w_down, w_s, d_s, sems))
        if f == 0:
            acc[...] = add
        elif f == 1:
            acc[...] += add
        else:
            prod = (acc[...] + add).astype(BF)
            weighted = prod.astype(F32) * g_ref[e, :, 0:1]
            if save:
                prod_s[e] = prod
                sent.append(fetch(gate_s.at[e], gate_out.at[e], out_sems.at[e, 0]))
                sent.append(fetch(up_s.at[e], up_out.at[e], out_sems.at[e, 1]))
                sent.append(fetch(prod_s.at[e], prod_out.at[e], out_sems.at[e, 2]))
                if e == 0:
                    sent.append(fetch(f_s, f_out[0], out_sems.at[0, 3]))
                    sent.append(fetch(f_s.at[:, :D], f_out[1].at[:, :D], out_sems.at[0, 4]))
                else:
                    sent.append(fetch(act_s, f_out[1].at[:, D:], out_sems.at[1, 3]))
            if e == 0:
                total[...] = weighted
            else:
                part = (total[...] + weighted).astype(BF)
                for i, o in enumerate(outs):
                    o[...] = part[i * T : (i + 1) * T]
    for copy in sent:
        copy.wait()


def expert(hms, mine, w_in, w_down, save):
    outs, away = [sds((T, D), BF)] * 4, []
    scratch = [pltpu.VMEM((C, LANES), BF), pltpu.SemaphoreType.DMA((4, 2)), pltpu.VMEM((C, D), F32), pltpu.VMEM((C, D), F32)] + WEIGHT_SLOTS
    if save:
        outs = outs + [sds((2, C, LANES), F32)]
        away = [sds((C, FW), BF), sds((C, FW), BF), sds((2, C, FF), F32), sds((2, C, FF), F32), sds((2, C, D), BF)]
        scratch = [pltpu.VMEM((C, FF), BF) if i == 1 else pltpu.VMEM(o.shape, o.dtype) for i, o in enumerate(away)] + [pltpu.SemaphoreType.DMA((2, 5))] + scratch
    else:
        scratch = [pltpu.VMEM((C, D), BF), pltpu.VMEM((2, C, LANES), F32)] + scratch
    return call(
        lambda *refs: expert_kernel(save, *refs), "expert", [hms[0], mine], [*w_in, *w_down, *hms[1:]], outs, away, scratch,
        10 if save else 7.7, 24 if save else 16,
    )


def expert_back_kernel(save, *refs):
    own_ref, g_ref, put_ref, rest = refs[0], refs[1], refs[2], refs[3:]
    (gate_in, up_in, prod_in), w_in, w_down = rest[:3], rest[3:5], rest[5:7]
    g_in, outs, rest = rest[7:10], rest[10:14], rest[14:]
    if save:
        d_out, d_s, out_sems, rest = rest[:2], rest[2:4], rest[4], rest[5:]
    g_s, g_sems, lanes_s, dprod, gate_s, up_s, prod_s, in_sems, acc, total, w_s, d_w, sems = rest
    arrive = [fetch(b, g_s.at[i * T : (i + 1) * T, :], g_sems.at[i]) for i, b in enumerate(g_in, 1)]
    kept = [
        [fetch(src.at[e], dst.at[e], in_sems.at[e, i]) for i, (src, dst) in enumerate(((prod_in, prod_s), (gate_in, gate_s), (up_in, up_s)))]
        for e in range(2)
    ]
    copies = [fetch_step(step, w_in, w_down, w_s, d_w, sems) for step in range(SLOTS)]
    put = put_ref[...]
    g_s[0:T, :] = own_ref[...]
    for copy in arrive:
        copy.wait()
    sent = []
    for step in range(6):
        e, f, slot = step // 3, step % 3, step % SLOTS
        if f == 0:
            kept[e][0].wait()
            for i in range(4):
                at = slice(i * T, (i + 1) * T)
                g = g_s[at, :].astype(F32)
                d_prod = (g * g_ref[e, at, 0:1]).astype(BF)
                dprod[at, :] = d_prod
                if save:
                    d_s[e][at, D:] = d_prod
                d = jnp.sum(g * prod_s[e, at, :].astype(F32), axis=-1, keepdims=True)
                high = d.astype(BF).astype(F32)
                lanes = high * put[2 * e : 2 * e + 1, :] + (d - high) * put[2 * e + 1 : 2 * e + 2, :]
                lanes_s[at, :] = lanes if e == 0 else lanes_s[at, :] + lanes
            kept[e][1].wait()
            kept[e][2].wait()
        for copy in copies[step]:
            copy.wait()
        cols = slice(f * 256, (f + 1) * 256)
        d_act = mm(dprod[...], d_w[slot], NT)
        gate, up = gate_s[e, :, cols], up_s[e, :, cols]
        s = 1.0 / (1.0 + jnp.exp(-gate))
        dg = (d_act * up * (s * (1.0 + gate * (1.0 - s)))).astype(BF)
        du = (d_act * (gate * s)).astype(BF)
        if save:
            d_s[e][:, cols] = dg
            d_s[e][:, FF + f * 256 : FF + (f + 1) * 256] = du
        add = mm(jnp.concatenate([dg, du], axis=1), w_s[slot], NT)
        if step + SLOTS < 6:
            copies.append(fetch_step(step + SLOTS, w_in, w_down, w_s, d_w, sems))
        if f == 0:
            acc[...] = add
        elif f == 1:
            acc[...] += add
        else:
            rows_grad = (acc[...] + add).astype(BF).astype(F32)
            if save:
                sent.append(fetch(d_s[e], d_out[e], out_sems.at[e]))
            if e == 0:
                total[...] = rows_grad
            else:
                part = (total[...] + rows_grad).astype(BF)
                for i, o in enumerate(outs):
                    at = slice(i * T, (i + 1) * T)
                    o[:, :D] = part[at]
                    o[:, D:] = lanes_s[at, :].astype(BF)
    for copy in sent:
        copy.wait()


def expert_back(gs, kept, put, w_in, w_down, save):
    g_share, gate, up, produced = kept
    away, scratch = [], []
    if save:
        away = [sds((C, GW), BF)] * 2
        scratch = [pltpu.VMEM(o.shape, o.dtype) for o in away] + [pltpu.SemaphoreType.DMA((2,))]
    scratch = scratch + [
        pltpu.VMEM((C, D), BF), pltpu.SemaphoreType.DMA((4,)), pltpu.VMEM((C, LANES), F32), pltpu.VMEM((C, D), BF), pltpu.VMEM((2, C, FF), F32), pltpu.VMEM((2, C, FF), F32),
        pltpu.VMEM((2, C, D), BF), pltpu.SemaphoreType.DMA((2, 3)), pltpu.VMEM((C, D), F32), pltpu.VMEM((C, D), F32),
    ] + WEIGHT_SLOTS
    return call(
        lambda *refs: expert_back_kernel(save, *refs), "expert_back", [gs[0], g_share, put], [gate, up, produced, *w_in, *w_down, *gs[1:]],
        [sds((T, D + LANES), BF)] * 4, away, scratch, 12.5 if save else 11, 24,
    )


def norm_back(x, gain, grad):
    r = lax.rsqrt(jnp.mean(x * x, axis=-1, keepdims=True) + EPS)
    n = x * r
    scaled = grad * gain
    back = r * (scaled - n * jnp.mean(scaled * n, axis=-1, keepdims=True))
    return jnp.sum(grad * n, axis=0, keepdims=True), back


def mid_back_kernel(*refs):
    own_refs, g_refs, mid_ref, hm_refs, gain_ref, w_ref, far = refs[:2], refs[2:4], refs[4], refs[5:7], refs[7], refs[8], refs[9:15]
    dmid_ref, datt_ref, dl_ref, gain_out, wr_s, sem, far_s, sems = refs[15:]
    arrive = [fetch(b, far_s.at[i], sems.at[i]) for i, b in enumerate(far)]
    copy = fetch(w_ref.at[:, 2048:], wr_s, sem)
    grads = jnp.zeros((1, D), F32)
    for m in range(2):
        rows = slice(m * T, (m + 1) * T)
        total = own_refs[m][...].astype(F32)
        for i in range(3 * m, 3 * m + 3):
            arrive[i].wait()
            total = total + far_s[i].astype(F32)
        lanes = total[:, D:]
        d_gate = lanes + pltpu.roll(lanes, LANES - N_EXPERTS, 1)
        share = hm_refs[m][:, D:].astype(F32)
        gate = share + pltpu.roll(share, LANES - N_EXPERTS, 1)
        gate = jnp.where(lax.broadcasted_iota(jnp.int32, (T, LANES), 1) < N_EXPERTS, gate, 0.0)
        inner = jnp.sum(gate * d_gate, axis=-1, keepdims=True)
        d_logits = (gate * (d_gate - inner)).astype(BF)
        dl_ref[rows, :] = d_logits
        if m == 0:
            copy.wait()
        d_hm = total[:, :D] + mm(d_logits, wr_s[...], NT)
        grad_gain, back = norm_back(mid_ref[rows, :], gain_ref[1:2, :], d_hm)
        grads = grads + grad_gain
        d_mid = g_refs[m][...].astype(F32) + back
        dmid_ref[rows, :] = d_mid
        datt_ref[rows, :] = d_mid.astype(BF)
    gain_out[...] = jnp.broadcast_to(grads, (8, D))


def mid_back(rets, gs, mid, hms, gains, w):
    return call(
        mid_back_kernel, "mid_back", [rets[0], rets[4], *gs, mid, *hms, gains], [w, *rets[1:4], *rets[5:8]],
        [sds((R, D), F32), sds((R, D), BF), sds((R, LANES), BF), sds((8, D), F32)], [],
        [pltpu.VMEM((D, LANES), BF), pltpu.SemaphoreType.DMA, pltpu.VMEM((6, T, D + LANES), BF), pltpu.SemaphoreType.DMA((6,))],
        2.8, 8,
    )


def attn_back_kernel(*refs):
    spots_ref, datt_ref, q_ref, own_ref, allowed_ref, cos_ref, sin_ref = refs[:7]
    w_refs, kv_refs, rest = refs[7:15], (None,) + refs[15:22], refs[22:]
    dq_ref, same_ref, other_ref, da, kv_s, kv_acc, w_s, sems, kv_sems = rest
    copies = fetch_w_out(spots_ref, w_refs, w_s, sems)
    key_copies = fetch_keys(kv_refs, kv_s, kv_sems)
    own_keys(own_ref, kv_s)
    for copy in copies:
        copy.wait()
    for j in range(4):
        piece = mm(datt_ref[...], w_s[j * 384 : (j + 1) * 384, :], NT).astype(BF)
        for m in range(2):
            for i in range(3):
                da[m, j * 3 + i] = piece[m * T : (m + 1) * T, i * HS : (i + 1) * HS]
    for copy in key_copies:
        copy.wait()
    allowed = allowed_ref[...]
    cos, sin = cos_ref[:T, :], sin_ref[:T, :]
    for m in range(2):
        rows = slice(m * T, (m + 1) * T)
        for k in range(KV_HEADS):
            keys = kv_s[m, :, k * HS : (k + 1) * HS]
            values = kv_s[m, :, KW + k * HS : KW + (k + 1) * HS]
            q6 = heads_of(q_ref, m, k)
            d6 = da[m, k * GROUP : (k + 1) * GROUP].reshape(GROUP * T, HS)
            p = probs_of(q6, keys, allowed)
            dp = mm(d6, values, NT)
            ds = (p * (dp - jnp.sum(p * dp, axis=-1, keepdims=True)) * SCALE).astype(BF)
            dq = mm(ds, keys)
            for g in range(GROUP):
                h = k * GROUP + g
                dq_ref[rows, h * HS : (h + 1) * HS] = rope_back(dq[g * T : (g + 1) * T], cos, sin).astype(BF)
            kv_acc[:, k * HS : (k + 1) * HS] = mm(ds, q6, TN)
            kv_acc[:, KW + k * HS : KW + (k + 1) * HS] = mm(p.astype(BF), d6, TN)
        for i in range(4):
            at = slice(i * R + m * T, i * R + (m + 1) * T)
            same_ref[at, :] = kv_acc[i * T : (i + 1) * T].astype(BF)
            other_ref[at, :] = kv_acc[C + i * T : C + (i + 1) * T].astype(BF)


def attn_back(spots, d_att, w_o, q, kvs, allowed, cos, sin):
    return call(
        attn_back_kernel, "attn_back", [d_att, q, kvs[0], allowed, cos, sin], [*w_o, *kvs[1:]],
        [sds((R, D), BF), sds((4 * R, 512), BF), sds((4 * R, 512), BF)], [],
        [pltpu.VMEM((2, HEADS, T, HS), BF), pltpu.VMEM((2, SEQ, 512), BF), pltpu.VMEM((SEQ, 512), F32),
         pltpu.VMEM((D, D), BF), pltpu.SemaphoreType.DMA((32,)), pltpu.SemaphoreType.DMA((2, 8))],
        9, 16, spots,
    )


MSG = 512 + LANES


def qkv_back_kernel(*refs):
    own_ref, dq_ref, dl_ref, gm_ref, x0_ref, x1_ref, gain_ref, cos_ref, sin_ref, dmid_ref, w_ref = refs[:11]
    gin_ref, low0_ref, low1_ref, msg_ref, dh, w_s, sems, far_s, far_sems = refs[14:]
    arrive = [fetch(b, far_s.at[i], far_sems.at[i]) for i, b in enumerate(refs[11:14])]
    copies = [fetch(w_ref.at[j * 384 : (j + 1) * 384, 0:2048], w_s.at[j], sems.at[j]) for j in range(4)]
    d_kv = own_ref[...].astype(F32)
    for i in range(3):
        arrive[i].wait()
        d_kv = d_kv + far_s[i].astype(F32)
    cos, sin = cos_ref[...], sin_ref[...]
    for i in range(KV_HEADS):
        at = slice(i * HS, (i + 1) * HS)
        msg_ref[:R, at] = rope_back(d_kv[:, at], cos, sin).astype(BF)
    msg_ref[:R, KW:512] = d_kv[:, KW:].astype(BF)
    msg_ref[:R, 512:] = dl_ref[...]
    for j in range(4):
        copies[j].wait()
        dh[:, j * 384 : (j + 1) * 384] = mm(dq_ref[...], w_s[j, :, :D], NT) + mm(msg_ref[:R, :512], w_s[j, :, D:], NT)
    grads = jnp.zeros((1, D), F32)
    for m, (x_ref, low_ref) in enumerate(((x0_ref, low0_ref), (x1_ref, low1_ref))):
        rows = slice(m * T, (m + 1) * T)
        grad_gain, back = norm_back(x_ref[...].astype(F32), gain_ref[0:1, :], dh[rows])
        grads = grads + grad_gain
        g_in = dmid_ref[rows, :] + back
        gin_ref[rows, :] = g_in
        low_ref[...] = g_in.astype(BF)
    row = lax.broadcasted_iota(jnp.int32, (16, 512), 0)
    both = jnp.zeros((16, 512), F32)
    for c in range(3):
        at = slice(c * 512, (c + 1) * 512)
        both = jnp.where(row == c, jnp.broadcast_to(grads[:, at], (16, 512)), both)
        both = jnp.where(row == 3 + c, jnp.broadcast_to(gm_ref[0:1, at], (16, 512)), both)
    msg_ref[R:, :512] = both.astype(BF)
    msg_ref[R:, 512:] = jnp.zeros((16, LANES), BF)


def qkv_back(rets, dq, dl, gm, x0, x1, gains, w, cos, sin, d_mid):
    return call(
        qkv_back_kernel, "qkv_back", [rets[0], dq, dl, gm, x0, x1, gains, cos, sin, d_mid], [w, *rets[1:]],
        [sds((R, D), F32), sds((T, D), BF), sds((T, D), BF), sds((R + 16, MSG), BF)], [],
        [pltpu.VMEM((R, D), F32), pltpu.VMEM((4, 384, 2048), BF), pltpu.SemaphoreType.DMA((4,)),
         pltpu.VMEM((3, R, 512), BF), pltpu.SemaphoreType.DMA((3,))],
        6.2, 12,
    )


ROWS = SLICE + 16


def attn_grad_kernel(*refs):
    order_ref, left_ref, blocks, send_ref, (lh, rq, ro, rm, rg, sems) = refs[0], refs[1], refs[2:26], refs[26], refs[27:]
    left_copies, q_copies, o_copies, m_copies = [], [], [], []
    for i in range(8):
        at = slice(i * R, (i + 1) * R)
        left_copies.append(fetch(left_ref.at[order_ref[i]], lh.at[at, :], sems.at[0, i]))
        o_copies.append(fetch(blocks[16 + i], ro.at[at, :], sems.at[1, i]))
        q_copies.append(fetch(blocks[8 + i], rq.at[at, :], sems.at[2, i]))
        m_copies.append(fetch(blocks[i].at[:R, :], rm.at[at, :], sems.at[3, i]))
        m_copies.append(fetch(blocks[i].at[R:, :], rg.at[i], sems.at[4, i]))
    for copy in left_copies + o_copies:
        copy.wait()

    def spread(grads, width, lane):
        for r in range(8):
            send_ref[r, :SLICE, lane : lane + width] = grads[:SLICE, r * width : (r + 1) * width].astype(BF)

    spread(mm(lh[:, 256:512], ro[...], TN), SLICE, 320)
    for copy in q_copies:
        copy.wait()
    spread(mm(lh[:, :256], rq[...], TN), SLICE, 0)
    for copy in m_copies:
        copy.wait()
    spread(mm(lh[:, :256], rm[:, :512], TN), 64, SLICE)
    small = mm(lh[:, 512:], rm[:, 512:], TN)[:SLICE, :64].astype(BF)
    gains = sum(rg[i, :, :512].astype(F32) for i in range(8)).astype(BF)
    for r in range(8):
        send_ref[r, :SLICE, 256:320] = small
        send_ref[r, SLICE:, :] = gains


def attn_grad(order, left, msgs, dqs, datts):
    return pl.pallas_call(
        attn_grad_kernel,
        name="attn_grad",
        in_specs=[SCALARS] + [AWAY] * 25,
        out_specs=HERE,
        out_shape=sds((8, ROWS, 512), BF),
        scratch_shapes=[
            pltpu.VMEM((8 * R, 768), BF), pltpu.VMEM((8 * R, D), BF), pltpu.VMEM((8 * R, D), BF), pltpu.VMEM((8 * R, MSG), BF),
            pltpu.VMEM((8, 16, MSG), BF), pltpu.SemaphoreType.DMA((5, 8)),
        ],
        compiler_params=pltpu.CompilerParams(vmem_limit_bytes=20 * 2**20),
        cost_estimate=work(8.5),
    )(order, *in_hbm((left, *msgs, *dqs, *datts)))


def turn_kernel(*refs):
    lefts, (h_out, a_out, f_s, h_s, a_s, sems) = refs[:4], refs[4:]
    copies = [fetch(left, f_s.at[i], sems.at[i]) for i, left in enumerate(lefts)]
    for i in range(4):
        copies[i].wait()
        h_s[:, i * C : (i + 1) * C] = f_s[i, :, :D].T
        a_s[:, i * C : (i + 1) * C] = f_s[i, :, D:].T
    sent = [fetch(h_s, h_out, sems.at[4]), fetch(a_s, a_out, sems.at[5])]
    for copy in sent:
        copy.wait()


def turn(lefts):
    return call(
        turn_kernel, "turn", [], lefts, [], [sds((D, 4 * C), BF), sds((FF, 4 * C), BF)],
        [pltpu.VMEM((4, C, FW), BF), pltpu.VMEM((D, 4 * C), BF), pltpu.VMEM((FF, 4 * C), BF), pltpu.SemaphoreType.DMA((6,))],
        5, 14,
    )


def expert_grad_kernel(in_ref, down_ref, *refs):
    rights, out_ref, right = refs[:4], refs[4], refs[5]
    j = pl.program_id(0)
    for i in range(4):
        right[i * C : (i + 1) * C, :] = rights[i][...]

    def grads(left_ref, rows, first):
        for r in range(8):
            out_ref[r, first : first + rows, :] = mm(left_ref[r * rows : (r + 1) * rows, :], right[...]).astype(BF)

    @pl.when(j % 2 == 0)
    def _():
        grads(in_ref, SLICE, 0)

    @pl.when(j % 2 == 1)
    def _():
        grads(down_ref, SLICE // 2, SLICE)


def expert_grad(left_in, left_down, rights):
    return pl.pallas_call(
        expert_grad_kernel,
        name="expert_grad",
        grid=(12,),
        in_specs=[whole((D, 4 * C)), whole((FF, 4 * C))] + [pl.BlockSpec((C, 256), lambda j: (0, (j % 2) * 6 + j // 2))] * 4,
        out_specs=pl.BlockSpec((8, SLICE + SLICE // 2, 256), lambda j: (0, 0, j // 2)),
        out_shape=pltpu.HBM((8, SLICE + SLICE // 2, D), BF),
        scratch_shapes=[pltpu.VMEM((4 * C, 256), BF)],
        compiler_params=pltpu.CompilerParams(dimension_semantics=("arbitrary",), vmem_limit_bytes=VMEM),
        cost_estimate=work(20),
    )(*in_hbm((left_in, left_down, *rights)))


def body(tokens_in, cotangent, routes, gain_attn, w_query, w_keyval, w_out, gain_moe, w_router, w_in, w_down):
    is_first = lax.axis_index("section") == 0
    shard = lax.axis_index("shard")
    rep = lax.axis_index("rep")
    chip, core = shard // 2, shard % 2
    micros = range(2)

    extra = jnp.concatenate([w_router[0], gain_attn[0][:, None], gain_moe[0][:, None]], axis=1)
    extra = jnp.pad(extra, ((0, 0), (0, LANES - extra.shape[1])))
    packed = jnp.concatenate([w_query[0], w_keyval[0], extra], axis=1)
    w = lax.all_gather(packed, "shard", axis=0, tiled=True)
    pick = (jnp.arange(LANES)[None, :] == (jnp.arange(8)[:, None] + N_EXPERTS)) & (jnp.arange(8)[:, None] < 2)
    gains = mm(pick.astype(BF), w[:, 2048:], NT)
    z = rep // 2

    quarter = lax.dynamic_slice_in_dim(w_out[0], z * (SLICE // 4), SLICE // 4, 0)
    quarters = jnp.stack(from_chips(quarter))
    along_z = [quarters] + [lax.ppermute(quarters, "rep", [(i, ((i // 2 + k) % 4) * 2 + i % 2) for i in range(8)]) for k in (1, 2, 3)]
    w_o = along_z + [swap(piece) for piece in along_z]
    spots = [((chip - ky) % 4) * 2 * SLICE + c * SLICE + ((z - kz) % 4) * (SLICE // 4) for c in (core, 1 - core) for kz in range(4) for ky in range(4)]
    spots = jnp.stack(spots).astype(jnp.int32)

    inner = (w_in[0, 0], swap(w_in[0, 0]))
    outer = (w_down[0, 0], swap(w_down[0, 0]))
    w, gains, inner, outer = lax.optimization_barrier((w, gains, inner, outer))

    half = HS // 2
    frequency = ROPE_BASE ** (-jnp.arange(half, dtype=F32) * 2.0 / HS)
    place = shard * T + jnp.arange(T, dtype=jnp.int32)
    angles = place.astype(F32)[:, None] * frequency[None, :]
    angles = jnp.concatenate([angles, angles], axis=0)
    cos = jnp.concatenate([jnp.cos(angles)] * 2, axis=1)
    sin = jnp.concatenate([-jnp.sin(angles), jnp.sin(angles)], axis=1)
    order = jnp.stack([((chip - k) % 4) * 2 + c for c in (core, 1 - core) for k in range(4)]).astype(jnp.int32)
    key_place = (order[:, None] * T + jnp.arange(T, dtype=jnp.int32)[None, :]).reshape(1, SEQ)
    allowed = (key_place <= place[:, None]).astype(F32)
    lane = jnp.arange(LANES, dtype=jnp.int32)
    other = shard ^ 1
    mine = jnp.stack([(lane == e) | (lane == e + N_EXPERTS) for e in (shard, other)]).astype(F32)
    mine = jnp.pad(mine, ((0, 6), (0, 0)))
    put = jnp.stack([lane == shard, lane == shard + N_EXPERTS, lane == other, lane == other + N_EXPERTS]).astype(F32)
    put = jnp.pad(put, ((0, 4), (0, 0)))
    chosen = jnp.any(routes[0, :, 0].reshape(R, -1)[:, :, None] == lane[None, None, :], axis=1).astype(F32)

    hold = lax.optimization_barrier

    def layer(x, save):
        q, kv, h_attn = qkv(x[0], x[1], gains, w, cos, sin)
        kvs = gather_blocks(kv)
        att, mid, hm0, hm1, *left = attend(spots, q, kvs, allowed, x[0], x[1], w_o, w, gains, chosen, h_attn, save)
        hms = (hm0, hm1)
        first = from_chips(hm0)
        first, hm1 = hold((first, hm1))
        second = from_chips(hm1)
        out = expert(first, mine, inner, outer, save)
        second[0], _ = hold((second[0], out[0]))
        outs = [out, expert(second, mine, inner, outer, save)]
        return [out[:4] for out in outs], (x, q, kvs, mid, hms), [out[4:] for out in outs], left

    def finish(parts, mid):
        rets = [to_chips(part) for part in parts]
        return [(mid[m * T : (m + 1) * T] + sum(r.astype(F32) for r in rets[m])).astype(BF) for m in micros]

    def experts_back(blocks, more, save):
        rets, saved = [], []
        for m in micros:
            g_share, gate, up, produced = more[m][0], *more[m][3:]
            if m == 1:
                blocks[1][0], _ = hold((blocks[1][0], out[0]))
            out = expert_back(blocks[m], (g_share, gate, up, produced), put, inner, outer, save)
            rets += to_chips(out[:4])
            saved.append(out[4:])
        return rets, saved

    def keys_back(same, other):
        got = swap(other)
        return to_chips([plus(same[k * R : (k + 1) * R], got[k * R : (k + 1) * R]) for k in range(4)])

    tokens = [tokens_in[m, 0] for m in micros]
    given = [cotangent[m, 0] for m in micros]
    first, kept, *_ = layer(tokens, False)
    first = finish(first, kept[3])
    arrived = [lax.ppermute(first[m], "section", [(0, 1)]) for m in micros]
    arrived, given_first = hold((arrived, from_chips(given[0])))
    inputs = [jnp.where(is_first, tokens[m], arrived[m]) for m in micros]
    parts, kept, more, left = layer(inputs, True)
    (left,) = left
    f_own = [more[m][1] for m in micros]
    f_got = [swap(more[m][2]) for m in micros]

    x, q, kvs, mid, hms = kept
    left, _ = hold((left, parts[1]))
    left = lax.all_to_all(left, "shard", split_axis=0, concat_axis=0, tiled=True)
    rets, _ = experts_back([given_first, from_chips(given[1])], more, False)
    rets, f_got, left = hold((rets, f_got, left))
    d_mid, d_att, dl, gm = mid_back(rets, given, mid, hms, gains, w)
    dq, kv_same, kv_other = attn_back(spots, d_att, w_o, q, kvs, allowed, cos, sin)
    kv_rets, (h_turned, act_turned) = hold((keys_back(kv_same, kv_other), turn(f_own + f_got)))
    _, low0, low1, _ = qkv_back(kv_rets, dq, dl, gm, x[0], x[1], gains, w, cos, sin, d_mid)
    arrived = [lax.ppermute(low, "section", [(1, 0)]) for low in (low0, low1)]
    parts, _ = hold((parts, low0))
    acts = finish(parts, mid)
    arrived, acts = hold((arrived, acts))
    given = [jnp.where(is_first, arrived[m], given[m]) for m in micros]

    first = from_chips(given[0])
    first, second = hold((first, given[1]))
    rets, saved = experts_back([first, from_chips(second)], more, True)
    rights = [saved[m][0] for m in micros] + [swap(saved[m][1]) for m in micros]
    rets, send = hold((rets, expert_grad(h_turned, act_turned, rights)))
    expert_parts = lax.all_to_all(send, "rep", split_axis=0, concat_axis=0, tiled=True)
    d_mid, d_att, dl, gm = mid_back(rets, given, mid, hms, gains, w)
    datts = from_chips(d_att)
    dq, kv_same, kv_other = attn_back(spots, d_att, w_o, q, kvs, allowed, cos, sin)
    datts, kv_same, kv_other = hold((datts, kv_same, kv_other))
    kv_rets = keys_back(kv_same, kv_other)
    kv_rets, dq_sent = hold((kv_rets, dq))
    dqs = from_chips(dq_sent)
    g_in, _, _, msg = qkv_back(kv_rets, dq, dl, gm, x[0], x[1], gains, w, cos, sin, d_mid)

    msgs = from_chips(msg)
    dqs, msgs = hold((dqs, msgs))
    dqs, datts, msgs = (blocks + [swap(b) for b in blocks] for blocks in (dqs, datts, msgs))
    send = attn_grad(order, left, msgs, dqs, datts)
    expert_parts, send = hold((expert_parts, send))
    got = lax.all_to_all(send, "rep", split_axis=0, concat_axis=0, tiled=True)
    sums = jnp.sum(got.astype(F32), axis=0)
    g_q, g_kv, g_r, g_o = (sums[:SLICE, a:b] for a, b in ((0, 192), (192, 256), (256, 256 + N_EXPERTS), (320, 512)))
    g_gains = lax.dynamic_slice(sums[SLICE : SLICE + 6].reshape(2, D), (0, shard * SLICE), (2, SLICE))
    expert_sums = jnp.sum(expert_parts.astype(F32), axis=0)

    return (
        jnp.stack(acts)[None, :, None],
        g_in.reshape(1, 2, 1, T, D),
        g_gains[0:1],
        g_q[None],
        g_kv[None],
        g_o[None],
        g_gains[1:2],
        g_r[None],
        expert_sums[None, None, :SLICE],
        expert_sums[None, None, SLICE:],
    )


def solution(mesh):
    in_specs = (
        P(None, "rep", "shard", None),
        P(None, "rep", "shard", None),
        P("section", None, "rep", "shard", None),
        P("section", "shard"),
        P("section", "shard", None),
        P("section", "shard", None),
        P("section", "shard", None),
        P("section", "shard"),
        P("section", "shard", None),
        P("section", "shard", None, None),
        P("section", "shard", None, None),
    )
    out_specs = (
        P("section", None, "rep", "shard", None),
        P("section", None, "rep", "shard", None),
        P("section", "shard"),
        P("section", "shard", "rep"),
        P("section", "shard", "rep"),
        P("section", "shard", "rep"),
        P("section", "shard"),
        P("section", "shard", None),
        P("section", "shard", "rep", None),
        P("section", "shard", "rep", None),
    )
    return jax.shard_map(body, mesh=mesh, in_specs=in_specs, out_specs=out_specs, check_vma=False)
```

```python
import jax
import jax.numpy as jnp
from jax import lax
from jax.experimental import pallas as pl
from jax.experimental.pallas import tpu as pltpu
from jax.sharding import PartitionSpec as P

D = 1536
T = 64
R = 2 * T
C = 4 * T
B = 4 * R
HEADS = 12
KV_HEADS = 2
GROUP = HEADS // KV_HEADS
HS = 128
KW = KV_HEADS * HS
SLICE = D // 8
FF = 768
SEQ = 512
N_EXPERTS = 8
LANES = 128
EPS = 1e-06
ROPE_BASE = 1000000.0
SCALE = HS**-0.5
BF = jnp.bfloat16
VMEM = 18 * 2**20
F32 = jnp.float32

NN = (((1,), (0,)), ((), ()))
NT = (((1,), (1,)), ((), ()))
TN = (((0,), (0,)), ((), ()))


def mm(a, b, dims=NN):
    return lax.dot_general(a, b, dims, preferred_element_type=F32)


def sds(shape, dtype):
    return jax.ShapeDtypeStruct(shape, dtype)


def whole(shape):
    return pl.BlockSpec(shape, lambda *_: (0,) * len(shape))


def in_hbm(args):
    return [pltpu.with_memory_space_constraint(a, pltpu.HBM) for a in args]


HERE = pl.BlockSpec(memory_space=pltpu.VMEM)
AWAY = pl.BlockSpec(memory_space=pltpu.HBM)
SCALARS = pl.BlockSpec(memory_space=pltpu.SMEM)


def work(us):
    return pl.CostEstimate(flops=1, bytes_accessed=int(us * 3.7 * 10**6), transcendentals=0)


def call(kernel, name, here, away, outs, outs_away, scratch, us, vmem, scalars=None):
    scalars = [] if scalars is None else [scalars]
    return pl.pallas_call(
        kernel,
        name=name,
        in_specs=[SCALARS] * len(scalars) + [HERE] * len(here) + [AWAY] * len(away),
        out_specs=[HERE] * len(outs) + [AWAY] * len(outs_away),
        out_shape=outs + [pltpu.HBM(o.shape, o.dtype) for o in outs_away],
        scratch_shapes=scratch,
        compiler_params=pltpu.CompilerParams(vmem_limit_bytes=vmem * 2**20),
        cost_estimate=work(us),
    )(*scalars, *here, *in_hbm(away))


def fetch(src, dst, sem):
    copy = pltpu.make_async_copy(src, dst, sem)
    copy.start()
    return copy


def swap(x):
    return lax.ppermute(x, "shard", [(i, i ^ 1) for i in range(8)])


def along_y(x, k):
    return lax.ppermute(x, "shard", [(i, (i + 2 * k) % 8) for i in range(8)])


def from_chips(x):
    return [x, along_y(x, 1), along_y(x, 2), along_y(x, 3)]


def halves_from_chips(lo, hi):
    near_lo, over_hi = along_y(lo, 1), along_y(hi, 3)
    far_lo, far_hi = along_y(near_lo, 1), along_y(over_hi, 3)
    return [lo, hi, near_lo, along_y(hi, 1), far_lo, far_hi, along_y(lo, 3), over_hi]


def to_chips(blocks):
    return [blocks[0]] + [along_y(blocks[k], -k) for k in (1, 2, 3)]


def gather_blocks(x):
    same = from_chips(x)
    return same + [swap(b) for b in same]


def plus(a, b):
    return (a.astype(F32) + b.astype(F32)).astype(BF)


def rope(x, cos, sin):
    return x * cos + pltpu.roll(x, HS // 2, 1) * sin


def rope_back(x, cos, sin):
    return x * cos - pltpu.roll(x, HS // 2, 1) * sin


def qkv_kernel(x0_ref, x1_ref, gain_ref, cos_ref, sin_ref, w_ref, q_ref, kv_ref, h_ref, w_s, sems):
    copies = [fetch(w_ref.at[:, j * 512 : (j + 1) * 512], w_s.at[j], sems.at[j]) for j in range(4)]
    for m, x_ref in enumerate((x0_ref, x1_ref)):
        x = x_ref[...].astype(F32)
        r = lax.rsqrt(jnp.mean(x * x, axis=-1, keepdims=True) + EPS)
        h_ref[m * T : (m + 1) * T, :] = (x * r * gain_ref[0:1, :]).astype(BF)
    cos, sin = cos_ref[...], sin_ref[...]
    for j in range(4):
        copies[j].wait()
        y = mm(h_ref[...], w_s[j])
        for i in range(4 if j < 3 else 2):
            at = slice(i * HS, (i + 1) * HS)
            turned = rope(y[:, at], cos, sin).astype(BF)
            if j < 3:
                q_ref[:, j * 512 + i * HS : j * 512 + (i + 1) * HS] = turned
            else:
                kv_ref[:, at] = turned
        if j == 3:
            kv_ref[:, KW:] = y[:, KW:].astype(BF)


def qkv(x0, x1, gains, w, cos, sin):
    return call(
        qkv_kernel, "qkv", [x0, x1, gains, cos, sin], [w],
        [sds((R, D), BF), sds((R, 512), BF), sds((R, D), BF)], [],
        [pltpu.VMEM((4, D, 512), BF), pltpu.SemaphoreType.DMA((4,))],
        3.5, 8,
    )


def fetch_keys(kv_refs, kv_s, sems):
    return [
        fetch(kv_refs[i].at[m * T : (m + 1) * T, :], kv_s.at[m, i * T : (i + 1) * T, :], sems.at[m, i]) for i in range(1, 8) for m in range(2)
    ]


def own_keys(own, kv_s):
    for m in range(2):
        kv_s[m, 0:T, :] = own[m * T : (m + 1) * T, :]


def heads_of(ref, m, k):
    rows = slice(m * T, (m + 1) * T)
    return jnp.concatenate([ref[rows, h * HS : (h + 1) * HS] for h in range(k * GROUP, (k + 1) * GROUP)], axis=0)


def probs_of(q6, keys, allowed):
    s = mm(q6, keys, NT) * SCALE
    s = jnp.where(allowed[None] > 0, s.reshape(GROUP, T, SEQ), -1e30)
    e = jnp.exp(s - jnp.max(s, axis=-1, keepdims=True))
    p = e * (1.0 / jnp.sum(e, axis=-1, keepdims=True))
    return p.reshape(GROUP * T, SEQ)


def fetch_w_out(spots_ref, pieces, w_s, sems):
    copies = []
    for p, piece in enumerate(pieces):
        for k in range(4):
            i = p * 4 + k
            at = pl.ds(pl.multiple_of(spots_ref[i], 16), SLICE // 4)
            copies.append(fetch(piece.at[k], w_s.at[at, :], sems.at[i]))
    return copies


def attend_kernel(save, *refs):
    spots_ref, q_ref, own_ref, allowed_ref, x0_ref, x1_ref, gain_ref, chosen_ref, rest = *refs[:8], refs[8:]
    if save:
        h_ref, rest = rest[0], rest[1:]
    w_refs, wp_ref, kv_refs, rest = rest[:8], rest[8], (None,) + rest[9:16], rest[16:]
    if save:
        att_ref, mid_ref, hm0_ref, hm1_ref, left_ref, kv_s, w_s, wr_s, sems, kv_sems = rest
    else:
        att_ref, mid_ref, hm0_ref, hm1_ref, kv_s, w_s, wr_s, sems, kv_sems = rest
    key_copies = fetch_keys(kv_refs, kv_s, kv_sems)
    router_copy = fetch(wp_ref.at[:, 2048:], wr_s, sems.at[32])
    copies = fetch_w_out(spots_ref, w_refs, w_s, sems)
    own_keys(own_ref, kv_s)
    allowed = allowed_ref[...]
    for copy in key_copies:
        copy.wait()
    for m in range(2):
        for k in range(KV_HEADS):
            p = probs_of(heads_of(q_ref, m, k), kv_s[m, :, k * HS : (k + 1) * HS], allowed).astype(BF)
            o = mm(p, kv_s[m, :, KW + k * HS : KW + (k + 1) * HS])
            for g in range(GROUP):
                h = k * GROUP + g
                att_ref[m * T : (m + 1) * T, h * HS : (h + 1) * HS] = o[g * T : (g + 1) * T].astype(BF)
    square = [0.0, 0.0]
    for copy in copies:
        copy.wait()
    for j in range(3):
        at = slice(j * 512, (j + 1) * 512)
        y = mm(att_ref[...], w_s[:, at])
        for m, x_ref in enumerate((x0_ref, x1_ref)):
            rows = slice(m * T, (m + 1) * T)
            mid = x_ref[:, at].astype(F32) + y[rows]
            mid_ref[rows, at] = mid
            square[m] = square[m] + jnp.sum(mid * mid, axis=-1, keepdims=True)
    router_copy.wait()
    for m, hm_ref in enumerate((hm0_ref, hm1_ref)):
        rows = slice(m * T, (m + 1) * T)
        r = lax.rsqrt(square[m] * (1.0 / D) + EPS)
        hm_ref[:, :D] = (mid_ref[rows, :] * r * gain_ref[1:2, :]).astype(BF)
        logits = mm(hm_ref[:, :D], wr_s[...])
        chosen = chosen_ref[rows, :] > 0
        top = jnp.max(jnp.where(chosen, logits, -jnp.inf), axis=-1, keepdims=True)
        e = jnp.where(chosen, jnp.exp(jnp.minimum(logits - top, 0.0)), 0.0)
        gate = e / jnp.sum(e, axis=-1, keepdims=True)
        high = gate.astype(BF).astype(F32)
        hm_ref[:, D:] = (high + pltpu.roll(gate - high, N_EXPERTS, 1)).astype(BF)
        if save:
            for a in range(3):
                for i in range(8):
                    cut = slice(i * SLICE, (i + 1) * SLICE)
                    rows_of = hm_ref[:, cut] if a == 2 else (h_ref, att_ref)[a][rows, cut]
                    left_ref[i, rows, a * 256 : a * 256 + SLICE] = rows_of
                    left_ref[i, rows, a * 256 + SLICE : (a + 1) * 256] = jnp.zeros((T, 256 - SLICE), BF)


def attend(spots, q, kvs, allowed, x0, x1, w_o, w, gains, chosen, h_attn, save):
    more = [h_attn] if save else []
    return call(
        lambda *refs: attend_kernel(save, *refs), "attend", [q, kvs[0], allowed, x0, x1, gains, chosen, *more], [*w_o, w, *kvs[1:]],
        [sds((R, D), BF), sds((R, D), F32)] + [sds((T, D + LANES), BF)] * 2 + [sds((8, R, 768), BF) for _ in more], [],
        [pltpu.VMEM((2, SEQ, 512), BF), pltpu.VMEM((D, D), BF), pltpu.VMEM((D, LANES), BF), pltpu.SemaphoreType.DMA((33,)),
         pltpu.SemaphoreType.DMA((2, 8))],
        7, 11, spots,
    )


FW = D + FF
GW = 2 * D
SLOTS = 3
WEIGHT_SLOTS = [pltpu.VMEM((SLOTS, D, 512), BF), pltpu.VMEM((SLOTS, 256, D), BF), pltpu.SemaphoreType.DMA((SLOTS, 3))]


def fetch_step(step, w_in, w_down, w_s, d_s, sems):
    e, f, slot = step // 3, step % 3, step % SLOTS
    return [
        fetch(w_in[e].at[:, f * 256 : (f + 1) * 256], w_s.at[slot, :, 0:256], sems.at[slot, 0]),
        fetch(w_in[e].at[:, FF + f * 256 : FF + (f + 1) * 256], w_s.at[slot, :, 256:512], sems.at[slot, 1]),
        fetch(w_down[e].at[f * 256 : (f + 1) * 256, :], d_s.at[slot], sems.at[slot, 2]),
    ]


def expert_kernel(own, save, *refs):
    own_refs, refs = refs[:own], refs[own:]
    mine_ref, w_in, w_down, hm_refs, refs = refs[0], refs[1:3], refs[3:5], refs[5 : 5 + 3 * own], refs[5 + 3 * own :]
    outs, rest = refs[:4], refs[4:]
    if save:
        g_ref, f_out, (gate_out, up_out, prod_out), rest = rest[0], rest[1:3], rest[3:6], rest[6:]
        (f_s, act_s, gate_s, up_s, prod_s, out_sems), rest = rest[:6], rest[6:]
        h_ref = f_s
    else:
        h_ref, g_ref, rest = rest[0], rest[1], rest[2:]
    lanes_s, hm_sems, acc, total, w_s, d_s, sems = rest
    n = own_refs[0].shape[0]
    arrive = []
    for i, b in enumerate(hm_refs, own):
        at = slice(i * n, (i + 1) * n)
        arrive.append(fetch(b.at[:, :D], h_ref.at[at, :D], hm_sems.at[i, 0]))
        arrive.append(fetch(b.at[:, D:], lanes_s.at[at, :], hm_sems.at[i, 1]))
    copies = [fetch_step(step, w_in, w_down, w_s, d_s, sems) for step in range(SLOTS)]
    for i, b in enumerate(own_refs):
        h_ref[i * n : (i + 1) * n, :D] = b[:, :D]
        lanes_s[i * n : (i + 1) * n, :] = b[:, D:]
    for copy in arrive:
        copy.wait()
    lanes = lanes_s[...].astype(F32)
    for e in range(2):
        g = jnp.sum(lanes * mine_ref[e : e + 1, :], axis=-1, keepdims=True)
        g_ref[e] = jnp.broadcast_to(g, (4 * own * n, LANES))
    sent = []
    for step in range(6):
        e, f, slot = step // 3, step % 3, step % SLOTS
        for copy in copies[step]:
            copy.wait()
        both = mm(h_ref[:, :D], w_s[slot])
        gate, up = both[:, :256], both[:, 256:]
        act = (gate / (1.0 + jnp.exp(-gate)) * up).astype(BF)
        add = mm(act, d_s[slot])
        if save:
            cols = slice(f * 256, (f + 1) * 256)
            gate_s[e, :, cols] = gate.astype(BF)
            up_s[e, :, cols] = up.astype(BF)
            if e == 0:
                f_s[:, D + f * 256 : D + (f + 1) * 256] = act
            else:
                act_s[:, cols] = act
        if step + SLOTS < 6:
            copies.append(fetch_step(step + SLOTS, w_in, w_down, w_s, d_s, sems))
        if f == 0:
            acc[...] = add
        elif f == 1:
            acc[...] += add
        else:
            prod = (acc[...] + add).astype(BF)
            weighted = prod.astype(F32) * g_ref[e, :, 0:1]
            if save:
                prod_s[e] = prod
                sent.append(fetch(gate_s.at[e], gate_out.at[e], out_sems.at[e, 0]))
                sent.append(fetch(up_s.at[e], up_out.at[e], out_sems.at[e, 1]))
                sent.append(fetch(prod_s.at[e], prod_out.at[e], out_sems.at[e, 2]))
                if e == 0:
                    sent.append(fetch(f_s, f_out[0], out_sems.at[0, 3]))
                    sent.append(fetch(f_s.at[:, :D], f_out[1].at[:, :D], out_sems.at[0, 4]))
                else:
                    sent.append(fetch(act_s, f_out[1].at[:, D:], out_sems.at[1, 3]))
            if e == 0:
                total[...] = weighted
            else:
                part = (total[...] + weighted).astype(BF)
                for i, o in enumerate(outs):
                    o[...] = part[i * own * n : (i + 1) * own * n]
    for copy in sent:
        copy.wait()


def expert(hms, mine, w_in, w_down, save):
    own, n = len(hms) // 4, hms[0].shape[0]
    rows = len(hms) * n
    outs, away = [sds((own * n, D), BF)] * 4, []
    scratch = [pltpu.VMEM((rows, LANES), BF), pltpu.SemaphoreType.DMA((8, 2)), pltpu.VMEM((rows, D), F32), pltpu.VMEM((rows, D), F32)] + WEIGHT_SLOTS
    if save:
        outs = outs + [sds((2, rows, LANES), F32)]
        away = [sds((rows, FW), BF), sds((rows, FW), BF), sds((2, rows, FF), BF), sds((2, rows, FF), BF), sds((2, rows, D), BF)]
        scratch = [pltpu.VMEM((rows, FF), BF) if i == 1 else pltpu.VMEM(o.shape, o.dtype) for i, o in enumerate(away)] + [pltpu.SemaphoreType.DMA((2, 5))] + scratch
    else:
        scratch = [pltpu.VMEM((rows, D), BF), pltpu.VMEM((2, rows, LANES), F32)] + scratch
    return call(
        lambda *refs: expert_kernel(own, save, *refs), "expert", [*hms[:own], mine], [*w_in, *w_down, *hms[own:]], outs, away, scratch,
        14 if save else 7.7, 34 if save else 12,
    )


def expert_back_kernel(own, save, *refs):
    own_refs, refs = refs[:own], refs[own:]
    g_ref, put_ref, rest = refs[0], refs[1], refs[2:]
    (gate_in, up_in, prod_in), w_in, w_down = rest[:3], rest[3:5], rest[5:7]
    g_in, rest = rest[7 : 7 + 3 * own], rest[7 + 3 * own :]
    outs, rest = rest[:4], rest[4:]
    if save:
        d_out, d_s, out_sems, rest = rest[:2], rest[2:4], rest[4], rest[5:]
    g_s, g_sems, lanes_s, dprod, gate_s, up_s, prod_s, in_sems, acc, total, w_s, d_w, sems = rest
    n = own_refs[0].shape[0]
    arrive = [fetch(b, g_s.at[i * n : (i + 1) * n, :], g_sems.at[i]) for i, b in enumerate(g_in, own)]
    kept = [
        [fetch(src.at[e], dst.at[e], in_sems.at[e, i]) for i, (src, dst) in enumerate(((prod_in, prod_s), (gate_in, gate_s), (up_in, up_s)))]
        for e in range(2)
    ]
    copies = [fetch_step(step, w_in, w_down, w_s, d_w, sems) for step in range(SLOTS)]
    put = put_ref[...]
    for i, b in enumerate(own_refs):
        g_s[i * n : (i + 1) * n, :] = b[...]
    for copy in arrive:
        copy.wait()
    sent = []
    for step in range(6):
        e, f, slot = step // 3, step % 3, step % SLOTS
        if f == 0:
            kept[e][0].wait()
            for i in range(8):
                at = slice(i * T, (i + 1) * T)
                g = g_s[at, :].astype(F32)
                d_prod = (g * g_ref[e, at, 0:1]).astype(BF)
                dprod[at, :] = d_prod
                if save:
                    d_s[e][at, D:] = d_prod
                d = jnp.sum(g * prod_s[e, at, :].astype(F32), axis=-1, keepdims=True)
                high = d.astype(BF).astype(F32)
                lanes = high * put[2 * e : 2 * e + 1, :] + (d - high) * put[2 * e + 1 : 2 * e + 2, :]
                lanes_s[at, :] = lanes if e == 0 else lanes_s[at, :] + lanes
            kept[e][1].wait()
            kept[e][2].wait()
        for copy in copies[step]:
            copy.wait()
        cols = slice(f * 256, (f + 1) * 256)
        d_act = mm(dprod[...], d_w[slot], NT)
        gate, up = gate_s[e, :, cols].astype(F32), up_s[e, :, cols].astype(F32)
        s = 1.0 / (1.0 + jnp.exp(-gate))
        dg = (d_act * up * (s * (1.0 + gate * (1.0 - s)))).astype(BF)
        du = (d_act * (gate * s)).astype(BF)
        if save:
            d_s[e][:, cols] = dg
            d_s[e][:, FF + f * 256 : FF + (f + 1) * 256] = du
        add = mm(jnp.concatenate([dg, du], axis=1), w_s[slot], NT)
        if step + SLOTS < 6:
            copies.append(fetch_step(step + SLOTS, w_in, w_down, w_s, d_w, sems))
        if f == 0:
            acc[...] = add
        elif f == 1:
            acc[...] += add
        else:
            rows_grad = (acc[...] + add).astype(BF).astype(F32)
            if save:
                sent.append(fetch(d_s[e], d_out[e], out_sems.at[e]))
            if e == 0:
                total[...] = rows_grad.astype(BF)
            else:
                part = (total[...].astype(F32) + rows_grad).astype(BF)
                for i, o in enumerate(outs):
                    at = slice(i * R, (i + 1) * R)
                    o[:, :D] = part[at]
                    o[:, D:] = lanes_s[at, :].astype(BF)
    for copy in sent:
        copy.wait()


def expert_back(gs, kept, put, w_in, w_down, save):
    g_share, gate, up, produced = kept
    own, rows = len(gs) // 4, B
    away, scratch = [], []
    if save:
        away = [sds((rows, GW), BF)] * 2
        scratch = [pltpu.VMEM(o.shape, o.dtype) for o in away] + [pltpu.SemaphoreType.DMA((2,))]
    scratch = scratch + [
        pltpu.VMEM((rows, D), BF), pltpu.SemaphoreType.DMA((8,)), pltpu.VMEM((rows, LANES), F32), pltpu.VMEM((rows, D), BF), pltpu.VMEM((2, rows, FF), BF), pltpu.VMEM((2, rows, FF), BF),
        pltpu.VMEM((2, rows, D), BF), pltpu.SemaphoreType.DMA((2, 3)), pltpu.VMEM((rows, D), F32), pltpu.VMEM((rows, D), BF),
    ] + WEIGHT_SLOTS
    return call(
        lambda *refs: expert_back_kernel(own, save, *refs), "expert_back", [*gs[:own], g_share, put], [gate, up, produced, *w_in, *w_down, *gs[own:]],
        [sds((R, D + LANES), BF)] * 4, away, scratch, 17 if save else 15, 36 if save else 30,
    )


def norm_back(x, gain, grad):
    r = lax.rsqrt(jnp.mean(x * x, axis=-1, keepdims=True) + EPS)
    n = x * r
    scaled = grad * gain
    back = r * (scaled - n * jnp.mean(scaled * n, axis=-1, keepdims=True))
    return jnp.sum(grad * n, axis=0, keepdims=True), back


def mid_back_kernel(*refs):
    own_ref, g_ref, mid_ref, hm_refs, gain_ref, w_ref, far = *refs[:3], refs[3:5], refs[5], refs[6], refs[7:10]
    dmid_ref, datt0_ref, datt1_ref, dl_ref, gain_out, wr_s, sem, far_s, sems = refs[10:]
    arrive = [fetch(b, far_s.at[i], sems.at[i]) for i, b in enumerate(far)]
    copy = fetch(w_ref.at[:, 2048:], wr_s, sem)
    grads = jnp.zeros((1, D), F32)
    for m in range(2):
        rows = slice(m * T, (m + 1) * T)
        total = own_ref[rows, :].astype(F32)
        for i in range(3):
            if m == 0:
                arrive[i].wait()
            total = total + far_s[i, rows, :].astype(F32)
        lanes = total[:, D:]
        d_gate = lanes + pltpu.roll(lanes, LANES - N_EXPERTS, 1)
        share = hm_refs[m][:, D:].astype(F32)
        gate = share + pltpu.roll(share, LANES - N_EXPERTS, 1)
        gate = jnp.where(lax.broadcasted_iota(jnp.int32, (T, LANES), 1) < N_EXPERTS, gate, 0.0)
        inner = jnp.sum(gate * d_gate, axis=-1, keepdims=True)
        d_logits = (gate * (d_gate - inner)).astype(BF)
        dl_ref[rows, :] = d_logits
        if m == 0:
            copy.wait()
        d_hm = total[:, :D] + mm(d_logits, wr_s[...], NT)
        grad_gain, back = norm_back(mid_ref[rows, :], gain_ref[1:2, :], d_hm)
        grads = grads + grad_gain
        d_mid = g_ref[rows, :].astype(F32) + back
        dmid_ref[rows, :] = d_mid
        (datt0_ref, datt1_ref)[m][...] = d_mid.astype(BF)
    gain_out[...] = jnp.broadcast_to(grads, (8, D))


def mid_back(rets, g, mid, hms, gains, w):
    return call(
        mid_back_kernel, "mid_back", [rets[0], g, mid, *hms, gains], [w, *rets[1:]],
        [sds((R, D), F32), sds((T, D), BF), sds((T, D), BF), sds((R, LANES), BF), sds((8, D), F32)], [],
        [pltpu.VMEM((D, LANES), BF), pltpu.SemaphoreType.DMA, pltpu.VMEM((3, R, D + LANES), BF), pltpu.SemaphoreType.DMA((3,))],
        2.8, 4,
    )


def attn_back_kernel(*refs):
    spots_ref, datt0_ref, datt1_ref, q_ref, own_ref, allowed_ref, cos_ref, sin_ref = refs[:8]
    w_refs, kv_refs, rest = refs[8:16], (None,) + refs[16:23], refs[23:]
    dq0_ref, dq1_ref, same_ref, other_ref, da, kv_s, kv_acc, w_s, sems, kv_sems = rest
    copies = fetch_w_out(spots_ref, w_refs, w_s, sems)
    key_copies = fetch_keys(kv_refs, kv_s, kv_sems)
    own_keys(own_ref, kv_s)
    d_att = jnp.concatenate([datt0_ref[...], datt1_ref[...]], axis=0)
    for copy in copies:
        copy.wait()
    for j in range(4):
        piece = mm(d_att, w_s[j * 384 : (j + 1) * 384, :], NT).astype(BF)
        for m in range(2):
            for i in range(3):
                da[m, j * 3 + i] = piece[m * T : (m + 1) * T, i * HS : (i + 1) * HS]
    for copy in key_copies:
        copy.wait()
    allowed = allowed_ref[...]
    cos, sin = cos_ref[:T, :], sin_ref[:T, :]
    for m in range(2):
        rows = slice(m * T, (m + 1) * T)
        for k in range(KV_HEADS):
            keys = kv_s[m, :, k * HS : (k + 1) * HS]
            values = kv_s[m, :, KW + k * HS : KW + (k + 1) * HS]
            q6 = heads_of(q_ref, m, k)
            d6 = da[m, k * GROUP : (k + 1) * GROUP].reshape(GROUP * T, HS)
            p = probs_of(q6, keys, allowed)
            dp = mm(d6, values, NT)
            ds = (p * (dp - jnp.sum(p * dp, axis=-1, keepdims=True)) * SCALE).astype(BF)
            dq = mm(ds, keys)
            for g in range(GROUP):
                h = k * GROUP + g
                (dq0_ref, dq1_ref)[m][:, h * HS : (h + 1) * HS] = rope_back(dq[g * T : (g + 1) * T], cos, sin).astype(BF)
            kv_acc[:, k * HS : (k + 1) * HS] = mm(ds, q6, TN)
            kv_acc[:, KW + k * HS : KW + (k + 1) * HS] = mm(p.astype(BF), d6, TN)
        for i in range(4):
            at = slice(i * R + m * T, i * R + (m + 1) * T)
            same_ref[at, :] = kv_acc[i * T : (i + 1) * T].astype(BF)
            other_ref[at, :] = kv_acc[C + i * T : C + (i + 1) * T].astype(BF)


def attn_back(spots, d_atts, w_o, q, kvs, allowed, cos, sin):
    return call(
        attn_back_kernel, "attn_back", [*d_atts, q, kvs[0], allowed, cos, sin], [*w_o, *kvs[1:]],
        [sds((T, D), BF), sds((T, D), BF), sds((4 * R, 512), BF), sds((4 * R, 512), BF)], [],
        [pltpu.VMEM((2, HEADS, T, HS), BF), pltpu.VMEM((2, SEQ, 512), BF), pltpu.VMEM((SEQ, 512), F32),
         pltpu.VMEM((D, D), BF), pltpu.SemaphoreType.DMA((32,)), pltpu.SemaphoreType.DMA((2, 8))],
        9, 12, spots,
    )


MSG = 512 + LANES


def qkv_back_kernel(*refs):
    own_ref, dq0_ref, dq1_ref, dl_ref, gm_ref, x0_ref, x1_ref, gain_ref, cos_ref, sin_ref, dmid_ref, w_ref = refs[:12]
    gin_ref, low_ref, msg_ref, dh, w_s, sems, far_s, far_sems = refs[15:]
    arrive = [fetch(b, far_s.at[i], far_sems.at[i]) for i, b in enumerate(refs[12:15])]
    copies = [fetch(w_ref.at[j * 384 : (j + 1) * 384, 0:2048], w_s.at[j], sems.at[j]) for j in range(4)]
    d_kv = own_ref[...].astype(F32)
    for i in range(3):
        arrive[i].wait()
        d_kv = d_kv + far_s[i].astype(F32)
    cos, sin = cos_ref[...], sin_ref[...]
    for i in range(KV_HEADS):
        at = slice(i * HS, (i + 1) * HS)
        msg_ref[:R, at] = rope_back(d_kv[:, at], cos, sin).astype(BF)
    msg_ref[:R, KW:512] = d_kv[:, KW:].astype(BF)
    msg_ref[:R, 512:] = dl_ref[...]
    dq = jnp.concatenate([dq0_ref[...], dq1_ref[...]], axis=0)
    for j in range(4):
        copies[j].wait()
        dh[:, j * 384 : (j + 1) * 384] = mm(dq, w_s[j, :, :D], NT) + mm(msg_ref[:R, :512], w_s[j, :, D:], NT)
    grads = jnp.zeros((1, D), F32)
    for m, x_ref in enumerate((x0_ref, x1_ref)):
        rows = slice(m * T, (m + 1) * T)
        grad_gain, back = norm_back(x_ref[...].astype(F32), gain_ref[0:1, :], dh[rows])
        grads = grads + grad_gain
        g_in = dmid_ref[rows, :] + back
        gin_ref[rows, :] = g_in
        low_ref[rows, :] = g_in.astype(BF)
    row = lax.broadcasted_iota(jnp.int32, (16, 512), 0)
    both = jnp.zeros((16, 512), F32)
    for c in range(3):
        at = slice(c * 512, (c + 1) * 512)
        both = jnp.where(row == c, jnp.broadcast_to(grads[:, at], (16, 512)), both)
        both = jnp.where(row == 3 + c, jnp.broadcast_to(gm_ref[0:1, at], (16, 512)), both)
    msg_ref[R:, :512] = both.astype(BF)
    msg_ref[R:, 512:] = jnp.zeros((16, LANES), BF)


def qkv_back(rets, dqs, dl, gm, x0, x1, gains, w, cos, sin, d_mid):
    return call(
        qkv_back_kernel, "qkv_back", [rets[0], *dqs, dl, gm, x0, x1, gains, cos, sin, d_mid], [w, *rets[1:]],
        [sds((R, D), F32), sds((R, D), BF), sds((R + 16, MSG), BF)], [],
        [pltpu.VMEM((R, D), F32), pltpu.VMEM((4, 384, 2048), BF), pltpu.SemaphoreType.DMA((4,)),
         pltpu.VMEM((3, R, 512), BF), pltpu.SemaphoreType.DMA((3,))],
        6.2, 11,
    )


ROWS = SLICE + 16


def attn_grad_kernel(*refs):
    order_ref, left_ref, msgs, dqs, datts, send_ref, (lh, rq, ro, rm, rg, sems) = refs[0], refs[1], refs[2:10], refs[10:26], refs[26:42], refs[42], refs[43:]
    left_copies, q_copies, o_copies, m_copies = [], [], [], []
    for i in range(8):
        at = slice(i * R, (i + 1) * R)
        left_copies.append(fetch(left_ref.at[order_ref[i]], lh.at[at, :], sems.at[0, i]))
        for m in range(2):
            half = slice(i * R + m * T, i * R + (m + 1) * T)
            o_copies.append(fetch(datts[2 * i + m], ro.at[half, :], sems.at[1 + m, i]))
            q_copies.append(fetch(dqs[2 * i + m], rq.at[half, :], sems.at[3 + m, i]))
        m_copies.append(fetch(msgs[i].at[:R, :], rm.at[at, :], sems.at[5, i]))
        m_copies.append(fetch(msgs[i].at[R:, :], rg.at[i], sems.at[6, i]))
    for copy in left_copies + o_copies:
        copy.wait()

    def spread(grads, width, lane):
        for r in range(8):
            send_ref[r, :SLICE, lane : lane + width] = grads[:SLICE, r * width : (r + 1) * width].astype(BF)

    spread(mm(lh[:, 256:512], ro[...], TN), SLICE, 320)
    for copy in q_copies:
        copy.wait()
    spread(mm(lh[:, :256], rq[...], TN), SLICE, 0)
    for copy in m_copies:
        copy.wait()
    spread(mm(lh[:, :256], rm[:, :512], TN), 64, SLICE)
    small = mm(lh[:, 512:], rm[:, 512:], TN)[:SLICE, :64].astype(BF)
    gains = sum(rg[i, :, :512].astype(F32) for i in range(8)).astype(BF)
    for r in range(8):
        send_ref[r, :SLICE, 256:320] = small
        send_ref[r, SLICE:, :] = gains


def attn_grad(order, left, msgs, dqs, datts):
    return pl.pallas_call(
        attn_grad_kernel,
        name="attn_grad",
        in_specs=[SCALARS] + [AWAY] * 41,
        out_specs=HERE,
        out_shape=sds((8, ROWS, 512), BF),
        scratch_shapes=[
            pltpu.VMEM((8 * R, 768), BF), pltpu.VMEM((8 * R, D), BF), pltpu.VMEM((8 * R, D), BF), pltpu.VMEM((8 * R, MSG), BF),
            pltpu.VMEM((8, 16, MSG), BF), pltpu.SemaphoreType.DMA((7, 8)),
        ],
        compiler_params=pltpu.CompilerParams(vmem_limit_bytes=20 * 2**20),
        cost_estimate=work(8.5),
    )(order, *in_hbm((left, *msgs, *dqs, *datts)))


def turn_kernel(*refs):
    lefts, (h_out, a_out, f_s, h_s, a_s, sems) = refs[:2], refs[2:]
    copies = [fetch(left, f_s.at[i], sems.at[i]) for i, left in enumerate(lefts)]
    for i in range(2):
        copies[i].wait()
        h_s[:, i * B : (i + 1) * B] = f_s[i, :, :D].T
        a_s[:, i * B : (i + 1) * B] = f_s[i, :, D:].T
    sent = [fetch(h_s, h_out, sems.at[2]), fetch(a_s, a_out, sems.at[3])]
    for copy in sent:
        copy.wait()


def turn(lefts):
    return call(
        turn_kernel, "turn", [], lefts, [], [sds((D, 4 * C), BF), sds((FF, 4 * C), BF)],
        [pltpu.VMEM((2, B, FW), BF), pltpu.VMEM((D, 4 * C), BF), pltpu.VMEM((FF, 4 * C), BF), pltpu.SemaphoreType.DMA((6,))],
        5, 14,
    )


def expert_grad_kernel(in_ref, down_ref, *refs):
    rights, out_ref, right = refs[:2], refs[2], refs[3]
    j = pl.program_id(0)
    for i in range(2):
        right[i * B : (i + 1) * B, :] = rights[i][...]

    def grads(left_ref, rows, first):
        for r in range(0, 8, 2):
            out_ref[r : r + 2, first : first + rows, :] = mm(left_ref[r * rows : (r + 2) * rows, :], right[...]).astype(BF).reshape(2, rows, 512)

    @pl.when(j % 2 == 0)
    def _():
        grads(in_ref, SLICE, 0)

    @pl.when(j % 2 == 1)
    def _():
        grads(down_ref, SLICE // 2, SLICE)


def expert_grad(left_in, left_down, rights):
    return pl.pallas_call(
        expert_grad_kernel,
        name="expert_grad",
        grid=(6,),
        in_specs=[whole((D, 4 * C)), whole((FF, 4 * C))] + [pl.BlockSpec((B, 512), lambda j: (0, (j % 2) * 3 + j // 2))] * 2,
        out_specs=pl.BlockSpec((8, SLICE + SLICE // 2, 512), lambda j: (0, 0, j // 2)),
        out_shape=pltpu.HBM((8, SLICE + SLICE // 2, D), BF),
        scratch_shapes=[pltpu.VMEM((4 * C, 512), BF)],
        compiler_params=pltpu.CompilerParams(dimension_semantics=("arbitrary",), vmem_limit_bytes=26 * 2**20),
        cost_estimate=work(20),
    )(*in_hbm((left_in, left_down, *rights)))


def body(tokens_in, cotangent, routes, gain_attn, w_query, w_keyval, w_out, gain_moe, w_router, w_in, w_down):
    is_first = lax.axis_index("section") == 0
    shard = lax.axis_index("shard")
    rep = lax.axis_index("rep")
    chip, core = shard // 2, shard % 2
    micros = range(2)

    extra = jnp.concatenate([w_router[0], gain_attn[0][:, None], gain_moe[0][:, None]], axis=1)
    extra = jnp.pad(extra, ((0, 0), (0, LANES - extra.shape[1])))
    packed = jnp.concatenate([w_query[0], w_keyval[0], extra], axis=1)
    w = lax.all_gather(packed, "shard", axis=0, tiled=True)
    pick = (jnp.arange(LANES)[None, :] == (jnp.arange(8)[:, None] + N_EXPERTS)) & (jnp.arange(8)[:, None] < 2)
    gains = mm(pick.astype(BF), w[:, 2048:], NT)
    z = rep // 2

    quarter = lax.dynamic_slice_in_dim(w_out[0], z * (SLICE // 4), SLICE // 4, 0)
    quarters = jnp.stack(from_chips(quarter))
    along_z = [quarters] + [lax.ppermute(quarters, "rep", [(i, ((i // 2 + k) % 4) * 2 + i % 2) for i in range(8)]) for k in (1, 2, 3)]
    w_o = along_z + [swap(piece) for piece in along_z]
    spots = [((chip - ky) % 4) * 2 * SLICE + c * SLICE + ((z - kz) % 4) * (SLICE // 4) for c in (core, 1 - core) for kz in range(4) for ky in range(4)]
    spots = jnp.stack(spots).astype(jnp.int32)

    inner = (w_in[0, 0], swap(w_in[0, 0]))
    outer = (w_down[0, 0], swap(w_down[0, 0]))
    w, gains, inner, outer = lax.optimization_barrier((w, gains, inner, outer))

    half = HS // 2
    frequency = ROPE_BASE ** (-jnp.arange(half, dtype=F32) * 2.0 / HS)
    place = shard * T + jnp.arange(T, dtype=jnp.int32)
    angles = place.astype(F32)[:, None] * frequency[None, :]
    angles = jnp.concatenate([angles, angles], axis=0)
    cos = jnp.concatenate([jnp.cos(angles)] * 2, axis=1)
    sin = jnp.concatenate([-jnp.sin(angles), jnp.sin(angles)], axis=1)
    order = jnp.stack([((chip - k) % 4) * 2 + c for c in (core, 1 - core) for k in range(4)]).astype(jnp.int32)
    key_place = (order[:, None] * T + jnp.arange(T, dtype=jnp.int32)[None, :]).reshape(1, SEQ)
    allowed = (key_place <= place[:, None]).astype(F32)
    lane = jnp.arange(LANES, dtype=jnp.int32)
    other = shard ^ 1
    mine = jnp.stack([(lane == e) | (lane == e + N_EXPERTS) for e in (shard, other)]).astype(F32)
    mine = jnp.pad(mine, ((0, 6), (0, 0)))
    put = jnp.stack([lane == shard, lane == shard + N_EXPERTS, lane == other, lane == other + N_EXPERTS]).astype(F32)
    put = jnp.pad(put, ((0, 4), (0, 0)))
    chosen = jnp.any(routes[0, :, 0].reshape(R, -1)[:, :, None] == lane[None, None, :], axis=1).astype(F32)

    hold = lax.optimization_barrier

    def attention(x, save):
        q, kv, h_attn = qkv(x[0], x[1], gains, w, cos, sin)
        kvs = gather_blocks(kv)
        att, mid, *hm = attend(spots, q, kvs, allowed, x[0], x[1], w_o, w, gains, chosen, h_attn, save)
        return q, kvs, mid, hm

    def keys_back(same, other):
        got = swap(other)
        return to_chips([plus(same[k * R : (k + 1) * R], got[k * R : (k + 1) * R]) for k in range(4)])

    tokens = [tokens_in[m, 0] for m in micros]
    given = cotangent.reshape(R, D)
    _, _, mid, hms = attention(tokens, False)
    blocks = [from_chips(hm) for hm in hms]
    out = expert(blocks[0], mine, inner, outer, False)
    blocks[1][0], _ = hold((blocks[1][0], out[0]))
    outs = [out, expert(blocks[1], mine, inner, outer, False)]
    first = [(mid[m * T : (m + 1) * T] + sum(r.astype(F32) for r in to_chips(outs[m]))).astype(BF) for m in micros]
    arrived = [lax.ppermute(first[m], "section", [(0, 1)]) for m in micros]
    arrived, given_blocks = hold((arrived, from_chips(given)))

    x = [jnp.where(is_first, tokens[m], arrived[m]) for m in micros]
    q, kvs, mid, (*hms, left) = attention(x, True)
    out = expert(halves_from_chips(*hms), mine, inner, outer, True)
    parts, (g_share, f_own, f_other), kept = out[:4], out[4:7], out[7:]
    f_got = swap(f_other)

    acts = (mid + sum(r.astype(F32) for r in to_chips(parts))).astype(BF)
    out = expert_back(given_blocks, (g_share, *kept), put, inner, outer, False)
    out, acts = hold((out, acts))
    rets = to_chips(out)
    rets, f_got, left = hold((rets, f_got, left))
    left = lax.all_to_all(left, "shard", split_axis=0, concat_axis=0, tiled=True)
    d_mid, datt0, datt1, dl, gm = mid_back(rets, given, mid, hms, gains, w)
    dq0, dq1, kv_same, kv_other = attn_back(spots, (datt0, datt1), w_o, q, kvs, allowed, cos, sin)
    kv_rets, (h_turned, act_turned), left = hold((keys_back(kv_same, kv_other), turn([f_own, f_got]), left))
    _, low, _ = qkv_back(kv_rets, (dq0, dq1), dl, gm, x[0], x[1], gains, w, cos, sin, d_mid)
    arrived = lax.ppermute(low, "section", [(1, 0)])
    halves = [jnp.where(is_first, arrived[m * T : (m + 1) * T], given[m * T : (m + 1) * T]) for m in micros]
    given = jnp.where(is_first, arrived, given)

    out = expert_back(halves_from_chips(*halves), (g_share, *kept), put, inner, outer, True)
    rets, rights = to_chips(out[:4]), [out[4], swap(out[5])]
    rets, send = hold((rets, expert_grad(h_turned, act_turned, rights)))
    expert_parts = lax.all_to_all(send, "rep", split_axis=0, concat_axis=0, tiled=True)
    d_mid, datt0, datt1, dl, gm = mid_back(rets, given, mid, hms, gains, w)
    datts = halves_from_chips(datt0, datt1)
    dq0, dq1, kv_same, kv_other = attn_back(spots, (datt0, datt1), w_o, q, kvs, allowed, cos, sin)
    datts, kv_same, kv_other = hold((datts, kv_same, kv_other))
    kv_rets = keys_back(kv_same, kv_other)
    kv_rets, dq0_sent, dq1_sent = hold((kv_rets, dq0, dq1))
    dqs = halves_from_chips(dq0_sent, dq1_sent)
    g_in, _, msg = qkv_back(kv_rets, (dq0, dq1), dl, gm, x[0], x[1], gains, w, cos, sin, d_mid)

    msgs = from_chips(msg)
    dqs, msgs = hold((dqs, msgs))
    dqs, datts, msgs = (blocks + [swap(b) for b in blocks] for blocks in (dqs, datts, msgs))
    send = attn_grad(order, left, msgs, dqs, datts)
    expert_parts, send = hold((expert_parts, send))
    got = lax.all_to_all(send, "rep", split_axis=0, concat_axis=0, tiled=True)
    sums = jnp.sum(got.astype(F32), axis=0)
    g_q, g_kv, g_r, g_o = (sums[:SLICE, a:b] for a, b in ((0, 192), (192, 256), (256, 256 + N_EXPERTS), (320, 512)))
    g_gains = lax.dynamic_slice(sums[SLICE : SLICE + 6].reshape(2, D), (0, shard * SLICE), (2, SLICE))
    expert_sums = jnp.sum(expert_parts.astype(F32), axis=0)

    return (
        acts.reshape(1, 2, 1, T, D),
        g_in.reshape(1, 2, 1, T, D),
        g_gains[0:1],
        g_q[None],
        g_kv[None],
        g_o[None],
        g_gains[1:2],
        g_r[None],
        expert_sums[None, None, :SLICE],
        expert_sums[None, None, SLICE:],
    )


def solution(mesh):
    in_specs = (
        P(None, "rep", "shard", None),
        P(None, "rep", "shard", None),
        P("section", None, "rep", "shard", None),
        P("section", "shard"),
        P("section", "shard", None),
        P("section", "shard", None),
        P("section", "shard", None),
        P("section", "shard"),
        P("section", "shard", None),
        P("section", "shard", None, None),
        P("section", "shard", None, None),
    )
    out_specs = (
        P("section", None, "rep", "shard", None),
        P("section", None, "rep", "shard", None),
        P("section", "shard"),
        P("section", "shard", "rep"),
        P("section", "shard", "rep"),
        P("section", "shard", "rep"),
        P("section", "shard"),
        P("section", "shard", None),
        P("section", "shard", "rep", None),
        P("section", "shard", "rep", None),
    )
    return jax.shard_map(body, mesh=mesh, in_specs=in_specs, out_specs=out_specs, check_vma=False)
```

```python
import jax
import jax.numpy as jnp
from jax import lax
from jax.experimental import pallas as pl
from jax.experimental.pallas import tpu as pltpu
from jax.sharding import PartitionSpec as P

D = 1536
T = 64
R = 2 * T
C = 4 * T
B = 4 * R
HEADS = 12
KV_HEADS = 2
GROUP = HEADS // KV_HEADS
HS = 128
KW = KV_HEADS * HS
SLICE = D // 8
FF = 768
SEQ = 512
N_EXPERTS = 8
LANES = 128
EPS = 1e-06
ROPE_BASE = 1000000.0
SCALE = HS**-0.5
BF = jnp.bfloat16
VMEM = 18 * 2**20
F32 = jnp.float32

NN = (((1,), (0,)), ((), ()))
NT = (((1,), (1,)), ((), ()))
TN = (((0,), (0,)), ((), ()))


def mm(a, b, dims=NN):
    return lax.dot_general(a, b, dims, preferred_element_type=F32)


def sds(shape, dtype):
    return jax.ShapeDtypeStruct(shape, dtype)


def whole(shape):
    return pl.BlockSpec(shape, lambda *_: (0,) * len(shape))


def in_hbm(args):
    return [pltpu.with_memory_space_constraint(a, pltpu.HBM) for a in args]


HERE = pl.BlockSpec(memory_space=pltpu.VMEM)
AWAY = pl.BlockSpec(memory_space=pltpu.HBM)
SCALARS = pl.BlockSpec(memory_space=pltpu.SMEM)


def work(us):
    return pl.CostEstimate(flops=1, bytes_accessed=int(us * 3.7 * 10**6), transcendentals=0)


def call(kernel, name, here, away, outs, outs_away, scratch, us, vmem, scalars=None):
    scalars = [] if scalars is None else [scalars]
    return pl.pallas_call(
        kernel,
        name=name,
        in_specs=[SCALARS] * len(scalars) + [HERE] * len(here) + [AWAY] * len(away),
        out_specs=[HERE] * len(outs) + [AWAY] * len(outs_away),
        out_shape=outs + [pltpu.HBM(o.shape, o.dtype) for o in outs_away],
        scratch_shapes=scratch,
        compiler_params=pltpu.CompilerParams(vmem_limit_bytes=vmem * 2**20),
        cost_estimate=work(us),
    )(*scalars, *here, *in_hbm(away))


def fetch(src, dst, sem):
    copy = pltpu.make_async_copy(src, dst, sem)
    copy.start()
    return copy


def swap(x):
    return lax.ppermute(x, "shard", [(i, i ^ 1) for i in range(8)])


def along_y(x, k):
    return lax.ppermute(x, "shard", [(i, (i + 2 * k) % 8) for i in range(8)])


def from_chips(x):
    return [x, along_y(x, 1), along_y(x, 2), along_y(x, 3)]


def halves_from_chips(lo, hi):
    near_lo, over_hi = along_y(lo, 1), along_y(hi, 3)
    far_lo, far_hi = along_y(near_lo, 1), along_y(over_hi, 3)
    return [lo, hi, near_lo, along_y(hi, 1), far_lo, far_hi, along_y(lo, 3), over_hi]


def to_chips(blocks):
    return [blocks[0]] + [along_y(blocks[k], -k) for k in (1, 2, 3)]


def gather_blocks(x):
    same = from_chips(x)
    return same + [swap(b) for b in same]


def plus(a, b):
    return (a.astype(F32) + b.astype(F32)).astype(BF)


def rope(x, cos, sin):
    return x * cos + pltpu.roll(x, HS // 2, 1) * sin


def rope_back(x, cos, sin):
    return x * cos - pltpu.roll(x, HS // 2, 1) * sin


def qkv_kernel(x0_ref, x1_ref, gain_ref, cos_ref, sin_ref, w_ref, q_ref, kv_ref, h_ref, w_s, sems):
    copies = [fetch(w_ref.at[:, j * 512 : (j + 1) * 512], w_s.at[j], sems.at[j]) for j in range(4)]
    for m, x_ref in enumerate((x0_ref, x1_ref)):
        x = x_ref[...].astype(F32)
        r = lax.rsqrt(jnp.mean(x * x, axis=-1, keepdims=True) + EPS)
        h_ref[m * T : (m + 1) * T, :] = (x * r * gain_ref[0:1, :]).astype(BF)
    cos, sin = cos_ref[...], sin_ref[...]
    for j in range(4):
        copies[j].wait()
        y = mm(h_ref[...], w_s[j])
        for i in range(4 if j < 3 else 2):
            at = slice(i * HS, (i + 1) * HS)
            turned = rope(y[:, at], cos, sin).astype(BF)
            if j < 3:
                q_ref[:, j * 512 + i * HS : j * 512 + (i + 1) * HS] = turned
            else:
                kv_ref[:, at] = turned
        if j == 3:
            kv_ref[:, KW:] = y[:, KW:].astype(BF)


def qkv(x0, x1, gains, w, cos, sin):
    return call(
        qkv_kernel, "qkv", [x0, x1, gains, cos, sin], [w],
        [sds((R, D), BF), sds((R, 512), BF), sds((R, D), BF)], [],
        [pltpu.VMEM((4, D, 512), BF), pltpu.SemaphoreType.DMA((4,))],
        3.5, 8,
    )


def fetch_keys(kv_refs, kv_s, sems):
    return [
        fetch(kv_refs[i].at[m * T : (m + 1) * T, :], kv_s.at[m, i * T : (i + 1) * T, :], sems.at[m, i]) for i in range(1, 8) for m in range(2)
    ]


def own_keys(own, kv_s):
    for m in range(2):
        kv_s[m, 0:T, :] = own[m * T : (m + 1) * T, :]


def heads_of(ref, m, k):
    rows = slice(m * T, (m + 1) * T)
    return jnp.concatenate([ref[rows, h * HS : (h + 1) * HS] for h in range(k * GROUP, (k + 1) * GROUP)], axis=0)


def probs_of(q6, keys, allowed):
    s = mm(q6, keys, NT) * SCALE
    s = jnp.where(allowed[None] > 0, s.reshape(GROUP, T, SEQ), -1e30)
    e = jnp.exp(s - jnp.max(s, axis=-1, keepdims=True))
    p = e * (1.0 / jnp.sum(e, axis=-1, keepdims=True))
    return p.reshape(GROUP * T, SEQ)


def fetch_w_out(spots_ref, pieces, w_s, sems):
    copies = []
    for p, piece in enumerate(pieces):
        for k in range(4):
            i = p * 4 + k
            at = pl.ds(pl.multiple_of(spots_ref[i], 16), SLICE // 4)
            copies.append(fetch(piece.at[k], w_s.at[at, :], sems.at[i]))
    return copies


def attend_kernel(save, *refs):
    spots_ref, q_ref, own_ref, allowed_ref, x0_ref, x1_ref, gain_ref, chosen_ref, rest = *refs[:8], refs[8:]
    if save:
        h_ref, rest = rest[0], rest[1:]
    w_refs, wp_ref, kv_refs, rest = rest[:8], rest[8], (None,) + rest[9:16], rest[16:]
    if save:
        att_ref, mid_ref, hm0_ref, hm1_ref, left_ref, kv_s, w_s, wr_s, sems, kv_sems = rest
    else:
        att_ref, mid_ref, hm0_ref, hm1_ref, kv_s, w_s, wr_s, sems, kv_sems = rest
    key_copies = fetch_keys(kv_refs, kv_s, kv_sems)
    router_copy = fetch(wp_ref.at[:, 2048:], wr_s, sems.at[32])
    copies = fetch_w_out(spots_ref, w_refs, w_s, sems)
    own_keys(own_ref, kv_s)
    allowed = allowed_ref[...]
    for copy in key_copies:
        copy.wait()
    for m in range(2):
        for k in range(KV_HEADS):
            p = probs_of(heads_of(q_ref, m, k), kv_s[m, :, k * HS : (k + 1) * HS], allowed).astype(BF)
            o = mm(p, kv_s[m, :, KW + k * HS : KW + (k + 1) * HS])
            for g in range(GROUP):
                h = k * GROUP + g
                att_ref[m * T : (m + 1) * T, h * HS : (h + 1) * HS] = o[g * T : (g + 1) * T].astype(BF)
    square = [0.0, 0.0]
    for copy in copies:
        copy.wait()
    for j in range(3):
        at = slice(j * 512, (j + 1) * 512)
        y = mm(att_ref[...], w_s[:, at])
        for m, x_ref in enumerate((x0_ref, x1_ref)):
            rows = slice(m * T, (m + 1) * T)
            mid = x_ref[:, at].astype(F32) + y[rows]
            mid_ref[rows, at] = mid
            square[m] = square[m] + jnp.sum(mid * mid, axis=-1, keepdims=True)
    router_copy.wait()
    for m, hm_ref in enumerate((hm0_ref, hm1_ref)):
        rows = slice(m * T, (m + 1) * T)
        r = lax.rsqrt(square[m] * (1.0 / D) + EPS)
        hm_ref[:, :D] = (mid_ref[rows, :] * r * gain_ref[1:2, :]).astype(BF)
        logits = mm(hm_ref[:, :D], wr_s[...])
        chosen = chosen_ref[rows, :] > 0
        top = jnp.max(jnp.where(chosen, logits, -jnp.inf), axis=-1, keepdims=True)
        e = jnp.where(chosen, jnp.exp(jnp.minimum(logits - top, 0.0)), 0.0)
        gate = e / jnp.sum(e, axis=-1, keepdims=True)
        high = gate.astype(BF).astype(F32)
        hm_ref[:, D:] = (high + pltpu.roll(gate - high, N_EXPERTS, 1)).astype(BF)
        if save:
            for a in range(3):
                for i in range(8):
                    cut = slice(i * SLICE, (i + 1) * SLICE)
                    rows_of = hm_ref[:, cut] if a == 2 else (h_ref, att_ref)[a][rows, cut]
                    left_ref[i, rows, a * 256 : a * 256 + SLICE] = rows_of
                    left_ref[i, rows, a * 256 + SLICE : (a + 1) * 256] = jnp.zeros((T, 256 - SLICE), BF)


def attend(spots, q, kvs, allowed, x0, x1, w_o, w, gains, chosen, h_attn, save):
    more = [h_attn] if save else []
    return call(
        lambda *refs: attend_kernel(save, *refs), "attend", [q, kvs[0], allowed, x0, x1, gains, chosen, *more], [*w_o, w, *kvs[1:]],
        [sds((R, D), BF), sds((R, D), F32)] + [sds((T, D + LANES), BF)] * 2 + [sds((8, R, 768), BF) for _ in more], [],
        [pltpu.VMEM((2, SEQ, 512), BF), pltpu.VMEM((D, D), BF), pltpu.VMEM((D, LANES), BF), pltpu.SemaphoreType.DMA((33,)),
         pltpu.SemaphoreType.DMA((2, 8))],
        7, 11, spots,
    )


FW = D + FF
GW = 2 * D
SLOTS = 3
WEIGHT_SLOTS = [pltpu.VMEM((SLOTS, D, 512), BF), pltpu.VMEM((SLOTS, 256, D), BF), pltpu.SemaphoreType.DMA((SLOTS, 3))]


def fetch_step(step, w_in, w_down, w_s, d_s, sems):
    e, f, slot = step // 3, step % 3, step % SLOTS
    return [
        fetch(w_in[e].at[:, f * 256 : (f + 1) * 256], w_s.at[slot, :, 0:256], sems.at[slot, 0]),
        fetch(w_in[e].at[:, FF + f * 256 : FF + (f + 1) * 256], w_s.at[slot, :, 256:512], sems.at[slot, 1]),
        fetch(w_down[e].at[f * 256 : (f + 1) * 256, :], d_s.at[slot], sems.at[slot, 2]),
    ]


def expert_kernel(own, save, *refs):
    own_refs, refs = refs[:own], refs[own:]
    mine_ref, w_in, w_down, hm_refs, refs = refs[0], refs[1:3], refs[3:5], refs[5 : 5 + 3 * own], refs[5 + 3 * own :]
    outs, rest = refs[:4], refs[4:]
    if save:
        g_ref, f_out, (gate_out, up_out, prod_out), rest = rest[0], rest[1:3], rest[3:6], rest[6:]
        (f_s, act_s, gate_s, up_s, prod_s, out_sems), rest = rest[:6], rest[6:]
        h_ref = f_s
    else:
        h_ref, g_ref, rest = rest[0], rest[1], rest[2:]
    lanes_s, hm_sems, acc, total, w_s, d_s, sems = rest
    n = own_refs[0].shape[0]
    arrive = []
    for i, b in enumerate(hm_refs, own):
        at = slice(i * n, (i + 1) * n)
        arrive.append(fetch(b.at[:, :D], h_ref.at[at, :D], hm_sems.at[i, 0]))
        arrive.append(fetch(b.at[:, D:], lanes_s.at[at, :], hm_sems.at[i, 1]))
    copies = [fetch_step(step, w_in, w_down, w_s, d_s, sems) for step in range(SLOTS)]
    for i, b in enumerate(own_refs):
        h_ref[i * n : (i + 1) * n, :D] = b[:, :D]
        lanes_s[i * n : (i + 1) * n, :] = b[:, D:]
    for copy in arrive:
        copy.wait()
    lanes = lanes_s[...].astype(F32)
    for e in range(2):
        g = jnp.sum(lanes * mine_ref[e : e + 1, :], axis=-1, keepdims=True)
        g_ref[e] = jnp.broadcast_to(g, (4 * own * n, LANES))
    sent = []
    for step in range(6):
        e, f, slot = step // 3, step % 3, step % SLOTS
        for copy in copies[step]:
            copy.wait()
        both = mm(h_ref[:, :D], w_s[slot])
        gate, up = both[:, :256], both[:, 256:]
        act = (gate / (1.0 + jnp.exp(-gate)) * up).astype(BF)
        add = mm(act, d_s[slot])
        if save:
            cols = slice(f * 256, (f + 1) * 256)
            gate_s[e, :, cols] = gate.astype(BF)
            up_s[e, :, cols] = up.astype(BF)
            if e == 0:
                f_s[:, D + f * 256 : D + (f + 1) * 256] = act
            else:
                act_s[:, cols] = act
        if step + SLOTS < 6:
            copies.append(fetch_step(step + SLOTS, w_in, w_down, w_s, d_s, sems))
        if f == 0:
            acc[...] = add
        elif f == 1:
            acc[...] += add
        else:
            prod = (acc[...] + add).astype(BF)
            weighted = prod.astype(F32) * g_ref[e, :, 0:1]
            if save:
                prod_s[e] = prod
                sent.append(fetch(gate_s.at[e], gate_out.at[e], out_sems.at[e, 0]))
                sent.append(fetch(up_s.at[e], up_out.at[e], out_sems.at[e, 1]))
                sent.append(fetch(prod_s.at[e], prod_out.at[e], out_sems.at[e, 2]))
                if e == 0:
                    sent.append(fetch(f_s, f_out[0], out_sems.at[0, 3]))
                    sent.append(fetch(f_s.at[:, :D], f_out[1].at[:, :D], out_sems.at[0, 4]))
                else:
                    sent.append(fetch(act_s, f_out[1].at[:, D:], out_sems.at[1, 3]))
            if e == 0:
                total[...] = weighted
            else:
                part = (total[...] + weighted).astype(BF)
                for i, o in enumerate(outs):
                    o[...] = part[i * own * n : (i + 1) * own * n]
    for copy in sent:
        copy.wait()


def expert(hms, mine, w_in, w_down, save):
    own, n = len(hms) // 4, hms[0].shape[0]
    rows = len(hms) * n
    outs, away = [sds((own * n, D), BF)] * 4, []
    scratch = [pltpu.VMEM((rows, LANES), BF), pltpu.SemaphoreType.DMA((8, 2)), pltpu.VMEM((rows, D), F32), pltpu.VMEM((rows, D), F32)] + WEIGHT_SLOTS
    if save:
        outs = outs + [sds((2, rows, LANES), F32)]
        away = [sds((rows, FW), BF), sds((rows, FW), BF), sds((2, rows, FF), BF), sds((2, rows, FF), BF), sds((2, rows, D), BF)]
        scratch = [pltpu.VMEM((rows, FF), BF) if i == 1 else pltpu.VMEM(o.shape, o.dtype) for i, o in enumerate(away)] + [pltpu.SemaphoreType.DMA((2, 5))] + scratch
    else:
        scratch = [pltpu.VMEM((rows, D), BF), pltpu.VMEM((2, rows, LANES), F32)] + scratch
    return call(
        lambda *refs: expert_kernel(own, save, *refs), "expert", [*hms[:own], mine], [*w_in, *w_down, *hms[own:]], outs, away, scratch,
        14 if save else 7.7, 30 if save else 12,
    )


def expert_back_kernel(own, save, *refs):
    own_refs, refs = refs[:own], refs[own:]
    g_ref, put_ref, rest = refs[0], refs[1], refs[2:]
    (gate_in, up_in, prod_in), w_in, w_down = rest[:3], rest[3:5], rest[5:7]
    g_in, rest = rest[7 : 7 + 3 * own], rest[7 + 3 * own :]
    outs, rest = rest[:4], rest[4:]
    if save:
        d_out, d_s, out_sems, rest = rest[:2], rest[2:4], rest[4], rest[5:]
    g_s, g_sems, lanes_s, dprod, gate_s, up_s, prod_s, in_sems, acc, total, w_s, d_w, sems = rest
    n = own_refs[0].shape[0]
    arrive = [fetch(b, g_s.at[i * n : (i + 1) * n, :], g_sems.at[i]) for i, b in enumerate(g_in, own)]
    kept = [
        [fetch(src.at[e], dst.at[e], in_sems.at[e, i]) for i, (src, dst) in enumerate(((prod_in, prod_s), (gate_in, gate_s), (up_in, up_s)))]
        for e in range(2)
    ]
    copies = [fetch_step(step, w_in, w_down, w_s, d_w, sems) for step in range(SLOTS)]
    put = put_ref[...]
    for i, b in enumerate(own_refs):
        g_s[i * n : (i + 1) * n, :] = b[...]
    for copy in arrive:
        copy.wait()
    sent = []
    for step in range(6):
        e, f, slot = step // 3, step % 3, step % SLOTS
        if f == 0:
            kept[e][0].wait()
            for i in range(8):
                at = slice(i * T, (i + 1) * T)
                g = g_s[at, :].astype(F32)
                d_prod = (g * g_ref[e, at, 0:1]).astype(BF)
                dprod[at, :] = d_prod
                if save:
                    d_s[e][at, D:] = d_prod
                d = jnp.sum(g * prod_s[e, at, :].astype(F32), axis=-1, keepdims=True)
                high = d.astype(BF).astype(F32)
                lanes = high * put[2 * e : 2 * e + 1, :] + (d - high) * put[2 * e + 1 : 2 * e + 2, :]
                lanes_s[at, :] = lanes if e == 0 else lanes_s[at, :] + lanes
            kept[e][1].wait()
            kept[e][2].wait()
        for copy in copies[step]:
            copy.wait()
        cols = slice(f * 256, (f + 1) * 256)
        d_act = mm(dprod[...], d_w[slot], NT)
        gate, up = gate_s[e, :, cols].astype(F32), up_s[e, :, cols].astype(F32)
        s = 1.0 / (1.0 + jnp.exp(-gate))
        dg = (d_act * up * (s * (1.0 + gate * (1.0 - s)))).astype(BF)
        du = (d_act * (gate * s)).astype(BF)
        if save:
            d_s[e][:, cols] = dg
            d_s[e][:, FF + f * 256 : FF + (f + 1) * 256] = du
        add = mm(jnp.concatenate([dg, du], axis=1), w_s[slot], NT)
        if step + SLOTS < 6:
            copies.append(fetch_step(step + SLOTS, w_in, w_down, w_s, d_w, sems))
        if f == 0:
            acc[...] = add
        elif f == 1:
            acc[...] += add
        else:
            rows_grad = (acc[...] + add).astype(BF).astype(F32)
            if save:
                sent.append(fetch(d_s[e], d_out[e], out_sems.at[e]))
            if e == 0:
                total[...] = rows_grad.astype(BF)
            else:
                part = (total[...].astype(F32) + rows_grad).astype(BF)
                for i, o in enumerate(outs):
                    at = slice(i * R, (i + 1) * R)
                    o[:, :D] = part[at]
                    o[:, D:] = lanes_s[at, :].astype(BF)
    for copy in sent:
        copy.wait()


def expert_back(gs, kept, put, w_in, w_down, save):
    g_share, gate, up, produced = kept
    own, rows = len(gs) // 4, B
    away, scratch = [], []
    if save:
        away = [sds((rows, GW), BF)] * 2
        scratch = [pltpu.VMEM(o.shape, o.dtype) for o in away] + [pltpu.SemaphoreType.DMA((2,))]
    scratch = scratch + [
        pltpu.VMEM((rows, D), BF), pltpu.SemaphoreType.DMA((8,)), pltpu.VMEM((rows, LANES), F32), pltpu.VMEM((rows, D), BF), pltpu.VMEM((2, rows, FF), BF), pltpu.VMEM((2, rows, FF), BF),
        pltpu.VMEM((2, rows, D), BF), pltpu.SemaphoreType.DMA((2, 3)), pltpu.VMEM((rows, D), F32), pltpu.VMEM((rows, D), BF),
    ] + WEIGHT_SLOTS
    return call(
        lambda *refs: expert_back_kernel(own, save, *refs), "expert_back", [*gs[:own], g_share, put], [gate, up, produced, *w_in, *w_down, *gs[own:]],
        [sds((R, D + LANES), BF)] * 4, away, scratch, 19 if save else 17, 32 if save else 26,
    )


def norm_back(x, gain, grad):
    r = lax.rsqrt(jnp.mean(x * x, axis=-1, keepdims=True) + EPS)
    n = x * r
    scaled = grad * gain
    back = r * (scaled - n * jnp.mean(scaled * n, axis=-1, keepdims=True))
    return jnp.sum(grad * n, axis=0, keepdims=True), back


def mid_back_kernel(*refs):
    own_ref, g_ref, mid_ref, hm_refs, gain_ref, w_ref, far = *refs[:3], refs[3:5], refs[5], refs[6], refs[7:10]
    dmid_ref, datt0_ref, datt1_ref, dl_ref, gain_out, wr_s, sem, far_s, sems = refs[10:]
    arrive = [fetch(b, far_s.at[i], sems.at[i]) for i, b in enumerate(far)]
    copy = fetch(w_ref.at[:, 2048:], wr_s, sem)
    grads = jnp.zeros((1, D), F32)
    for m in range(2):
        rows = slice(m * T, (m + 1) * T)
        total = own_ref[rows, :].astype(F32)
        for i in range(3):
            if m == 0:
                arrive[i].wait()
            total = total + far_s[i, rows, :].astype(F32)
        lanes = total[:, D:]
        d_gate = lanes + pltpu.roll(lanes, LANES - N_EXPERTS, 1)
        share = hm_refs[m][:, D:].astype(F32)
        gate = share + pltpu.roll(share, LANES - N_EXPERTS, 1)
        gate = jnp.where(lax.broadcasted_iota(jnp.int32, (T, LANES), 1) < N_EXPERTS, gate, 0.0)
        inner = jnp.sum(gate * d_gate, axis=-1, keepdims=True)
        d_logits = (gate * (d_gate - inner)).astype(BF)
        dl_ref[rows, :] = d_logits
        if m == 0:
            copy.wait()
        d_hm = total[:, :D] + mm(d_logits, wr_s[...], NT)
        grad_gain, back = norm_back(mid_ref[rows, :], gain_ref[1:2, :], d_hm)
        grads = grads + grad_gain
        d_mid = g_ref[rows, :].astype(F32) + back
        dmid_ref[rows, :] = d_mid
        (datt0_ref, datt1_ref)[m][...] = d_mid.astype(BF)
    gain_out[...] = jnp.broadcast_to(grads, (8, D))


def mid_back(rets, g, mid, hms, gains, w):
    return call(
        mid_back_kernel, "mid_back", [rets[0], g, mid, *hms, gains], [w, *rets[1:]],
        [sds((R, D), F32), sds((T, D), BF), sds((T, D), BF), sds((R, LANES), BF), sds((8, D), F32)], [],
        [pltpu.VMEM((D, LANES), BF), pltpu.SemaphoreType.DMA, pltpu.VMEM((3, R, D + LANES), BF), pltpu.SemaphoreType.DMA((3,))],
        2.8, 4,
    )


def attn_back_kernel(*refs):
    spots_ref, datt0_ref, datt1_ref, q_ref, own_ref, allowed_ref, cos_ref, sin_ref = refs[:8]
    w_refs, kv_refs, rest = refs[8:16], (None,) + refs[16:23], refs[23:]
    dq0_ref, dq1_ref, same_ref, other_ref, da, kv_s, kv_acc, w_s, sems, kv_sems = rest
    copies = fetch_w_out(spots_ref, w_refs, w_s, sems)
    key_copies = fetch_keys(kv_refs, kv_s, kv_sems)
    own_keys(own_ref, kv_s)
    d_att = jnp.concatenate([datt0_ref[...], datt1_ref[...]], axis=0)
    for copy in copies:
        copy.wait()
    for j in range(4):
        piece = mm(d_att, w_s[j * 384 : (j + 1) * 384, :], NT).astype(BF)
        for m in range(2):
            for i in range(3):
                da[m, j * 3 + i] = piece[m * T : (m + 1) * T, i * HS : (i + 1) * HS]
    for copy in key_copies:
        copy.wait()
    allowed = allowed_ref[...]
    cos, sin = cos_ref[:T, :], sin_ref[:T, :]
    for m in range(2):
        rows = slice(m * T, (m + 1) * T)
        for k in range(KV_HEADS):
            keys = kv_s[m, :, k * HS : (k + 1) * HS]
            values = kv_s[m, :, KW + k * HS : KW + (k + 1) * HS]
            q6 = heads_of(q_ref, m, k)
            d6 = da[m, k * GROUP : (k + 1) * GROUP].reshape(GROUP * T, HS)
            p = probs_of(q6, keys, allowed)
            dp = mm(d6, values, NT)
            ds = (p * (dp - jnp.sum(p * dp, axis=-1, keepdims=True)) * SCALE).astype(BF)
            dq = mm(ds, keys)
            for g in range(GROUP):
                h = k * GROUP + g
                (dq0_ref, dq1_ref)[m][:, h * HS : (h + 1) * HS] = rope_back(dq[g * T : (g + 1) * T], cos, sin).astype(BF)
            kv_acc[:, k * HS : (k + 1) * HS] = mm(ds, q6, TN)
            kv_acc[:, KW + k * HS : KW + (k + 1) * HS] = mm(p.astype(BF), d6, TN)
        for i in range(4):
            at = slice(i * R + m * T, i * R + (m + 1) * T)
            same_ref[at, :] = kv_acc[i * T : (i + 1) * T].astype(BF)
            other_ref[at, :] = kv_acc[C + i * T : C + (i + 1) * T].astype(BF)


def attn_back(spots, d_atts, w_o, q, kvs, allowed, cos, sin):
    return call(
        attn_back_kernel, "attn_back", [*d_atts, q, kvs[0], allowed, cos, sin], [*w_o, *kvs[1:]],
        [sds((T, D), BF), sds((T, D), BF), sds((4 * R, 512), BF), sds((4 * R, 512), BF)], [],
        [pltpu.VMEM((2, HEADS, T, HS), BF), pltpu.VMEM((2, SEQ, 512), BF), pltpu.VMEM((SEQ, 512), F32),
         pltpu.VMEM((D, D), BF), pltpu.SemaphoreType.DMA((32,)), pltpu.SemaphoreType.DMA((2, 8))],
        9, 12, spots,
    )


MSG = 512 + LANES


def qkv_back_kernel(*refs):
    own_ref, dq0_ref, dq1_ref, dl_ref, gm_ref, x0_ref, x1_ref, gain_ref, cos_ref, sin_ref, dmid_ref, w_ref = refs[:12]
    gin_ref, low_ref, msg_ref, dh, w_s, sems, far_s, far_sems = refs[15:]
    arrive = [fetch(b, far_s.at[i], far_sems.at[i]) for i, b in enumerate(refs[12:15])]
    copies = [fetch(w_ref.at[j * 384 : (j + 1) * 384, 0:2048], w_s.at[j], sems.at[j]) for j in range(4)]
    d_kv = own_ref[...].astype(F32)
    for i in range(3):
        arrive[i].wait()
        d_kv = d_kv + far_s[i].astype(F32)
    cos, sin = cos_ref[...], sin_ref[...]
    for i in range(KV_HEADS):
        at = slice(i * HS, (i + 1) * HS)
        msg_ref[:R, at] = rope_back(d_kv[:, at], cos, sin).astype(BF)
    msg_ref[:R, KW:512] = d_kv[:, KW:].astype(BF)
    msg_ref[:R, 512:] = dl_ref[...]
    dq = jnp.concatenate([dq0_ref[...], dq1_ref[...]], axis=0)
    for j in range(4):
        copies[j].wait()
        dh[:, j * 384 : (j + 1) * 384] = mm(dq, w_s[j, :, :D], NT) + mm(msg_ref[:R, :512], w_s[j, :, D:], NT)
    grads = jnp.zeros((1, D), F32)
    for m, x_ref in enumerate((x0_ref, x1_ref)):
        rows = slice(m * T, (m + 1) * T)
        grad_gain, back = norm_back(x_ref[...].astype(F32), gain_ref[0:1, :], dh[rows])
        grads = grads + grad_gain
        g_in = dmid_ref[rows, :] + back
        gin_ref[rows, :] = g_in
        low_ref[rows, :] = g_in.astype(BF)
    row = lax.broadcasted_iota(jnp.int32, (16, 512), 0)
    both = jnp.zeros((16, 512), F32)
    for c in range(3):
        at = slice(c * 512, (c + 1) * 512)
        both = jnp.where(row == c, jnp.broadcast_to(grads[:, at], (16, 512)), both)
        both = jnp.where(row == 3 + c, jnp.broadcast_to(gm_ref[0:1, at], (16, 512)), both)
    msg_ref[R:, :512] = both.astype(BF)
    msg_ref[R:, 512:] = jnp.zeros((16, LANES), BF)


def qkv_back(rets, dqs, dl, gm, x0, x1, gains, w, cos, sin, d_mid):
    return call(
        qkv_back_kernel, "qkv_back", [rets[0], *dqs, dl, gm, x0, x1, gains, cos, sin, d_mid], [w, *rets[1:]],
        [sds((R, D), F32), sds((R, D), BF), sds((R + 16, MSG), BF)], [],
        [pltpu.VMEM((R, D), F32), pltpu.VMEM((4, 384, 2048), BF), pltpu.SemaphoreType.DMA((4,)),
         pltpu.VMEM((3, R, 512), BF), pltpu.SemaphoreType.DMA((3,))],
        6.2, 11,
    )


ROWS = SLICE + 16


def attn_grad_kernel(*refs):
    order_ref, left_ref, msgs, dqs, datts, send_ref, (lh, rq, ro, rm, rg, sems) = refs[0], refs[1], refs[2:10], refs[10:26], refs[26:42], refs[42], refs[43:]
    left_copies, q_copies, o_copies, m_copies = [], [], [], []
    for i in range(8):
        at = slice(i * R, (i + 1) * R)
        left_copies.append(fetch(left_ref.at[order_ref[i]], lh.at[at, :], sems.at[0, i]))
        for m in range(2):
            half = slice(i * R + m * T, i * R + (m + 1) * T)
            o_copies.append(fetch(datts[2 * i + m], ro.at[half, :], sems.at[1 + m, i]))
            q_copies.append(fetch(dqs[2 * i + m], rq.at[half, :], sems.at[3 + m, i]))
        m_copies.append(fetch(msgs[i].at[:R, :], rm.at[at, :], sems.at[5, i]))
        m_copies.append(fetch(msgs[i].at[R:, :], rg.at[i], sems.at[6, i]))
    for copy in left_copies + o_copies:
        copy.wait()

    def spread(grads, width, lane):
        for r in range(8):
            send_ref[r, :SLICE, lane : lane + width] = grads[:SLICE, r * width : (r + 1) * width].astype(BF)

    spread(mm(lh[:, 256:512], ro[...], TN), SLICE, 320)
    for copy in q_copies:
        copy.wait()
    spread(mm(lh[:, :256], rq[...], TN), SLICE, 0)
    for copy in m_copies:
        copy.wait()
    spread(mm(lh[:, :256], rm[:, :512], TN), 64, SLICE)
    small = mm(lh[:, 512:], rm[:, 512:], TN)[:SLICE, :64].astype(BF)
    gains = sum(rg[i, :, :512].astype(F32) for i in range(8)).astype(BF)
    for r in range(8):
        send_ref[r, :SLICE, 256:320] = small
        send_ref[r, SLICE:, :] = gains


def attn_grad(order, left, msgs, dqs, datts):
    return pl.pallas_call(
        attn_grad_kernel,
        name="attn_grad",
        in_specs=[SCALARS] + [AWAY] * 41,
        out_specs=HERE,
        out_shape=sds((8, ROWS, 512), BF),
        scratch_shapes=[
            pltpu.VMEM((8 * R, 768), BF), pltpu.VMEM((8 * R, D), BF), pltpu.VMEM((8 * R, D), BF), pltpu.VMEM((8 * R, MSG), BF),
            pltpu.VMEM((8, 16, MSG), BF), pltpu.SemaphoreType.DMA((7, 8)),
        ],
        compiler_params=pltpu.CompilerParams(vmem_limit_bytes=20 * 2**20),
        cost_estimate=work(8.5),
    )(order, *in_hbm((left, *msgs, *dqs, *datts)))


def turn_kernel(*refs):
    lefts, (h_out, a_out, f_s, h_s, a_s, sems) = refs[:2], refs[2:]
    copies = [fetch(left, f_s.at[i], sems.at[i]) for i, left in enumerate(lefts)]
    for i in range(2):
        copies[i].wait()
        h_s[:, i * B : (i + 1) * B] = f_s[i, :, :D].T
        a_s[:, i * B : (i + 1) * B] = f_s[i, :, D:].T
    sent = [fetch(h_s, h_out, sems.at[2]), fetch(a_s, a_out, sems.at[3])]
    for copy in sent:
        copy.wait()


def turn(lefts):
    return call(
        turn_kernel, "turn", [], lefts, [], [sds((D, 4 * C), BF), sds((FF, 4 * C), BF)],
        [pltpu.VMEM((2, B, FW), BF), pltpu.VMEM((D, 4 * C), BF), pltpu.VMEM((FF, 4 * C), BF), pltpu.SemaphoreType.DMA((6,))],
        5, 14,
    )


def expert_grad_kernel(in_ref, down_ref, *refs):
    rights, out_ref, right = refs[:2], refs[2], refs[3]
    j = pl.program_id(0)
    for i in range(2):
        right[i * B : (i + 1) * B, :] = rights[i][...]

    def grads(left_ref, rows, first):
        for r in range(0, 8, 2):
            out_ref[r : r + 2, first : first + rows, :] = mm(left_ref[r * rows : (r + 2) * rows, :], right[...]).astype(BF).reshape(2, rows, 512)

    @pl.when(j % 2 == 0)
    def _():
        grads(in_ref, SLICE, 0)

    @pl.when(j % 2 == 1)
    def _():
        grads(down_ref, SLICE // 2, SLICE)


def expert_grad(left_in, left_down, rights):
    return pl.pallas_call(
        expert_grad_kernel,
        name="expert_grad",
        grid=(6,),
        in_specs=[whole((D, 4 * C)), whole((FF, 4 * C))] + [pl.BlockSpec((B, 512), lambda j: (0, (j % 2) * 3 + j // 2))] * 2,
        out_specs=pl.BlockSpec((8, SLICE + SLICE // 2, 512), lambda j: (0, 0, j // 2)),
        out_shape=pltpu.HBM((8, SLICE + SLICE // 2, D), BF),
        scratch_shapes=[pltpu.VMEM((4 * C, 512), BF)],
        compiler_params=pltpu.CompilerParams(dimension_semantics=("arbitrary",), vmem_limit_bytes=26 * 2**20),
        cost_estimate=work(20),
    )(*in_hbm((left_in, left_down, *rights)))


def body(tokens_in, cotangent, routes, gain_attn, w_query, w_keyval, w_out, gain_moe, w_router, w_in, w_down):
    is_first = lax.axis_index("section") == 0
    shard = lax.axis_index("shard")
    rep = lax.axis_index("rep")
    chip, core = shard // 2, shard % 2
    micros = range(2)

    extra = jnp.concatenate([w_router[0], gain_attn[0][:, None], gain_moe[0][:, None]], axis=1)
    extra = jnp.pad(extra, ((0, 0), (0, LANES - extra.shape[1])))
    packed = jnp.concatenate([w_query[0], w_keyval[0], extra], axis=1)
    w = lax.all_gather(packed, "shard", axis=0, tiled=True)
    pick = (jnp.arange(LANES)[None, :] == (jnp.arange(8)[:, None] + N_EXPERTS)) & (jnp.arange(8)[:, None] < 2)
    gains = mm(pick.astype(BF), w[:, 2048:], NT)
    z = rep // 2

    quarter = lax.dynamic_slice_in_dim(w_out[0], z * (SLICE // 4), SLICE // 4, 0)
    quarters = jnp.stack(from_chips(quarter))
    along_z = [quarters] + [lax.ppermute(quarters, "rep", [(i, ((i // 2 + k) % 4) * 2 + i % 2) for i in range(8)]) for k in (1, 2, 3)]
    w_o = along_z + [swap(piece) for piece in along_z]
    spots = [((chip - ky) % 4) * 2 * SLICE + c * SLICE + ((z - kz) % 4) * (SLICE // 4) for c in (core, 1 - core) for kz in range(4) for ky in range(4)]
    spots = jnp.stack(spots).astype(jnp.int32)

    inner = (w_in[0, 0], swap(w_in[0, 0]))
    outer = (w_down[0, 0], swap(w_down[0, 0]))
    w, gains, inner, outer = lax.optimization_barrier((w, gains, inner, outer))

    half = HS // 2
    frequency = ROPE_BASE ** (-jnp.arange(half, dtype=F32) * 2.0 / HS)
    place = shard * T + jnp.arange(T, dtype=jnp.int32)
    angles = place.astype(F32)[:, None] * frequency[None, :]
    angles = jnp.concatenate([angles, angles], axis=0)
    cos = jnp.concatenate([jnp.cos(angles)] * 2, axis=1)
    sin = jnp.concatenate([-jnp.sin(angles), jnp.sin(angles)], axis=1)
    order = jnp.stack([((chip - k) % 4) * 2 + c for c in (core, 1 - core) for k in range(4)]).astype(jnp.int32)
    key_place = (order[:, None] * T + jnp.arange(T, dtype=jnp.int32)[None, :]).reshape(1, SEQ)
    allowed = (key_place <= place[:, None]).astype(F32)
    lane = jnp.arange(LANES, dtype=jnp.int32)
    other = shard ^ 1
    mine = jnp.stack([(lane == e) | (lane == e + N_EXPERTS) for e in (shard, other)]).astype(F32)
    mine = jnp.pad(mine, ((0, 6), (0, 0)))
    put = jnp.stack([lane == shard, lane == shard + N_EXPERTS, lane == other, lane == other + N_EXPERTS]).astype(F32)
    put = jnp.pad(put, ((0, 4), (0, 0)))
    chosen = jnp.any(routes[0, :, 0].reshape(R, -1)[:, :, None] == lane[None, None, :], axis=1).astype(F32)

    hold = lax.optimization_barrier

    def attention(x, save):
        q, kv, h_attn = qkv(x[0], x[1], gains, w, cos, sin)
        kvs = gather_blocks(kv)
        att, mid, *hm = attend(spots, q, kvs, allowed, x[0], x[1], w_o, w, gains, chosen, h_attn, save)
        return q, kvs, mid, hm

    def keys_back(same, other):
        got = swap(other)
        return to_chips([plus(same[k * R : (k + 1) * R], got[k * R : (k + 1) * R]) for k in range(4)])

    tokens = [tokens_in[m, 0] for m in micros]
    given = cotangent.reshape(R, D)
    _, _, mid, hms = attention(tokens, False)
    blocks = [from_chips(hm) for hm in hms]
    out = expert(blocks[0], mine, inner, outer, False)
    blocks[1][0], _ = hold((blocks[1][0], out[0]))
    outs = [out, expert(blocks[1], mine, inner, outer, False)]
    first = [(mid[m * T : (m + 1) * T] + sum(r.astype(F32) for r in to_chips(outs[m]))).astype(BF) for m in micros]
    arrived = [lax.ppermute(first[m], "section", [(0, 1)]) for m in micros]
    arrived, given_blocks = hold((arrived, halves_from_chips(cotangent[0, 0], cotangent[1, 0])))

    x = [jnp.where(is_first, tokens[m], arrived[m]) for m in micros]
    q, kvs, mid, (*hms, left) = attention(x, True)
    out = expert(halves_from_chips(*hms), mine, inner, outer, True)
    parts, (g_share, f_own, f_other), kept = out[:4], out[4:7], out[7:]
    f_got = swap(f_other)

    acts = (mid + sum(r.astype(F32) for r in to_chips(parts))).astype(BF)
    out = expert_back(given_blocks, (g_share, *kept), put, inner, outer, False)
    out, acts = hold((out, acts))
    rets = to_chips(out)
    rets, f_got, left = hold((rets, f_got, left))
    left = lax.all_to_all(left, "shard", split_axis=0, concat_axis=0, tiled=True)
    d_mid, datt0, datt1, dl, gm = mid_back(rets, given, mid, hms, gains, w)
    dq0, dq1, kv_same, kv_other = attn_back(spots, (datt0, datt1), w_o, q, kvs, allowed, cos, sin)
    kv_rets, (h_turned, act_turned), left = hold((keys_back(kv_same, kv_other), turn([f_own, f_got]), left))
    _, low, _ = qkv_back(kv_rets, (dq0, dq1), dl, gm, x[0], x[1], gains, w, cos, sin, d_mid)
    arrived = lax.ppermute(low, "section", [(1, 0)])
    halves = [jnp.where(is_first, arrived[m * T : (m + 1) * T], given[m * T : (m + 1) * T]) for m in micros]
    given = jnp.where(is_first, arrived, given)

    out = expert_back(halves_from_chips(*halves), (g_share, *kept), put, inner, outer, True)
    rets, rights = to_chips(out[:4]), [out[4], swap(out[5])]
    rets, send = hold((rets, expert_grad(h_turned, act_turned, rights)))
    expert_parts = lax.all_to_all(send, "rep", split_axis=0, concat_axis=0, tiled=True)
    d_mid, datt0, datt1, dl, gm = mid_back(rets, given, mid, hms, gains, w)
    datts = halves_from_chips(datt0, datt1)
    dq0, dq1, kv_same, kv_other = attn_back(spots, (datt0, datt1), w_o, q, kvs, allowed, cos, sin)
    datts, kv_same, kv_other = hold((datts, kv_same, kv_other))
    kv_rets = keys_back(kv_same, kv_other)
    kv_rets, dq0_sent, dq1_sent = hold((kv_rets, dq0, dq1))
    dqs = halves_from_chips(dq0_sent, dq1_sent)
    g_in, _, msg = qkv_back(kv_rets, (dq0, dq1), dl, gm, x[0], x[1], gains, w, cos, sin, d_mid)

    msgs = from_chips(msg)
    dqs, msgs = hold((dqs, msgs))
    dqs, datts, msgs = (blocks + [swap(b) for b in blocks] for blocks in (dqs, datts, msgs))
    send = attn_grad(order, left, msgs, dqs, datts)
    expert_parts, send = hold((expert_parts, send))
    got = lax.all_to_all(send, "rep", split_axis=0, concat_axis=0, tiled=True)
    sums = jnp.sum(got.astype(F32), axis=0)
    g_q, g_kv, g_r, g_o = (sums[:SLICE, a:b] for a, b in ((0, 192), (192, 256), (256, 256 + N_EXPERTS), (320, 512)))
    g_gains = lax.dynamic_slice(sums[SLICE : SLICE + 6].reshape(2, D), (0, shard * SLICE), (2, SLICE))
    expert_sums = jnp.sum(expert_parts.astype(F32), axis=0)

    return (
        acts.reshape(1, 2, 1, T, D),
        g_in.reshape(1, 2, 1, T, D),
        g_gains[0:1],
        g_q[None],
        g_kv[None],
        g_o[None],
        g_gains[1:2],
        g_r[None],
        expert_sums[None, None, :SLICE],
        expert_sums[None, None, SLICE:],
    )


def solution(mesh):
    in_specs = (
        P(None, "rep", "shard", None),
        P(None, "rep", "shard", None),
        P("section", None, "rep", "shard", None),
        P("section", "shard"),
        P("section", "shard", None),
        P("section", "shard", None),
        P("section", "shard", None),
        P("section", "shard"),
        P("section", "shard", None),
        P("section", "shard", None, None),
        P("section", "shard", None, None),
    )
    out_specs = (
        P("section", None, "rep", "shard", None),
        P("section", None, "rep", "shard", None),
        P("section", "shard"),
        P("section", "shard", "rep"),
        P("section", "shard", "rep"),
        P("section", "shard", "rep"),
        P("section", "shard"),
        P("section", "shard", None),
        P("section", "shard", "rep", None),
        P("section", "shard", "rep", None),
    )
    return jax.shard_map(body, mesh=mesh, in_specs=in_specs, out_specs=out_specs, check_vma=False)
```
